32 devices in a mesh: section: 2 (over core), dp: 16 (over z, y, x).
Axes of the slice: x: 2, y: 2, z: 4, core: 2. Of those that a mesh axis runs over, the one named last changes fastest.
Arguments:
- inputs: bfloat16 [32, 1024, 768], P('dp'), may hold values from -6 to 6
- cotangent: bfloat16 [32, 1024, 768], P('dp'), may hold values from -6 to 6
- lengths: int32 [32], replicated, may hold values from 64 to 1024, as said below
- assignment: int32 [32], P('dp'), may hold values from 0 to 31, each once
- skip_flags: int32 [2, 2], P(None, 'section'), may hold values from 0 to 1, as said below
- head_counts: int32 [2, 2], P(None, 'section'), may hold values from 8 to 12, as said below
- ffn_counts: int32 [2, 2], P(None, 'section'), may hold values from 1920 to 3072, as said below
- w_qkv: bfloat16 [2, 768, 2304], P('section'), may hold values from -0.21875 to 0.21875
- bias_q: bfloat16 [2, 768], P('section'), may hold values from -1 to 1
- bias_v: bfloat16 [2, 768], P('section'), may hold values from -1 to 1
- w_out: bfloat16 [2, 768, 768], P('section'), may hold values from -0.875 to 0.875
- bias_out: bfloat16 [2, 768], P('section'), may hold values from -1 to 1
- norm1_gain: bfloat16 [2, 768], P('section'), may hold values from 0.5 to 1.5
- norm1_bias: bfloat16 [2, 768], P('section'), may hold values from -1 to 1
- w_up: bfloat16 [2, 768, 3072], P('section'), may hold values from -0.21875 to 0.21875
- bias_up: bfloat16 [2, 3072], P('section'), may hold values from -1 to 1
- w_down: bfloat16 [2, 3072, 768], P('section'), may hold values from -0.109375 to 0.109375
- bias_down: bfloat16 [2, 768], P('section'), may hold values from -1 to 1
- norm2_gain: bfloat16 [2, 768], P('section'), may hold values from 0.5 to 1.5
- norm2_bias: bfloat16 [2, 768], P('section'), may hold values from -1 to 1
Outputs:
- output: float32 [32, 1024, 768], P('dp', None, 'section')
- input_grad: float32 [32, 1024, 768], P('dp', None, 'section')
- grad_w_qkv: float32 [2, 768, 2304], P('section')
- grad_bias_q: float32 [2, 768], P('section')
- grad_bias_v: float32 [2, 768], P('section')
- grad_w_out: float32 [2, 768, 768], P('section')
- grad_bias_out: float32 [2, 768], P('section')
- grad_norm1_gain: float32 [2, 768], P('section')
- grad_norm1_bias: float32 [2, 768], P('section')
- grad_w_up: float32 [2, 768, 3072], P('section')
- grad_bias_up: float32 [2, 3072], P('section')
- grad_w_down: float32 [2, 3072, 768], P('section')
- grad_bias_down: float32 [2, 768], P('section')
- grad_norm2_gain: float32 [2, 768], P('section')
- grad_norm2_bias: float32 [2, 768], P('section')
The draws below stay inside these ranges and needn't reach their ends.
Inputs may be any that keep to these rules, and one draw needn't show every extreme that they name: `lengths`: some utterance has 1024 frames and some has the least. `skip_flags`: each micro-batch skips at most one layer; some micro-batch skips one. `head_counts`: in each micro-batch one layer has all 12 heads and the other 12 - 2k heads with k 1 or 2; k is 2 in some micro-batch. `ffn_counts`: in each micro-batch one layer has all 3072 units and the other 3072 - k * (96) with k from 1 to 12; k is 12 in some micro-batch.
All inputs are finite; a program needn't handle non-finite values.
Results may differ from the reference program's by a relative error of at most 0.014.
Values may be sent and summed in bfloat16 or wider, within the bound.
No kernel may reach another device: no remote copies, remote signals or barrier semaphores. Data moves between devices by JAX's collectives and lax.ppermute only.
A program may use at most 576 MiB of HBM per device.

```python
import jax
import jax.numpy as jnp
from jax import lax

D = 768
HEADS = 12
FF = 3072
LENGTH = 1024
MICRO = 2
SEQS = 1
LAYERS = 2
UTT = 32


def draw_lengths(key, part):
    key = jax.random.fold_in(key, 11)
    shape_key, pick_key = jax.random.split(key)
    steps_drawn = jax.random.randint(shape_key, (UTT,), 0, 17)
    floor_len = max(1, LENGTH // 16)
    drawn = floor_len + (LENGTH - floor_len) * steps_drawn * (steps_drawn + 16) // 512
    chosen = jax.random.randint(pick_key, (), 0, UTT)
    order = jnp.arange(UTT)
    drawn = jnp.where(order == chosen, LENGTH, drawn)
    drawn = jnp.where(order == (chosen + 1) % UTT, floor_len, drawn)
    return drawn.astype(jnp.int32)


def draw_skip_flags(key, part):
    key = jax.random.fold_in(key, 23)
    pick_key, micro_key, layer_key = jax.random.split(key, 3)
    picked = jax.random.randint(pick_key, (MICRO,), 0, LAYERS + 1)
    forced_micro = jax.random.randint(micro_key, (), 0, MICRO)
    forced_layer = jax.random.randint(layer_key, (), 1, LAYERS + 1)
    picked = jnp.where(jnp.arange(MICRO) == forced_micro, forced_layer, picked)
    flags = jnp.arange(LAYERS)[None, :] + 1 == picked[:, None]
    return flags.astype(jnp.int32)


def subnet_counts(key, full_width, step_width, most_steps):
    step_key, full_key, micro_key = jax.random.split(key, 3)
    steps_drawn = jax.random.randint(step_key, (MICRO,), 1, most_steps + 1)
    forced_micro = jax.random.randint(micro_key, (), 0, MICRO)
    steps_drawn = jnp.where(jnp.arange(MICRO) == forced_micro, most_steps, steps_drawn)
    full_layer = jax.random.randint(full_key, (MICRO,), 0, LAYERS)
    reduced = full_width - step_width * steps_drawn
    counts = jnp.where(jnp.arange(LAYERS)[None, :] == full_layer[:, None], full_width, reduced[:, None])
    return counts.astype(jnp.int32)


def draw_head_counts(key, part):
    key = jax.random.fold_in(key, 37)
    return subnet_counts(key, HEADS, max(1, HEADS // 6), 2)


def draw_ffn_counts(key, part):
    key = jax.random.fold_in(key, 41)
    return subnet_counts(key, FF, FF // 32, 12)


def shard_levels(stream_key, shape, cuts, smallest, largest):
    level, own = 1.0, jax.random.fold_in(stream_key, 6)
    for axis_at, parts in cuts:
        draws = jnp.exp(jax.random.uniform(jax.random.fold_in(own, axis_at), (parts,), jnp.float32, smallest / len(cuts), largest / len(cuts)))
        level = level * jnp.repeat(draws, shape[axis_at] // parts).reshape([-1 if axis == axis_at else 1 for axis in range(len(shape))])
    return level


def noise(rng, extent, width, limit, cuts=(), dtype=jnp.bfloat16):
    gain = shard_levels(rng, extent, cuts, -0.22, 0.18) if cuts else 1.0
    values = jax.random.normal(rng, extent, jnp.float32) * width * gain
    return jnp.minimum(jnp.maximum(values, -limit), limit).astype(dtype)


def setup_inputs(seed: int = 0) -> dict:
    seeds = jax.random.split(jax.random.key(seed), 21)
    inputs = noise(seeds[0], (UTT, LENGTH, D), 1.0, 6.0, ((0, 16),))
    cotangent = noise(seeds[1], (UTT, LENGTH, D), 1.0, 6.0, ((0, 16),))
    lengths = draw_lengths(jax.random.fold_in(seeds[20], 71), 0)
    assignment = jax.random.permutation(seeds[3], UTT).astype(jnp.int32)
    skip_flags = draw_skip_flags(jax.random.fold_in(seeds[20], 71), 0)
    head_counts = draw_head_counts(jax.random.fold_in(seeds[20], 71), 0)
    ffn_counts = draw_ffn_counts(jax.random.fold_in(seeds[20], 71), 0)
    w_qkv = noise(seeds[7], (LAYERS, D, 3 * D), D ** -0.5, 0.21875, ((0, 2),))
    bias_q = noise(seeds[8], (LAYERS, D), 0.2, 1.0, ((0, 2),))
    bias_v = noise(seeds[9], (LAYERS, D), 0.2, 1.0, ((0, 2),))
    w_out = noise(seeds[10], (LAYERS, D, D), (D // 16) ** -0.5, 0.875, ((0, 2),))
    bias_out = noise(seeds[11], (LAYERS, D), 0.2, 1.0, ((0, 2),))
    norm1_gain = jnp.clip(1.0 + 0.1 * jax.random.normal(seeds[12], (LAYERS, D), jnp.float32), 0.5, 1.5).astype(jnp.bfloat16)
    norm1_bias = noise(seeds[13], (LAYERS, D), 0.2, 1.0, ((0, 2),))
    w_up = noise(seeds[14], (LAYERS, D, FF), D ** -0.5, 0.21875, ((0, 2),))
    bias_up = noise(seeds[15], (LAYERS, FF), 0.2, 1.0, ((0, 2),))
    w_down = noise(seeds[16], (LAYERS, FF, D), FF ** -0.5, 0.109375, ((0, 2),))
    bias_down = noise(seeds[17], (LAYERS, D), 0.2, 1.0, ((0, 2),))
    norm2_gain = jnp.clip(1.0 + 0.1 * jax.random.normal(seeds[18], (LAYERS, D), jnp.float32), 0.5, 1.5).astype(jnp.bfloat16)
    norm2_bias = noise(seeds[19], (LAYERS, D), 0.2, 1.0, ((0, 2),))
    return dict(inputs=inputs, cotangent=cotangent, lengths=lengths, assignment=assignment, skip_flags=skip_flags, head_counts=head_counts, ffn_counts=ffn_counts, w_qkv=w_qkv, bias_q=bias_q, bias_v=bias_v, w_out=w_out, bias_out=bias_out, norm1_gain=norm1_gain, norm1_bias=norm1_bias, w_up=w_up, bias_up=bias_up, w_down=w_down, bias_down=bias_down, norm2_gain=norm2_gain, norm2_bias=norm2_bias)


NORM_EPS = 1e-05
NEG_FILL = -1e+30

@jax.custom_vjp
def low(v):
    return lax.optimization_barrier(v.astype(jnp.bfloat16)).astype(jnp.float32)

@jax.custom_vjp
def low_back(v):
    return v

def low_keep(v):
    return (low(v), None)

def low_pass(kept, grad):
    return (grad,)

def back_keep(v):
    return (v, None)

def back_low(kept, grad):
    return (low(grad),)
low.defvjp(low_keep, low_pass)
low_back.defvjp(back_keep, back_low)

def layer_norm(values, scale_gain, shift_bias):
    center = lax.optimization_barrier(jnp.mean(values, axis=-1, keepdims=True))
    spread = lax.optimization_barrier(jnp.mean((values - center) ** 2, axis=-1, keepdims=True))
    return (values - center) * lax.rsqrt(spread + NORM_EPS) * scale_gain + shift_bias

def one_layer(hidden, frame_mask, layer_params, heads_on, units_on, skipped):
    w_qkv, bias_q, bias_v, w_out, bias_out, gain_one, shift_one, w_up, bias_up, w_down, bias_down, gain_two, shift_two = layer_params
    seq_len, model_width = hidden.shape
    head_size = model_width // HEADS
    highest = lax.Precision.HIGHEST
    qkv_bias = jnp.concatenate([bias_q, jnp.zeros_like(bias_q), bias_v])
    projected = low(low_back(jnp.dot(hidden, w_qkv, precision=highest) + qkv_bias))
    queries = projected[:, :model_width].reshape(seq_len, HEADS, head_size)
    keys_all = projected[:, model_width:2 * model_width].reshape(seq_len, HEADS, head_size)
    values_all = projected[:, 2 * model_width:].reshape(seq_len, HEADS, head_size)
    scores = jnp.einsum('qhd,khd->hqk', queries, keys_all, precision=highest) * head_size ** (-0.5)
    scores = low_back(jnp.where(frame_mask[None, None, :] > 0, scores, NEG_FILL))
    probs = jax.nn.softmax(scores, axis=-1)
    context = jnp.einsum('hqk,khd->qhd', low(probs), values_all, precision=highest) * heads_on[None, :, None]
    context = low(low_back(context.reshape(seq_len, model_width)))
    attended = low_back(jnp.dot(context, w_out, precision=highest) + bias_out)
    normed = layer_norm(hidden + attended, gain_one, shift_one)
    lifted = low_back(jnp.dot(low(normed), w_up, precision=highest) + bias_up)
    gated = jax.nn.gelu(lifted, approximate=False) * units_on
    dropped = low_back(jnp.dot(low(gated), w_down, precision=highest) + bias_down)
    result = layer_norm(normed + dropped, gain_two, shift_two) * frame_mask[:, None]
    return jnp.where(skipped > 0, hidden, result)

def reference(inputs, cotangent, lengths, assignment, skip_flags, head_counts, ffn_counts, w_qkv, bias_q, bias_v, w_out, bias_out, norm1_gain, norm1_bias, w_up, bias_up, w_down, bias_down, norm2_gain, norm2_bias):
    slot_len = lengths[assignment]
    frames_live = (jnp.arange(LENGTH)[None, :] < slot_len[:, None]).astype(jnp.float32)
    micro_of_slot = (jnp.arange(UTT) % (MICRO * SEQS) // SEQS).astype(jnp.int32)
    heads_on = (jnp.arange(HEADS)[None, None, :] < head_counts[:, :, None]).astype(jnp.float32)
    units_on = (jnp.arange(FF)[None, None, :] < ffn_counts[:, :, None]).astype(jnp.float32)
    params = tuple((weight.astype(jnp.float32) for weight in (w_qkv, bias_q, bias_v, w_out, bias_out, norm1_gain, norm1_bias, w_up, bias_up, w_down, bias_down, norm2_gain, norm2_bias)))

    def forward(frames_in, *weights):

        def per_sequence(sequence):
            hidden, frame_mask, micro_index = sequence
            for depth_index in range(LAYERS):
                layer_params = tuple((weight[depth_index] for weight in weights))
                hidden = one_layer(hidden, frame_mask, layer_params, heads_on[micro_index, depth_index], units_on[micro_index, depth_index], skip_flags[micro_index, depth_index])
                if depth_index + 1 < LAYERS:
                    hidden = low(hidden)
            return hidden
        return lax.map(jax.checkpoint(per_sequence), (frames_in, frames_live, micro_of_slot))
    result, pullback = jax.vjp(forward, inputs.astype(jnp.float32), *params)
    gradients = pullback(cotangent.astype(jnp.float32))
    return (result, gradients[0], gradients[1], gradients[2], gradients[3], gradients[4], gradients[5], gradients[6], gradients[7], gradients[8], gradients[9], gradients[10], gradients[11], gradients[12], gradients[13])
```

```python
import functools

import jax
import jax.numpy as jnp
from jax import lax
from jax.experimental import pallas as pl
from jax.experimental.pallas import tpu as pltpu
from jax.sharding import PartitionSpec as P

HEADS = 12
MICRO = 2
NORM_EPS = 1e-05
NEG_FILL = -1e30
F32 = jnp.float32
BF16 = jnp.bfloat16

ROWS = 256
UNITS = 512
VMEM_BYTES = 64 * 1024 * 1024

OWN, BLOCKS, LIVE, LENGTH, PAIRS, COUNT, CHUNKS, SLOT, SKIP, SECTION = range(10)
V_BQ, V_ZERO, V_BV, V_BO, V_G1, V_B1, V_BU, V_BD, V_G2, V_B2 = 0, 1, 2, 3, 4, 5, 6, 10, 11, 12


def dot(left, right):
    return lax.dot_general(left, right, (((1,), (0,)), ((), ())), preferred_element_type=F32)


def dot_nt(left, right):
    return lax.dot_general(left, right, (((1,), (1,)), ((), ())), preferred_element_type=F32)


def dot_tn(left, right):
    return lax.dot_general(left, right, (((0,), (0,)), ((), ())), preferred_element_type=F32)


def rows_at(block):
    if isinstance(block, int):
        return pl.ds(block * ROWS, ROWS)
    return pl.ds(pl.multiple_of(block * ROWS, ROWS), ROWS)


def cols_at(start, size):
    if isinstance(start, int):
        return pl.ds(start, size)
    return pl.ds(pl.multiple_of(start, 128), size)


def by_blocks(count, most, body):
    for blocks in range(1, most + 1):
        pl.when(count == blocks)(functools.partial(body, blocks))


def fetch_start(s, dst, own_ref, other_ref, sem):
    @pl.when(s[OWN] == 1)
    def _():
        pltpu.make_async_copy(own_ref, dst, sem).start()

    @pl.when(s[OWN] == 0)
    def _():
        pltpu.make_async_copy(other_ref, dst, sem).start()


def live_column(s, block):
    frame = lax.broadcasted_iota(jnp.int32, (ROWS, 1), 0) + block * ROWS
    return frame < s[LENGTH]


def gelu_parts(values):
    size = jnp.abs(values) * 0.7071067811865476
    under = 1.0 + 0.3275911 * size
    t = pl.reciprocal(under, approx=True)
    t = t * (2.0 - under * t)
    poly = t * (
        0.127414796 + t * (-0.142248368 + t * (0.7107068705 + t * (-0.7265760135 + t * 0.5307027145)))
    )
    bell = jnp.exp(-0.5 * values * values)
    tail = poly * bell
    below = jnp.where(values >= 0, 1.0 - tail, tail)
    return values * below, below + values * bell * 0.3989422804014327


def norm_parts(values):
    center = jnp.mean(values, axis=-1, keepdims=True)
    shifted = values - center
    spread = jnp.mean(shifted * shifted, axis=-1, keepdims=True)
    inverse = lax.rsqrt(spread + NORM_EPS)
    return shifted * inverse, inverse


def vec_row(vec_ref, row):
    return vec_ref[row : row + 1, :].astype(F32)


def forward_kernel(
    last,
    s,
    x_hbm,
    wq0, wq1, wo0, wo1, wu0, wu1, wd0, wd1, v0, v1,
    *rest,
):
    if last:
        keep_hbm, send_hbm = rest[:2]
        rest = rest[2:]
    else:
        pass_hbm = rest[0]
        rest = rest[1:]
    (
        proj_hbm, ctx_hbm, stat_hbm, gated_hbm, slope_hbm, x1_hbm, x2_hbm,
        h, wq, wo, wu, wd, vec, proj, ctx, stat, gated, slope, x1, x2, acc, normed_b, bias_up, out_a, out_b,
        in_sem, w_sem, out_sem,
    ) = rest
    most = h.shape[0] // ROWS
    width = h.shape[1]
    pairs_all = width // 128
    blocks = s[BLOCKS]
    live = s[LIVE]
    lane = lax.broadcasted_iota(jnp.int32, (1, 128), 1)
    low = lane < 64

    def source(block):
        if last:
            return x_hbm.at[rows_at(block)]
        return x_hbm.at[s[SLOT], rows_at(block)]

    def h_copy(block):
        return pltpu.make_async_copy(source(block), h.at[rows_at(block)], in_sem.at[block])

    for block in range(most):
        pl.when(block < live)(lambda block=block: h_copy(block).start())

    @pl.when(blocks > 0)
    def _():
        fetch_start(s, vec, v0, v1, w_sem.at[0])
        fetch_start(s, wq, wq0, wq1, w_sem.at[1])
        fetch_start(s, wo, wo0, wo1, w_sem.at[2])
        fetch_start(s, wu, wu0, wu1, w_sem.at[3])
        fetch_start(s, wd, wd0, wd1, w_sem.at[4])

    for block in range(most):
        pl.when(block < live)(lambda block=block: h_copy(block).wait())

    def save(what, source_ref, target_ref, block):
        return pltpu.make_async_copy(
            source_ref.at[rows_at(block)], target_ref.at[rows_at(block)], out_sem.at[what, block]
        )

    def emit(block, value):
        if last:
            half = width // 2
            first = s[SECTION] == 0
            out_a[rows_at(block), :] = jnp.where(first, value[:, :half], value[:, half:])
            out_b[rows_at(block), :] = jnp.where(first, value[:, half:], value[:, :half]).astype(BF16)
            save(7, out_a, keep_hbm, block).start()
            save(8, out_b, send_hbm, block).start()
        else:
            out_b[rows_at(block), :] = value.astype(BF16)
            save(7, out_b, pass_hbm, block).start()

    @pl.when(blocks > 0)
    def _():
        pltpu.make_async_copy(v0, vec, w_sem.at[0]).wait()
        for piece in range(wu.shape[1] // width):
            bias_up[0:1, piece * width : (piece + 1) * width] = vec_row(vec, V_BU + piece)
        pltpu.make_async_copy(wq0, wq, w_sem.at[1]).wait()

        def project(block, carry):
            rows = rows_at(block)
            for part, row in ((0, V_BQ), (1, V_ZERO), (2, V_BV)):
                cols = slice(part * width, (part + 1) * width)
                proj[rows, cols] = (dot(h[rows, :], wq[:, cols]) + vec_row(vec, row)).astype(BF16)
            save(0, proj, proj_hbm, block).start()
            stat[rows, :] = jnp.zeros((ROWS, 128), F32)
            return carry

        lax.fori_loop(0, blocks, project, 0)

        for pair in range(pairs_all):
            @pl.when(pair >= s[PAIRS])
            def _(pair=pair):
                ctx[:, pair * 128 : (pair + 1) * 128] = jnp.zeros((h.shape[0], 128), BF16)

        def attend(count):
            span = count * ROWS
            key_at = lax.broadcasted_iota(jnp.int32, (1, span), 1)
            fill = jnp.where(key_at < s[LENGTH], 0.0, NEG_FILL)

            def one(step, carry):
                pair, block = step // count, step % count
                rows = rows_at(block)
                cols = cols_at(pair * 128, 128)
                q = proj[rows, cols] * jnp.asarray(0.125, BF16)
                k = proj[0:span, cols_at(width + pair * 128, 128)]
                v = proj[0:span, cols_at(2 * width + pair * 128, 128)]
                zero = jnp.zeros_like(q)
                ones = jnp.ones_like(v)
                found, peaks = [], []
                for own in (low, ~low):
                    scores = dot_nt(jnp.where(own, q, zero), k) + fill
                    peak = jnp.max(scores, axis=-1, keepdims=True)
                    exps = jnp.exp(scores - peak).astype(BF16)
                    found.append(dot(exps, jnp.where(own, v, ones)))
                    peaks.append(peak)
                above = jnp.where(low, found[0], found[1])
                total = pltpu.roll(jnp.where(low, found[1], found[0]), 64, 1)
                ctx[rows, cols] = (above / total).astype(BF16)
                logs = jnp.where(low, peaks[0], peaks[1]) + jnp.log(total)
                kept = stat[rows, :]
                kept = jnp.where(lane == 2 * pair, logs[:, 0:1], kept)
                kept = jnp.where(lane == 2 * pair + 1, logs[:, 64:65], kept)
                stat[rows, :] = kept
                return carry

            lax.fori_loop(0, s[PAIRS] * count, one, 0)

        by_blocks(blocks, most, attend)

        pltpu.make_async_copy(wo0, wo, w_sem.at[2]).wait()
        pltpu.make_async_copy(wu0, wu, w_sem.at[3]).wait()
        pltpu.make_async_copy(wd0, wd, w_sem.at[4]).wait()

        def finish(block, carry):
            rows = rows_at(block)
            save(1, ctx, ctx_hbm, block).start()
            res = h[rows, :].astype(F32) + dot(ctx[rows, :], wo[...]) + vec_row(vec, V_BO)
            hat, inverse_one = norm_parts(res)
            x1[rows, :] = hat.astype(BF16)
            save(5, x1, x1_hbm, block).start()
            normed = hat * vec_row(vec, V_G1) + vec_row(vec, V_B1)
            normed_b[...] = normed.astype(BF16)
            acc[...] = normed + vec_row(vec, V_BD)

            def chunk(c, inner):
                cols = cols_at(c * UNITS, UNITS)
                lifted = dot(normed_b[...], wu[:, cols]) + bias_up[0:1, cols]
                value, grad = gelu_parts(lifted)
                unit = lax.broadcasted_iota(jnp.int32, (1, UNITS), 1) + c * UNITS
                on = unit < s[COUNT]
                value_b = jnp.where(on, value, 0.0).astype(BF16)
                gated[rows, cols] = value_b
                slope[rows, cols] = jnp.where(on, grad, 0.0).astype(BF16)
                acc[...] += dot(value_b, wd[cols, :])
                return inner

            lax.fori_loop(0, s[CHUNKS], chunk, 0)
            save(3, gated, gated_hbm, block).start()
            save(4, slope, slope_hbm, block).start()
            hat_two, inverse_two = norm_parts(acc[...])
            x2[rows, :] = hat_two.astype(BF16)
            save(6, x2, x2_hbm, block).start()
            kept = stat[rows, :]
            kept = jnp.where(lane == HEADS, inverse_one, kept)
            stat[rows, :] = jnp.where(lane == HEADS + 1, inverse_two, kept)
            save(2, stat, stat_hbm, block).start()
            result = hat_two * vec_row(vec, V_G2) + vec_row(vec, V_B2)
            emit(block, jnp.where(live_column(s, block), result, 0.0))
            return carry

        lax.fori_loop(0, blocks, finish, 0)

    @pl.when(s[SKIP] == 1)
    def _():
        def carry_on(block, carry):
            value = h[rows_at(block), :].astype(F32)
            emit(block, jnp.where(live_column(s, block), value, 0.0) if last else value)
            return carry

        lax.fori_loop(0, live, carry_on, 0)

    if last:
        def clear(block, carry):
            emit(block, jnp.zeros((ROWS, width), F32))
            return carry

        lax.fori_loop(live, most, clear, 0)

    for block in range(most):
        @pl.when(block < blocks)
        def _(block=block):
            save(0, proj, proj_hbm, block).wait()
            save(1, ctx, ctx_hbm, block).wait()
            save(2, stat, stat_hbm, block).wait()
            save(3, gated, gated_hbm, block).wait()
            save(4, slope, slope_hbm, block).wait()
            save(5, x1, x1_hbm, block).wait()
            save(6, x2, x2_hbm, block).wait()

        if last:
            save(7, out_a, keep_hbm, block).wait()
            save(8, out_b, send_hbm, block).wait()
        else:
            pl.when(block < live)(lambda block=block: save(7, out_b, pass_hbm, block).wait())


HBM = pl.BlockSpec(memory_space=pltpu.HBM)
SMEM = pl.BlockSpec(memory_space=pltpu.SMEM)


def layer_forward(last, scalars, x, weights):
    length, width = x.shape[-2:]
    units = weights[4].shape[1]
    shape = jax.ShapeDtypeStruct
    outs = (
        [shape((length, width // 2), F32), shape((length, width // 2), BF16)]
        if last
        else [shape((length, width), BF16)]
    )
    outs += [
        shape((length, 3 * width), BF16),
        shape((length, width), BF16),
        shape((length, 128), F32),
        shape((length, units), BF16),
        shape((length, units), BF16),
        shape((length, width), BF16),
        shape((length, width), BF16),
    ]
    out_width = width // 2 if last else width
    blocks = length // ROWS
    return pl.pallas_call(
        functools.partial(forward_kernel, last),
        out_shape=outs,
        in_specs=[SMEM] + [HBM] * 11,
        out_specs=[HBM] * len(outs),
        scratch_shapes=[
            pltpu.VMEM((length, width), BF16),
            pltpu.VMEM((width, 3 * width), BF16),
            pltpu.VMEM((width, width), BF16),
            pltpu.VMEM((width, units), BF16),
            pltpu.VMEM((units, width), BF16),
            pltpu.VMEM(weights[8].shape, BF16),
            pltpu.VMEM((length, 3 * width), BF16),
            pltpu.VMEM((length, width), BF16),
            pltpu.VMEM((length, 128), F32),
            pltpu.VMEM((length, units), BF16),
            pltpu.VMEM((length, units), BF16),
            pltpu.VMEM((length, width), BF16),
            pltpu.VMEM((length, width), BF16),
            pltpu.VMEM((ROWS, width), F32),
            pltpu.VMEM((ROWS, width), BF16),
            pltpu.VMEM((8, units), F32),
            pltpu.VMEM((length if last else 8, width // 2), F32),
            pltpu.VMEM((length, out_width), BF16),
            pltpu.SemaphoreType.DMA((blocks,)),
            pltpu.SemaphoreType.DMA((5,)),
            pltpu.SemaphoreType.DMA((9, blocks)),
        ],
        compiler_params=pltpu.CompilerParams(vmem_limit_bytes=VMEM_BYTES),
        name="layer_forward",
    )(scalars, x, *weights)


def ffn_back_kernel(
    first_pass,
    s,
    g_hbm,
    wu0, wu1, wd0, wd1, v0, v1,
    stat_hbm, gated_hbm, slope_hbm, x1_hbm, x2_hbm,
    *rest,
):
    if not first_pass:
        rest = rest[5:]
    (
    res_hbm, gd_keep, gd_send, gu_keep, gu_send, vec_hbm,
    g_out, wu, wd, vec, stat, gated, slope, x1, x2, res, down, normed, gd, gu, acc, sums, sums_up,
    in_sem, w_sem, out_sem, gd_sem, gu_sem,
    ) = rest
    layer = 1 if first_pass else 0
    most = g_out.shape[0] // ROWS
    width = g_out.shape[1]
    units = wu.shape[1]
    chunks = units // UNITS
    blocks = s[BLOCKS]

    def load(what, block):
        target, source = (
            (g_out, g_hbm.at[s[SLOT]] if first_pass else g_hbm),
            (stat, stat_hbm), (gated, gated_hbm), (slope, slope_hbm), (x1, x1_hbm), (x2, x2_hbm),
        )[what]
        return pltpu.make_async_copy(
            source.at[rows_at(block)], target.at[rows_at(block)], in_sem.at[what, block]
        )

    @pl.when(blocks > 0)
    def _():
        fetch_start(s, vec, v0, v1, w_sem.at[0])

    for block in range(most):
        @pl.when(block < blocks)
        def _(block=block):
            for what in (0, 1, 5, 3, 4):
                load(what, block).start()

        if block == 0:
            @pl.when(blocks > 0)
            def _():
                fetch_start(s, wd, wd0, wd1, w_sem.at[2])
                fetch_start(s, wu, wu0, wu1, w_sem.at[1])

    for block in range(most):
        pl.when(block < blocks)(lambda block=block: load(2, block).start())

    sums[...] = jnp.zeros(sums.shape, F32)
    sums_up[...] = jnp.zeros(sums_up.shape, F32)

    @pl.when(blocks > 0)
    def _():
        pltpu.make_async_copy(v0, vec, w_sem.at[0]).wait()

        def step(block, carry):
            rows = rows_at(block)
            for what in (0, 1, 5):
                load(what, block).wait()
            inverse_one = stat[rows, HEADS : HEADS + 1]
            inverse_two = stat[rows, HEADS + 1 : HEADS + 2]
            gn = jnp.where(live_column(s, block), g_out[rows, :].astype(F32), 0.0)
            hat = x2[rows, :].astype(F32)
            sums[2:3, :] += jnp.sum(gn * hat, axis=0, keepdims=True)
            sums[3:4, :] += jnp.sum(gn, axis=0, keepdims=True)
            gh = gn * vec_row(vec, V_G2)
            mean_one = jnp.mean(gh, axis=-1, keepdims=True)
            mean_two = jnp.mean(gh * hat, axis=-1, keepdims=True)
            g_res = (gh - mean_one - hat * mean_two) * inverse_two
            down_b = g_res.astype(BF16)
            sums[4:5, :] += jnp.sum(down_b.astype(F32), axis=0, keepdims=True)
            down[rows, :] = down_b
            acc[...] = g_res

            @pl.when(block == 0)
            def _():
                pltpu.make_async_copy(wd0, wd, w_sem.at[2]).wait()
                pltpu.make_async_copy(wu0, wu, w_sem.at[1]).wait()

            load(3, block).wait()
            load(4, block).wait()

            def chunk(c, inner):
                cols = cols_at(c * UNITS, UNITS)
                g_gated = dot_nt(down[rows, :], wd[cols, :])
                lift = (g_gated * slope[rows, cols].astype(F32)).astype(BF16)
                slope[rows, cols] = lift
                sums_up[0:1, cols] += jnp.sum(lift.astype(F32), axis=0, keepdims=True)
                acc[...] += dot_nt(lift, wu[:, cols])
                return inner

            lax.fori_loop(0, s[CHUNKS], chunk, 0)
            g_normed = acc[...]
            hat = x1[rows, :].astype(F32)
            normed[rows, :] = (hat * vec_row(vec, V_G1) + vec_row(vec, V_B1)).astype(BF16)
            sums[0:1, :] += jnp.sum(g_normed * hat, axis=0, keepdims=True)
            sums[1:2, :] += jnp.sum(g_normed, axis=0, keepdims=True)
            gh = g_normed * vec_row(vec, V_G1)
            mean_one = jnp.mean(gh, axis=-1, keepdims=True)
            mean_two = jnp.mean(gh * hat, axis=-1, keepdims=True)
            res[rows, :] = (gh - mean_one - hat * mean_two) * inverse_one
            pltpu.make_async_copy(res.at[rows], res_hbm.at[rows], out_sem.at[block]).start()
            return carry

        lax.fori_loop(0, blocks, step, 0)
        for block in range(most):
            pl.when(block < blocks)(lambda block=block: load(2, block).wait())


    half_rows = units // 2
    half_cols = units // 2
    per_half = chunks // 2

    def chunk_copies(c):
        half, inside = c // per_half, c % per_half
        down_part = gd.at[cols_at(c * UNITS, UNITS), :]
        up_part = gu.at[:, cols_at(c * UNITS, UNITS)]
        place = cols_at(inside * UNITS, UNITS)
        return half, down_part, up_part, place

    def send_chunk(c):
        half, down_part, up_part, place = chunk_copies(c)

        @pl.when(half == s[SECTION])
        def _():
            pltpu.make_async_copy(down_part, gd_keep.at[layer, place, :], gd_sem.at[c]).start()
            pltpu.make_async_copy(up_part, gu_keep.at[layer, :, place], gu_sem.at[c]).start()

        @pl.when(half != s[SECTION])
        def _():
            pltpu.make_async_copy(down_part, gd_send.at[layer, place, :], gd_sem.at[c]).start()
            pltpu.make_async_copy(up_part, gu_send.at[layer, :, place], gu_sem.at[c]).start()

    def weigh(count):
        span = count * ROWS

        def one(c, carry):
            cols = cols_at(c * UNITS, UNITS)
            gd[cols, :] = dot_tn(gated[0:span, cols], down[0:span, :]).astype(BF16)
            gu[:, cols] = dot_tn(normed[0:span, :], slope[0:span, cols]).astype(BF16)
            send_chunk(c)
            return carry

        lax.fori_loop(0, s[CHUNKS], one, 0)

    by_blocks(blocks, most, weigh)

    def nothing(c, carry):
        cols = cols_at(c * UNITS, UNITS)
        gd[cols, :] = jnp.zeros((UNITS, width), BF16)
        gu[:, cols] = jnp.zeros((width, UNITS), BF16)
        send_chunk(c)
        return carry

    lax.fori_loop(s[CHUNKS], chunks, nothing, 0)

    for c in range(chunks):
        _, down_part, up_part, place = chunk_copies(c)
        pltpu.make_async_copy(down_part, gd_keep.at[layer, place, :], gd_sem.at[c]).wait()
        pltpu.make_async_copy(up_part, gu_keep.at[layer, :, place], gu_sem.at[c]).wait()
    for piece in range(units // width):
        sums[8 + piece : 9 + piece, :] = sums_up[0:1, piece * width : (piece + 1) * width]
    pltpu.sync_copy(sums, vec_hbm.at[layer, 0:16])
    for block in range(most):
        @pl.when(block < blocks)
        def _(block=block):
            rows = rows_at(block)
            pltpu.make_async_copy(res.at[rows], res_hbm.at[rows], out_sem.at[block]).wait()


def ffn_back(first_pass, scalars, g_out, weights, saved, grads=()):
    length, width = g_out.shape[-2:]
    units = weights[4].shape[1]
    blocks = length // ROWS
    chunks = units // UNITS
    shape = jax.ShapeDtypeStruct
    _, _, stat, gated, slope, x1, x2 = saved
    return pl.pallas_call(
        functools.partial(ffn_back_kernel, first_pass),
        out_shape=[
            shape((length, width), F32),
            shape((2, units // 2, width), BF16),
            shape((2, units // 2, width), BF16),
            shape((2, width, units // 2), BF16),
            shape((2, width, units // 2), BF16),
            shape((2, 24, width), F32),
        ],
        in_specs=[SMEM] + [HBM] * (12 + len(grads)),
        out_specs=[HBM] * 6,
        input_output_aliases={13 + i: 1 + i for i in range(len(grads))},
        scratch_shapes=[
            pltpu.VMEM((length, width), BF16),
            pltpu.VMEM((width, units), BF16),
            pltpu.VMEM((units, width), BF16),
            pltpu.VMEM(weights[8].shape, BF16),
            pltpu.VMEM((length, 128), F32),
            pltpu.VMEM((length, units), BF16),
            pltpu.VMEM((length, units), BF16),
            pltpu.VMEM((length, width), BF16),
            pltpu.VMEM((length, width), BF16),
            pltpu.VMEM((length, width), F32),
            pltpu.VMEM((length, width), BF16),
            pltpu.VMEM((length, width), BF16),
            pltpu.VMEM((units, width), BF16),
            pltpu.VMEM((width, units), BF16),
            pltpu.VMEM((ROWS, width), F32),
            pltpu.VMEM((16, width), F32),
            pltpu.VMEM((8, units), F32),
            pltpu.SemaphoreType.DMA((6, blocks)),
            pltpu.SemaphoreType.DMA((3,)),
            pltpu.SemaphoreType.DMA((blocks,)),
            pltpu.SemaphoreType.DMA((chunks,)),
            pltpu.SemaphoreType.DMA((chunks,)),
        ],
        compiler_params=pltpu.CompilerParams(vmem_limit_bytes=VMEM_BYTES),
        name="ffn_back",
    )(scalars, g_out, *weights[4:8], *weights[8:10], stat, gated, slope, x1, x2, *grads)


def attention_back_kernel(
    first_layer,
    s,
    res_hbm, g_hbm, x_hbm,
    wq0, wq1, wo0, wo1,
    proj_hbm, ctx_hbm, stat_hbm,
    *rest,
):
    layer = 0 if first_layer else 1
    rest = rest[3 if first_layer else 1 :]
    if first_layer:
        in_keep, in_send = rest[:2]
        rest = rest[2:]
    else:
        in_hbm = rest[0]
        rest = rest[1:]
    (
        ga_keep, ga_send, vec_hbm,
        res, g_in, h, wq, wo, proj, ctx, stat, attn, g_ctx, g_proj, rows_log, rows_delta, g_q,
        go, gq, out_a, out_b, sums,
        in_sem, w_sem, out_sem, go_sem, gq_sem,
    ) = rest
    most = res.shape[0] // ROWS
    width = res.shape[1]
    half = width // 2
    pairs_all = width // 128
    blocks = s[BLOCKS]
    live = s[LIVE]
    lane = lax.broadcasted_iota(jnp.int32, (1, 128), 1)
    low = lane < 64
    zero_pair = jnp.zeros((1, 128), BF16)

    def load(what, block):
        target, source = (
            (res, res_hbm), (ctx, ctx_hbm), (stat, stat_hbm), (proj, proj_hbm),
            (h, x_hbm.at[s[SLOT]] if first_layer else x_hbm),
        )[what]
        return pltpu.make_async_copy(
            source.at[rows_at(block)], target.at[rows_at(block)], in_sem.at[what, block]
        )

    def load_g(block):
        source = g_hbm if first_layer else g_hbm.at[s[SLOT]]
        return pltpu.make_async_copy(
            source.at[rows_at(block)], g_in.at[rows_at(block)], in_sem.at[0, block]
        )

    for what in (0, 1):
        for block in range(most):
            pl.when(block < blocks)(lambda what=what, block=block: load(what, block).start())

    @pl.when(blocks > 0)
    def _():
        fetch_start(s, wo, wo0, wo1, w_sem.at[0])

    for what in (2, 3, 4):
        for block in range(most):
            pl.when(block < blocks)(lambda what=what, block=block: load(what, block).start())

    @pl.when(blocks > 0)
    def _():
        fetch_start(s, wq, wq0, wq1, w_sem.at[1])

    sums[...] = jnp.zeros(sums.shape, F32)

    def out_copies(block, wait):
        rows = rows_at(block)
        if first_layer:
            copies = [
                pltpu.make_async_copy(out_a.at[rows], in_keep.at[rows], out_sem.at[0, block]),
                pltpu.make_async_copy(out_b.at[rows], in_send.at[rows], out_sem.at[1, block]),
            ]
        else:
            copies = [pltpu.make_async_copy(out_b.at[rows], in_hbm.at[rows], out_sem.at[0, block])]
        for copy in copies:
            copy.wait() if wait else copy.start()

    def emit(block, value):
        rows = rows_at(block)
        if first_layer:
            front = s[SECTION] == 0
            out_a[rows, :] = jnp.where(front, value[:, :half], value[:, half:])
            out_b[rows, :] = jnp.where(front, value[:, half:], value[:, :half]).astype(BF16)
        else:
            out_b[rows, :] = value.astype(BF16)
        out_copies(block, False)

    def go_copy(part, keep):
        target = (ga_keep if keep else ga_send).at[layer, :, 0:half]
        return pltpu.make_async_copy(go.at[:, part * half : (part + 1) * half], target, go_sem.at[part])

    def gq_copy(part, keep):
        target = (ga_keep if keep else ga_send).at[layer, :, half : 4 * half]
        cols = slice(part * 3 * half, (part + 1) * 3 * half)
        return pltpu.make_async_copy(gq.at[:, cols], target, gq_sem.at[part])

    def start_halves(make):
        for part in range(2):
            pl.when(s[SECTION] == part)(lambda part=part: make(part, True).start())
            pl.when(s[SECTION] != part)(lambda part=part: make(part, False).start())

    @pl.when(blocks > 0)
    def _():
        pltpu.make_async_copy(wo0, wo, w_sem.at[0]).wait()
        spread = (
            lax.broadcasted_iota(jnp.int32, (128, width), 1) // 64
            == lax.broadcasted_iota(jnp.int32, (128, width), 0)
        ).astype(BF16)

        def before(block, carry):
            rows = rows_at(block)
            load(0, block).wait()
            load(1, block).wait()
            attn_b = res[rows, :].astype(BF16)
            attn[rows, :] = attn_b
            sums[2:3, :] += jnp.sum(attn_b.astype(F32), axis=0, keepdims=True)
            g_context = dot_nt(attn_b, wo[...]).astype(BF16)
            g_ctx[rows, :] = g_context
            product = (g_context.astype(F32) * ctx[rows, :].astype(F32)).astype(BF16)
            rows_delta[:, rows] = dot_nt(spread, product)
            load(2, block).wait()
            rows_log[:, rows] = stat[rows, :].T
            load(3, block).wait()
            return carry

        lax.fori_loop(0, blocks, before, 0)

        def weigh_out(count):
            span = count * ROWS
            go[...] = dot_tn(ctx[0:span, :], attn[0:span, :]).astype(BF16)

        by_blocks(blocks, most, weigh_out)
        start_halves(go_copy)

        for pair in range(pairs_all):
            @pl.when(pair >= s[PAIRS])
            def _(pair=pair):
                for part in range(3):
                    cols = slice(part * width + pair * 128, part * width + (pair + 1) * 128)
                    g_proj[:, cols] = jnp.zeros((g_proj.shape[0], 128), BF16)

        def attend_back(count):
            span = count * ROWS

            def one_pair(pair, carry):
                cols = cols_at(pair * 128, 128)
                g_q[0:span, :] = jnp.zeros((span, 128), F32)

                def one_block(block, inner):
                    rows = rows_at(block)
                    q = proj[0:span, cols]
                    d_ctx = g_ctx[0:span, cols]
                    k = proj[rows, cols_at(width + pair * 128, 128)] * jnp.asarray(0.125, BF16)
                    v = proj[rows, cols_at(2 * width + pair * 128, 128)]
                    fill = jnp.where(live_column(s, block), 0.0, NEG_FILL)
                    found_k, found_v, found_q = [], [], []
                    for head, own in ((0, low), (1, ~low)):
                        k_own = jnp.where(own, k, zero_pair)
                        v_own = jnp.where(own, v, zero_pair)
                        log_row = rows_log[pl.ds(2 * pair + head, 1), 0:span]
                        delta_row = rows_delta[pl.ds(2 * pair + head, 1), 0:span]
                        probs = jnp.exp(dot_nt(k_own, q) + fill - log_row)
                        g_probs = dot_nt(v_own, d_ctx)
                        g_scores = (probs * (g_probs - delta_row)).astype(BF16)
                        found_v.append(dot(probs.astype(BF16), d_ctx))
                        found_k.append(dot(g_scores, q))
                        found_q.append(dot_tn(g_scores, k_own))
                    g_q[0:span, :] += found_q[0] + found_q[1]
                    g_k = jnp.where(low, found_k[0], found_k[1]) * 0.125
                    g_v = jnp.where(low, found_v[0], found_v[1])
                    g_proj[rows, cols_at(width + pair * 128, 128)] = g_k.astype(BF16)
                    g_proj[rows, cols_at(2 * width + pair * 128, 128)] = g_v.astype(BF16)
                    return inner

                lax.fori_loop(0, count, one_block, 0)
                g_proj[0:span, cols] = g_q[0:span, :].astype(BF16)
                return carry

            lax.fori_loop(0, s[PAIRS], one_pair, 0)

        by_blocks(blocks, most, attend_back)

        for block in range(most):
            pl.when(block < blocks)(lambda block=block: load(4, block).wait())
        pltpu.make_async_copy(wq0, wq, w_sem.at[1]).wait()

        def weigh_in(count):
            span = count * ROWS

            def one(part, carry):
                cols = cols_at(part * width, width)
                gq[:, cols] = dot_tn(h[0:span, :], g_proj[0:span, cols]).astype(BF16)
                return carry

            lax.fori_loop(0, 3, one, 0)

        by_blocks(blocks, most, weigh_in)
        start_halves(gq_copy)

        def after(block, carry):
            rows = rows_at(block)
            grad = g_proj[rows, :]
            sums[0:1, :] += jnp.sum(grad[:, :width].astype(F32), axis=0, keepdims=True)
            sums[1:2, :] += jnp.sum(grad[:, 2 * width :].astype(F32), axis=0, keepdims=True)
            emit(block, res[rows, :] + dot_nt(grad, wq[...]))
            return carry

        lax.fori_loop(0, blocks, after, 0)

    @pl.when(s[SKIP] == 1)
    def _():
        go[...] = jnp.zeros(go.shape, BF16)
        gq[...] = jnp.zeros(gq.shape, BF16)
        start_halves(go_copy)
        start_halves(gq_copy)
        for block in range(most):
            pl.when(block < live)(lambda block=block: load_g(block).start())
        for block in range(most):
            pl.when(block < live)(lambda block=block: load_g(block).wait())

        def carry_on(block, carry):
            value = g_in[rows_at(block), :].astype(F32)
            emit(block, jnp.where(live_column(s, block), value, 0.0))
            return carry

        lax.fori_loop(0, live, carry_on, 0)

    if first_layer:
        def clear(block, carry):
            emit(block, jnp.zeros((ROWS, width), F32))
            return carry

        lax.fori_loop(live, most, clear, 0)

    pltpu.sync_copy(sums, vec_hbm.at[layer, 16:24])
    for part in range(2):
        go_copy(part, True).wait()
        gq_copy(part, True).wait()
    for block in range(most):
        if first_layer:
            out_copies(block, True)
        else:
            pl.when(block < live)(lambda block=block: out_copies(block, True))


def attention_back(first_layer, scalars, res, g_out, x, weights, saved, grads=()):
    length, width = res.shape
    blocks = length // ROWS
    shape = jax.ShapeDtypeStruct
    proj, ctx, stat = saved[:3]
    outs = (
        [shape((length, width // 2), F32), shape((length, width // 2), BF16)]
        if first_layer
        else [shape((length, width), BF16)]
    )
    outs += [
        shape((2, width, 2 * width), BF16),
        shape((2, width, 2 * width), BF16),
        shape((2, 24, width), F32),
    ]
    return pl.pallas_call(
        functools.partial(attention_back_kernel, first_layer),
        out_shape=outs,
        in_specs=[SMEM] + [HBM] * (10 + len(grads)),
        out_specs=[HBM] * len(outs),
        input_output_aliases={11 + i: len(outs) - len(grads) + i for i in range(len(grads))},
        scratch_shapes=[
            pltpu.VMEM((length, width), F32),
            pltpu.VMEM((length, width), BF16),
            pltpu.VMEM((length, width), BF16),
            pltpu.VMEM((width, 3 * width), BF16),
            pltpu.VMEM((width, width), BF16),
            pltpu.VMEM((length, 3 * width), BF16),
            pltpu.VMEM((length, width), BF16),
            pltpu.VMEM((length, 128), F32),
            pltpu.VMEM((length, width), BF16),
            pltpu.VMEM((length, width), BF16),
            pltpu.VMEM((length, 3 * width), BF16),
            pltpu.VMEM((128, length), F32),
            pltpu.VMEM((128, length), F32),
            pltpu.VMEM((length, 128), F32),
            pltpu.VMEM((width, width), BF16),
            pltpu.VMEM((width, 3 * width), BF16),
            pltpu.VMEM((length if first_layer else 8, width // 2), F32),
            pltpu.VMEM((length, width // 2 if first_layer else width), BF16),
            pltpu.VMEM((8, width), F32),
            pltpu.SemaphoreType.DMA((5, blocks)),
            pltpu.SemaphoreType.DMA((2,)),
            pltpu.SemaphoreType.DMA((2, blocks)),
            pltpu.SemaphoreType.DMA((2,)),
            pltpu.SemaphoreType.DMA((2,)),
        ],
        compiler_params=pltpu.CompilerParams(vmem_limit_bytes=VMEM_BYTES),
        name="attention_back",
    )(scalars, res, g_out, x, *weights[0:4], proj, ctx, stat, *grads)


def swap(part):
    return lax.ppermute(part, "section", [(0, 1), (1, 0)])


def across(part, bit):
    pairs = [(i, i ^ 1 << bit) for i in range(lax.axis_size("dp"))]
    return lax.ppermute(part, "dp", pairs)


FREE = pl.CostEstimate(flops=0, bytes_accessed=0, transcendentals=0)
LONG = pl.CostEstimate(flops=20_000_000_000, bytes_accessed=0, transcendentals=0)


def my_bit(bit):
    return (lax.axis_index("dp") >> bit) & 1


def half_sum_kernel(bit, turn, keep, got, before, out, own, new, in_sem, out_sem):
    layers, rows, _ = keep.shape
    half = rows // 2
    at = 1 - my_bit(bit) if turn == 0 else my_bit(bit)
    place = pl.ds(pl.multiple_of(at * half, 16), half)

    def loads(layer):
        return [
            pltpu.make_async_copy(keep.at[layer, place], own.at[layer], in_sem.at[layer, 0]),
            pltpu.make_async_copy(got.at[layer, place], new.at[layer], in_sem.at[layer, 1]),
        ]

    def store(layer):
        return pltpu.make_async_copy(own.at[layer], out.at[layer], out_sem.at[layer])

    for layer in range(layers):
        for copy in loads(layer):
            copy.start()
    for layer in range(layers):
        for copy in loads(layer):
            copy.wait()

        def add_rows(i, carry, layer=layer):
            place = pl.ds(pl.multiple_of(i * 16, 16), 16)
            total = own[layer, place, :].astype(F32) + new[layer, place, :].astype(F32)
            own[layer, place, :] = total.astype(BF16)
            return carry

        lax.fori_loop(0, half // 16, add_rows, 0, unroll=3)
        store(layer).start()
    for layer in range(layers):
        store(layer).wait()


def half_sum(bit, turn, keep, got, before):
    layers, rows, cols = keep.shape
    half = rows // 2
    if half % 48:
        at = 1 - my_bit(bit) if turn == 0 else my_bit(bit)
        own, new = [lax.dynamic_slice_in_dim(a, at * half, half, 1).astype(F32) for a in (keep, got)]
        return (own + new).astype(BF16)
    return pl.pallas_call(
        functools.partial(half_sum_kernel, bit, turn),
        out_shape=jax.ShapeDtypeStruct((layers, half, cols), BF16),
        in_specs=[HBM, HBM, HBM],
        out_specs=HBM,
        scratch_shapes=[
            pltpu.VMEM((layers, half, cols), BF16),
            pltpu.VMEM((layers, half, cols), BF16),
            pltpu.SemaphoreType.DMA((layers, 2)),
            pltpu.SemaphoreType.DMA((layers,)),
        ],
        compiler_params=pltpu.CompilerParams(vmem_limit_bytes=VMEM_BYTES),
        cost_estimate=FREE,
        name="half_sum",
    )(keep, got, before)


def add_kernel(one, two, before, out):
    out[...] = (one[...].astype(F32) + two[...].astype(F32)).astype(out.dtype)


def add(one, two, before):
    whole = pl.BlockSpec(memory_space=pltpu.VMEM)
    return pl.pallas_call(
        add_kernel,
        out_shape=jax.ShapeDtypeStruct(one.shape, one.dtype),
        in_specs=[whole, whole, HBM],
        out_specs=whole,
        cost_estimate=FREE,
        name="add",
    )(one, two, before)


def join_kernel(bit, part, got, before, both, held, in_sem, out_sem):
    layers, rows, _ = part.shape
    mine = my_bit(bit)
    steps = [(at, layer) for at in range(2) for layer in range(layers)]

    def load(at, layer):
        source = (part, got)[at].at[layer]
        return pltpu.make_async_copy(source, held.at[at, layer], in_sem.at[at, layer])

    def store(at, layer):
        place = mine if at == 0 else 1 - mine
        target = both.at[layer, pl.ds(pl.multiple_of(place * rows, 16), rows)]
        return pltpu.make_async_copy(held.at[at, layer], target, out_sem.at[at, layer])

    for step in steps:
        load(*step).start()
    for step in steps:
        load(*step).wait()
        store(*step).start()
    for step in steps:
        store(*step).wait()


def join(bit, part, got, before):
    layers, rows, cols = part.shape
    if rows % 16:
        at = jnp.arange(2)[:, None, None]
        both = jnp.where(at == my_bit(bit), part[:, None], got[:, None])
        return both.reshape(layers, 2 * rows, cols)
    return pl.pallas_call(
        functools.partial(join_kernel, bit),
        out_shape=jax.ShapeDtypeStruct((layers, 2 * rows, cols), BF16),
        in_specs=[HBM, HBM, HBM],
        out_specs=HBM,
        scratch_shapes=[
            pltpu.VMEM((2, layers, rows, cols), BF16),
            pltpu.SemaphoreType.DMA((2, layers)),
            pltpu.SemaphoreType.DMA((2, layers)),
        ],
        compiler_params=pltpu.CompilerParams(vmem_limit_bytes=VMEM_BYTES),
        cost_estimate=FREE,
        name="join",
    )(part, got, before)


class Stream:
    def __init__(self, layers, keep, send, order):
        self.layers, self.keep, self.send, self.order = layers, keep, send, order

    def enter(self):
        self.got = swap(self.send)

    def send_half(self, turn, chain):
        bit = self.order[turn]
        self.old = (self.keep, self.got)
        send = half_sum(bit, 0, *self.old, chain[-1])
        chain.append(send)
        self.got = across(send, bit)

    def keep_half(self, turn, chain):
        self.keep = half_sum(self.order[turn], 1, *self.old, chain[-1])
        chain.append(self.keep)

    def exchange(self, chain):
        section = lax.axis_index("section")
        part = add(self.keep, self.got, chain[-1])
        chain.append(part)
        if len(self.layers) == 1:
            self.own = part
            live = self.layers[0]
            self.got = lax.ppermute(part, "section", [(1 - live, live)])
        else:
            self.own = lax.dynamic_slice_in_dim(part, section, 1)
            self.got = swap(lax.dynamic_slice_in_dim(part, 1 - section, 1))

    def gather(self, turn, chain):
        bits = len(self.order)
        bit = self.order[bits - 1 - turn]
        if turn == 0:
            place = jnp.arange(2)[:, None, None]
            self.part = jnp.where(place == lax.axis_index("section"), self.own, self.got)
        else:
            self.part = join(self.order[bits - turn], self.part, self.got, chain[-1])
        chain.append(self.part)
        if len(self.layers) == 1:
            devices = lax.axis_size("dp")
            first = self.layers[0] * devices
            pairs = [(first + i, first + (i ^ 1 << bit)) for i in range(devices)]
            self.got = lax.ppermute(self.part, ("section", "dp"), pairs)
        else:
            self.got = across(self.part, bit)


def place_kernel(kind, turn, layers, first_bit, part, *refs):
    outs_count = 2 if kind == "attn" else 1
    refs = refs[outs_count + 1 if turn else 1 :]
    outs = refs[:outs_count]
    held, wide, in_sem, out_sem = refs[outs_count:]
    rows, cols = held.shape[1:]
    side = my_bit(first_bit) if turn == 0 else 1 - my_bit(first_bit)
    live = True if len(layers) == 2 else lax.axis_index("section") == layers[0]

    def target(half, at):
        if kind == "rows":
            return outs[0].at[0, pl.ds(pl.multiple_of((2 * half + side) * rows, 8), rows), :]
        at_rows = pl.ds(pl.multiple_of(side * rows, 8), rows)
        width = cols if kind == "cols" else (cols // 4 if at == 0 else 3 * cols // 4)
        return outs[at].at[0, at_rows, half * width : (half + 1) * width]

    def out_copies(half, wait):
        pieces = [(0, slice(0, cols))]
        if kind == "attn":
            pieces = [(0, slice(0, cols // 4)), (1, slice(cols // 4, cols))]
        for at, where in pieces:
            copy = pltpu.make_async_copy(wide.at[half, :, where], target(half, at), out_sem.at[half, at])
            copy.wait() if wait else copy.start()

    def load(half):
        return pltpu.make_async_copy(part.at[half], held.at[half], in_sem.at[half])

    for half in range(2):
        load(half).start()
    for half in range(2):
        load(half).wait()

        def convert(i, carry, half=half):
            at = pl.ds(pl.multiple_of(i * 16, 16), 16)
            value = held[half, at, :].astype(F32)
            wide[half, at, :] = value if live is True else jnp.where(live, value, 0.0)
            return carry

        lax.fori_loop(0, rows // 16, convert, 0, unroll=2)
        out_copies(half, False)
    for half in range(2):
        out_copies(half, True)


def place(kind, turn, layers, first_bit, part, shapes, extra):
    rows, cols = part.shape[1:]
    return pl.pallas_call(
        functools.partial(place_kernel, kind, turn, layers, first_bit),
        out_shape=[jax.ShapeDtypeStruct(out, F32) for out in shapes],
        in_specs=[HBM] * (1 + len(extra)),
        out_specs=[HBM] * len(shapes),
        input_output_aliases={1 + i: i for i in range(len(shapes))} if turn else {},
        scratch_shapes=[
            pltpu.VMEM((2, rows, cols), BF16),
            pltpu.VMEM((2, rows, cols), F32),
            pltpu.SemaphoreType.DMA((2,)),
            pltpu.SemaphoreType.DMA((2, 2)),
        ],
        compiler_params=pltpu.CompilerParams(vmem_limit_bytes=VMEM_BYTES),
        cost_estimate=LONG,
        name="place_" + kind,
    )(part, *extra)


def slots_kernel(keep, got, before, out, own, new, wide, in_sem, out_sem):
    section = lax.axis_index("section")
    mine = pltpu.make_async_copy(keep, own, in_sem.at[0])
    theirs = pltpu.make_async_copy(got, new, in_sem.at[1])
    mine.start()
    theirs.start()
    mine.wait()
    store_mine = pltpu.make_async_copy(own, out.at[section], out_sem.at[0])
    store_mine.start()
    theirs.wait()

    def convert(i, carry):
        at = pl.ds(pl.multiple_of(i * 32, 32), 32)
        wide[at, :] = new[at, :].astype(F32)
        return carry

    lax.fori_loop(0, new.shape[0] // 32, convert, 0)
    store_theirs = pltpu.make_async_copy(wide, out.at[1 - section], out_sem.at[1])
    store_theirs.start()
    store_mine.wait()
    store_theirs.wait()


def both_slots(keep, got, before):
    return pl.pallas_call(
        slots_kernel,
        out_shape=jax.ShapeDtypeStruct((2, *keep.shape), F32),
        in_specs=[HBM, HBM, HBM],
        out_specs=HBM,
        scratch_shapes=[
            pltpu.VMEM(keep.shape, F32),
            pltpu.VMEM(keep.shape, BF16),
            pltpu.VMEM(keep.shape, F32),
            pltpu.SemaphoreType.DMA((2,)),
            pltpu.SemaphoreType.DMA((2,)),
        ],
        compiler_params=pltpu.CompilerParams(vmem_limit_bytes=VMEM_BYTES),
        cost_estimate=FREE,
        name="both_slots",
    )(keep, got, before)


def tail(layers, grads, vecs, outs, ins, weight_shapes):
    section = lax.axis_index("section")
    bits = lax.axis_size("dp").bit_length() - 1
    by_x = list(range(bits))
    orders = (by_x[:1] + by_x[2:] + by_x[1:2], [1, 0] + by_x[2:], by_x[2:-1] + [1, 0] + by_x[-1:])
    streams = []
    for (keep, send), order in zip(grads, orders):
        if len(layers) == 1:
            keep, send = [a[layers[0] : layers[0] + 1] for a in (keep, send)]
        streams.append(Stream(layers, keep, send, order))
    for stream in streams:
        stream.enter()
    out_got, in_got = swap(outs[1]), swap(ins[1])
    chain = [ins[1]]
    total = lax.dynamic_slice_in_dim(vecs, section, 1)[0]
    vec_got = swap(lax.dynamic_slice_in_dim(vecs, 1 - section, 1)[0])
    for turn in range(bits):
        for stream in streams:
            stream.send_half(turn, chain)
        for stream in streams:
            stream.keep_half(turn, chain)
        total = add(total, vec_got, chain[-1])
        chain.append(total)
        vec_got = across(total, by_x[turn])
        if turn == 0:
            out_half = both_slots(outs[0], out_got, chain[-1])
            grad_half = both_slots(ins[0], in_got, out_half)
            chain.append(grad_half)
    for stream in streams:
        stream.exchange(chain)
    total = add(total, vec_got, chain[-1])
    for turn in range(bits):
        for stream in streams:
            stream.gather(turn, chain)
    kinds = ("rows", "cols", "attn")
    placed, results = [], []
    for kind, stream, shapes in zip(kinds, streams, weight_shapes):
        placed.append(place(kind, 0, layers, stream.order[0], stream.part, shapes, [chain[-1]]))
        chain.append(placed[-1][0])
    for kind, stream, shapes, half in zip(kinds, streams, weight_shapes, placed):
        half = [*half, chain[-1]]
        results += place(kind, 1, layers, stream.order[0], stream.got, shapes, half)
        chain.append(results[-1])
    return (*results, total, out_half, grad_half)


def on_device(
    inputs, cotangent, lengths, assignment, skip_flags, head_counts, ffn_counts,
    w_qkv, bias_q, bias_v, w_out, bias_out, norm1_gain, norm1_bias, w_up, bias_up, w_down,
    bias_down, norm2_gain, norm2_bias,
):
    section = lax.axis_index("section")
    first = section == 0
    slots, length, width = inputs.shape
    units = w_up.shape[2]
    zeros = jnp.zeros((1, width), BF16)
    own_vec = jnp.concatenate(
        [
            bias_q, zeros, bias_v, bias_out, norm1_gain, norm1_bias,
            bias_up.reshape(units // width, width),
            bias_down, norm2_gain, norm2_bias, zeros, zeros, zeros,
        ],
        axis=0,
    )
    own = [w_qkv[0], w_out[0], w_up[0], w_down[0], own_vec]
    own_counts = jnp.concatenate([skip_flags, head_counts, ffn_counts], axis=0)
    other_counts = swap(own_counts)
    other = [swap(part) for part in own]
    weights = []
    for mine, theirs in zip(own, other):
        weights += [mine, theirs]

    chosen = (jnp.arange(slots) == section).astype(jnp.int32)
    mine_at = jnp.sum(assignment * chosen)
    own_len = jnp.sum(jnp.where(jnp.arange(lengths.shape[0]) == mine_at, lengths, 0))
    scalars = []
    for layer in range(2):
        counts = jnp.where(section == layer, own_counts, other_counts)[:, 0].reshape(3, MICRO)
        skip, heads, unit_count = [
            jnp.sum(jnp.where(jnp.arange(MICRO) == section, counts[i], 0)) for i in range(3)
        ]
        live = (own_len + ROWS - 1) // ROWS
        on = 1 - skip
        scalars.append(
            jnp.stack(
                [
                    (section == layer).astype(jnp.int32), live * on, live, own_len, heads // 2,
                    unit_count, (unit_count + UNITS - 1) // UNITS * on, section, skip, section,
                ]
            ).astype(jnp.int32)
        )

    passed, *saved_one = layer_forward(False, scalars[0], inputs, weights)
    out_keep, out_send, *saved_two = layer_forward(True, scalars[1], passed, weights)

    res, *ffn, vecs = ffn_back(True, scalars[1], cotangent, weights, saved_two)
    g_mid, *attn, vecs = attention_back(
        False, scalars[1], res, cotangent, passed, weights, saved_two, [vecs]
    )
    res, *ffn, vecs = ffn_back(False, scalars[0], g_mid, weights, saved_one, [*ffn, vecs])
    in_keep, in_send, *attn, vecs = attention_back(
        True, scalars[0], res, g_mid, inputs, weights, saved_one, [*attn, vecs]
    )

    grads = (ffn[:2], ffn[2:], attn)
    weight_shapes = (
        [(1, units, width)], [(1, width, units)], [(1, width, width), (1, width, 3 * width)],
    )
    both_counts = [jnp.where(section == layer, own_counts, other_counts)[:, 0] for layer in range(2)]
    used = [jnp.sum(counts[:MICRO]) < MICRO for counts in both_counts]
    which = jnp.where(used[0] & used[1], 0, jnp.where(used[0], 1, 2))
    branches = [
        functools.partial(tail, layers, weight_shapes=weight_shapes) for layers in ((0, 1), (0,), (1,))
    ]
    grad_w_down, grad_w_up, grad_w_out, grad_w_qkv, vecs, out_half, grad_half = lax.switch(
        which, branches, grads, vecs, (out_keep, out_send), (in_keep, in_send)
    )
    grad_bias_up = vecs[8 : 8 + units // width].reshape(1, units)
    return (
        out_half, grad_half, grad_w_qkv, vecs[16:17], vecs[17:18], grad_w_out, vecs[18:19],
        vecs[0:1], vecs[1:2], grad_w_up, grad_bias_up, grad_w_down, vecs[4:5], vecs[2:3], vecs[3:4],
    )


def solution(mesh):
    three, two = P("section", None, None), P("section", None)
    return jax.shard_map(
        on_device,
        mesh=mesh,
        in_specs=(
            P("dp", None, None), P("dp", None, None), P(), P("dp"),
            P(None, "section"), P(None, "section"), P(None, "section"),
            three, two, two, three, two, two, two, three, two, three, two, two, two,
        ),
        out_specs=(
            P("dp", None, "section"), P("dp", None, "section"),
            three, two, two, three, two, two, two, three, two, three, two, two, two,
        ),
        check_vma=False,
    )
```

```python
import functools

import jax
import jax.numpy as jnp
from jax import lax
from jax.experimental import pallas as pl
from jax.experimental.pallas import tpu as pltpu
from jax.sharding import PartitionSpec as P

HEADS = 12
MICRO = 2
NORM_EPS = 1e-05
NEG_FILL = -1e30
F32 = jnp.float32
BF16 = jnp.bfloat16

ROWS = 256
UNITS = 512
LEAST = 1920 // UNITS
SAFE = 40.0
VMEM_BYTES = 64 * 1024 * 1024

OWN, BLOCKS, LIVE, LENGTH, PAIRS, COUNT, CHUNKS, SLOT, SKIP, SECTION = range(10)
V_BQ, V_ZERO, V_BV, V_BO, V_G1, V_B1, V_BU, V_BD, V_G2, V_B2 = 0, 1, 2, 3, 4, 5, 6, 10, 11, 12


def dot(left, right):
    return lax.dot_general(left, right, (((1,), (0,)), ((), ())), preferred_element_type=F32)


def dot_nt(left, right):
    return lax.dot_general(left, right, (((1,), (1,)), ((), ())), preferred_element_type=F32)


def dot_tn(left, right):
    return lax.dot_general(left, right, (((0,), (0,)), ((), ())), preferred_element_type=F32)


def rows_at(block):
    if isinstance(block, int):
        return pl.ds(block * ROWS, ROWS)
    return pl.ds(pl.multiple_of(block * ROWS, ROWS), ROWS)


def cols_at(start, size):
    if isinstance(start, int):
        return pl.ds(start, size)
    return pl.ds(pl.multiple_of(start, 128), size)


def facts(layer, own_counts, other_counts, assigned, lengths):
    section = lax.axis_index("section")
    own = section == layer

    def count(row):
        at = row * MICRO + section
        return jnp.where(own, own_counts[at], other_counts[at])

    skip, heads, units = count(0), count(1), count(2)
    length = lengths[assigned[section]]
    live = (length + ROWS - 1) // ROWS
    blocks = jnp.where(skip == 1, 0, live)
    chunks = jnp.where(skip == 1, 0, (units + UNITS - 1) // UNITS)
    return [own.astype(jnp.int32), blocks, live, length, heads // 2, units, chunks, section, skip, section]


def by_blocks(count, most, body):
    for blocks in range(2, most + 1, 2):
        pl.when((count == blocks) | (count == blocks - 1))(functools.partial(body, blocks))


def clear_odd(count, *refs):
    @pl.when(count % 2 == 1)
    def _():
        for ref in refs:
            ref[rows_at(count), :] = jnp.zeros((ROWS, ref.shape[1]), ref.dtype)


def by_chunks(count, most, body):
    body(0, LEAST + 1)
    pl.when(count > LEAST + 1)(functools.partial(body, LEAST + 1, most))


def fetch_start(s, dst, own_ref, other_ref, sem):
    @pl.when(s[OWN] == 1)
    def _():
        pltpu.make_async_copy(own_ref, dst, sem).start()

    @pl.when(s[OWN] == 0)
    def _():
        pltpu.make_async_copy(other_ref, dst, sem).start()


def live_column(s, block):
    frame = lax.broadcasted_iota(jnp.int32, (ROWS, 1), 0) + block * ROWS
    return frame < s[LENGTH]


def gelu_parts(values):
    under = 1.0 + 0.2316419 * jnp.abs(values)
    t = pl.reciprocal(under, approx=True)
    t = t * (2.0 - under * t)
    poly = t * (
        0.319381530 + t * (-0.356563782 + t * (1.781477937 + t * (-1.821255978 + t * 1.330274429)))
    )
    bell = jnp.exp2(values * values * -0.7213475204444817) * 0.3989422804014327
    tail = poly * bell
    below = jnp.where(values >= 0, 1.0 - tail, tail)
    return values * below, below + values * bell


def spread_heads(width):
    head = lax.broadcasted_iota(jnp.int32, (128, width), 1) // 64
    return (head == lax.broadcasted_iota(jnp.int32, (128, width), 0)).astype(BF16)


def norm_parts(values):
    center = jnp.mean(values, axis=-1, keepdims=True)
    shifted = values - center
    spread = jnp.mean(shifted * shifted, axis=-1, keepdims=True)
    inverse = lax.rsqrt(spread + NORM_EPS)
    return shifted * inverse, inverse


def vec_row(vec_ref, row):
    return vec_ref[row : row + 1, :].astype(F32)


def forward_kernel(
    last,
    phase,
    own_counts, other_counts, assigned, lengths,
    x_hbm,
    wq0, wq1, wo0, wo1, wu0, wu1, wd0, wd1, v0, v1,
    *rest,
):
    s = facts(1 if last else 0, own_counts, other_counts, assigned, lengths)
    attends, finishes = phase != "finish", phase != "attend"
    if not attends:
        ctx_in, stat_in = rest[:2]
        rest = rest[2:]
    if finishes and last:
        keep_hbm, send_hbm = rest[:2]
        rest = rest[2:]
    elif finishes:
        pass_hbm = rest[0]
        rest = rest[1:]
    if attends:
        proj_hbm, ctx_hbm, lse_hbm = rest[:3]
        rest = rest[3:]
    if finishes:
        stat_hbm, gated_hbm, slope_hbm, x1_hbm, x2_hbm = rest[:5]
        rest = rest[5:]
    (
        h, wq, wo, wu, wd, vec, proj, ctx, stat, gated, slope, x1, x2, acc, normed_b, bias_up, largest, out_a, out_b,
        in_sem, w_sem, out_sem,
    ) = rest
    most = h.shape[0] // ROWS
    width = h.shape[1]
    pairs_all = width // 128
    blocks = s[BLOCKS]
    live = s[LIVE]
    lane = lax.broadcasted_iota(jnp.int32, (1, 128), 1)
    low = lane < 64

    def source(block):
        if last:
            return x_hbm.at[rows_at(block)]
        return x_hbm.at[s[SLOT], rows_at(block)]

    def h_copy(block):
        return pltpu.make_async_copy(source(block), h.at[rows_at(block)], in_sem.at[block])

    for block in range(most):
        pl.when(block < live)(lambda block=block: h_copy(block).start())

    @pl.when(blocks > 0)
    def _():
        fetch_start(s, vec, v0, v1, w_sem.at[0])
        if attends:
            fetch_start(s, wq, wq0, wq1, w_sem.at[1])
        if finishes:
            fetch_start(s, wo, wo0, wo1, w_sem.at[2])
            fetch_start(s, wu, wu0, wu1, w_sem.at[3])
            fetch_start(s, wd, wd0, wd1, w_sem.at[4])

    def reload(what, block):
        target, source = ((ctx, ctx_in), (stat, stat_in))[what]
        return pltpu.make_async_copy(
            source.at[rows_at(block)], target.at[rows_at(block)], out_sem.at[what, block]
        )

    if not attends:
        for block in range(most):
            @pl.when(block < blocks)
            def _(block=block):
                reload(0, block).start()
                reload(1, block).start()

    for block in range(most):
        pl.when(block < live)(lambda block=block: h_copy(block).wait())

    def save(what, source_ref, target_ref, block):
        return pltpu.make_async_copy(
            source_ref.at[rows_at(block)], target_ref.at[rows_at(block)], out_sem.at[what, block]
        )

    def emit(block, value):
        if last:
            half = width // 2
            first = s[SECTION] == 0
            out_a[rows_at(block), :] = jnp.where(first, value[:, :half], value[:, half:])
            out_b[rows_at(block), :] = jnp.where(first, value[:, half:], value[:, :half]).astype(BF16)
            save(7, out_a, keep_hbm, block).start()
            save(8, out_b, send_hbm.at[0], block).start()
        else:
            out_b[rows_at(block), :] = value.astype(BF16)
            save(7, out_b, pass_hbm, block).start()

    def attention():
        pltpu.make_async_copy(wq0, wq, w_sem.at[1]).wait()

        spread = spread_heads(width)
        largest[...] = jnp.zeros(largest.shape, F32)

        def project(block, carry):
            rows = rows_at(block)
            for part, row in ((0, V_BQ), (1, V_ZERO), (2, V_BV)):
                cols = slice(part * width, (part + 1) * width)
                proj[rows, cols] = (dot(h[rows, :], wq[:, cols]) + vec_row(vec, row)).astype(BF16)
            save(0, proj, proj_hbm, block).start()
            for part in range(2):
                value = proj[rows, part * width : (part + 1) * width].astype(F32)
                squares = dot_nt(spread, (value * value).astype(BF16))
                largest[part] = jnp.maximum(largest[part], squares)
            stat[rows, :] = jnp.zeros((ROWS, 128), F32)
            return carry

        lax.fori_loop(0, blocks, project, 0)

        clear_odd(blocks, proj)
        for pair in range(pairs_all):
            @pl.when(pair >= s[PAIRS])
            def _(pair=pair):
                ctx[:, pair * 128 : (pair + 1) * 128] = jnp.zeros((h.shape[0], 128), BF16)

        bound = jnp.max(largest[0]) * jnp.max(largest[1]) * 1.02
        safe = bound <= (SAFE * 8.0) ** 2

        def attend_safe(count):
            key_at = lax.broadcasted_iota(jnp.int32, (1, ROWS), 1)
            fills = [
                jnp.where(key_at + part * ROWS < s[LENGTH], 0.0, NEG_FILL) for part in range(count)
            ]

            span = count * ROWS

            def one(pair, carry):
                cols = cols_at(pair * 128, 128)
                q = proj[0:span, cols] * jnp.asarray(0.125, BF16)
                zero = jnp.zeros_like(q)
                ones = jnp.ones((ROWS, 128), BF16)
                q_own = [jnp.where(own, q, zero) for own in (low, ~low)]
                found = [None, None]
                for part in range(count):
                    keys = slice(part * ROWS, (part + 1) * ROWS)
                    k = proj[keys, cols_at(width + pair * 128, 128)]
                    v = proj[keys, cols_at(2 * width + pair * 128, 128)]
                    for head, own in enumerate((low, ~low)):
                        scores = dot_nt(q_own[head], k)
                        if part >= count - 2:
                            scores = scores + fills[part]
                        exps = jnp.exp(scores).astype(BF16)
                        more = dot(exps, jnp.where(own, v, ones))
                        found[head] = more if part == 0 else found[head] + more
                above = jnp.where(low, found[0], found[1])
                total = pltpu.roll(jnp.where(low, found[1], found[0]), 64, 1)
                ctx[0:span, cols] = (above / total).astype(BF16)
                logs = jnp.log(total)
                kept = stat[0:span, :]
                kept = jnp.where(lane == 2 * pair, logs[:, 0:1], kept)
                kept = jnp.where(lane == 2 * pair + 1, logs[:, 64:65], kept)
                stat[0:span, :] = kept
                return carry

            lax.fori_loop(0, s[PAIRS], one, 0)

        def attend():
            span = most * ROWS
            key_live = lax.broadcasted_iota(jnp.int32, (1, span), 1) < s[LENGTH]

            def clear_rows(block, carry):
                proj[rows_at(block), width:] = jnp.zeros((ROWS, 2 * width), BF16)
                return carry

            lax.fori_loop(blocks, most, clear_rows, 0)

            def one(step, carry):
                pair, block = step // blocks, step % blocks
                rows = rows_at(block)
                cols = cols_at(pair * 128, 128)
                q = proj[rows, cols] * jnp.asarray(0.125, BF16)
                k = proj[:, cols_at(width + pair * 128, 128)]
                v = proj[:, cols_at(2 * width + pair * 128, 128)]
                zero = jnp.zeros_like(q)
                ones = jnp.ones_like(v)
                found, peaks = [], []
                for own in (low, ~low):
                    scores = jnp.where(key_live, dot_nt(jnp.where(own, q, zero), k), NEG_FILL)
                    peak = jnp.max(scores, axis=-1, keepdims=True)
                    exps = jnp.exp(scores - peak).astype(BF16)
                    found.append(dot(exps, jnp.where(own, v, ones)))
                    peaks.append(peak)
                above = jnp.where(low, found[0], found[1])
                total = pltpu.roll(jnp.where(low, found[1], found[0]), 64, 1)
                ctx[rows, cols] = (above / total).astype(BF16)
                logs = jnp.where(low, peaks[0], peaks[1]) + jnp.log(total)
                kept = stat[rows, :]
                kept = jnp.where(lane == 2 * pair, logs[:, 0:1], kept)
                kept = jnp.where(lane == 2 * pair + 1, logs[:, 64:65], kept)
                stat[rows, :] = kept
                return carry

            lax.fori_loop(0, s[PAIRS] * blocks, one, 0)

        by_blocks(jnp.where(safe, blocks, 0), most, attend_safe)
        pl.when(jnp.logical_not(safe))(attend)

    def feed_forward():
        for piece in range(wu.shape[1] // width):
            bias_up[0:1, piece * width : (piece + 1) * width] = vec_row(vec, V_BU + piece)
        pltpu.make_async_copy(wo0, wo, w_sem.at[2]).wait()
        pltpu.make_async_copy(wu0, wu, w_sem.at[3]).wait()
        pltpu.make_async_copy(wd0, wd, w_sem.at[4]).wait()

        def finish(block, carry):
            rows = rows_at(block)
            if attends:
                save(1, ctx, ctx_hbm, block).start()
            else:
                reload(0, block).wait()
                reload(1, block).wait()
            res = h[rows, :].astype(F32) + dot(ctx[rows, :], wo[...]) + vec_row(vec, V_BO)
            hat, inverse_one = norm_parts(res)
            x1[rows, :] = hat.astype(BF16)
            save(5, x1, x1_hbm, block).start()
            normed = hat * vec_row(vec, V_G1) + vec_row(vec, V_B1)
            normed_b[...] = normed.astype(BF16)
            acc[...] = normed + vec_row(vec, V_BD)

            def units(start, stop):
                def lift(c):
                    cols = slice(c * UNITS, (c + 1) * UNITS)
                    return dot(normed_b[...], wu[:, cols]) + bias_up[0:1, cols]

                more = None
                later = lift(start)
                for c in range(start, stop):
                    cols = slice(c * UNITS, (c + 1) * UNITS)
                    lifted = later
                    if c + 1 < stop:
                        later = lift(c + 1)
                    value, grad = gelu_parts(lifted)
                    if c >= LEAST:
                        unit = lax.broadcasted_iota(jnp.int32, (1, UNITS), 1) + c * UNITS
                        value = jnp.where(unit < s[COUNT], value, 0.0)
                        grad = jnp.where(unit < s[COUNT], grad, 0.0)
                    value_b = value.astype(BF16)
                    gated[rows, cols] = value_b
                    slope[rows, cols] = grad.astype(BF16)
                    part = dot(value_b, wd[cols, :])
                    more = part if more is None else more + part
                acc[...] += more

            units(0, wu.shape[1] // UNITS)
            save(3, gated, gated_hbm, block).start()
            save(4, slope, slope_hbm, block).start()
            hat_two, inverse_two = norm_parts(acc[...])
            x2[rows, :] = hat_two.astype(BF16)
            save(6, x2, x2_hbm, block).start()
            kept = stat[rows, :]
            kept = jnp.where(lane == HEADS, inverse_one, kept)
            stat[rows, :] = jnp.where(lane == HEADS + 1, inverse_two, kept)
            save(2, stat, stat_hbm, block).start()
            result = hat_two * vec_row(vec, V_G2) + vec_row(vec, V_B2)
            emit(block, jnp.where(live_column(s, block), result, 0.0))
            return carry

        lax.fori_loop(0, blocks, finish, 0)

    @pl.when(blocks > 0)
    def _():
        pltpu.make_async_copy(v0, vec, w_sem.at[0]).wait()
        if attends:
            attention()
        if finishes:
            feed_forward()

    if not finishes:
        def keep(block, carry):
            save(1, ctx, ctx_hbm, block).start()
            save(2, stat, lse_hbm, block).start()
            return carry

        lax.fori_loop(0, blocks, keep, 0)
        for block in range(most):
            @pl.when(block < blocks)
            def _(block=block):
                save(0, proj, proj_hbm, block).wait()
                save(1, ctx, ctx_hbm, block).wait()
                save(2, stat, lse_hbm, block).wait()
        return

    @pl.when(s[SKIP] == 1)
    def _():
        def carry_on(block, carry):
            value = h[rows_at(block), :].astype(F32)
            emit(block, jnp.where(live_column(s, block), value, 0.0) if last else value)
            return carry

        lax.fori_loop(0, live, carry_on, 0)

    if last:
        def clear(block, carry):
            emit(block, jnp.zeros((ROWS, width), F32))
            return carry

        lax.fori_loop(live, most, clear, 0)

    for block in range(most):
        @pl.when(block < blocks)
        def _(block=block):
            if attends:
                save(0, proj, proj_hbm, block).wait()
                save(1, ctx, ctx_hbm, block).wait()
            save(2, stat, stat_hbm, block).wait()
            save(3, gated, gated_hbm, block).wait()
            save(4, slope, slope_hbm, block).wait()
            save(5, x1, x1_hbm, block).wait()
            save(6, x2, x2_hbm, block).wait()

        if last:
            save(7, out_a, keep_hbm, block).wait()
            save(8, out_b, send_hbm.at[0], block).wait()
        else:
            pl.when(block < live)(lambda block=block: save(7, out_b, pass_hbm, block).wait())


HBM = pl.BlockSpec(memory_space=pltpu.HBM)
SMEM = pl.BlockSpec(memory_space=pltpu.SMEM)


def layer_forward(last, phase, scalars, x, weights, attended=()):
    length, width = x.shape[-2:]
    units = weights[4].shape[1]
    blocks = length // ROWS
    shape = jax.ShapeDtypeStruct
    attends, finishes = phase != "finish", phase != "attend"
    outs = []
    if finishes and last:
        outs += [shape((length, width // 2), F32), shape((2, length, width // 2), BF16)]
    elif finishes:
        outs += [shape((length, width), BF16)]
    if attends:
        outs += [
            shape((length, 3 * width), BF16),
            shape((length, width), BF16),
            shape((length, 128), F32),
        ]
    if finishes:
        outs += [
            shape((length, 128), F32),
            shape((length, units), BF16),
            shape((length, units), BF16),
            shape((length, width), BF16),
            shape((length, width), BF16),
        ]

    def held(used, size, dtype=BF16):
        return pltpu.VMEM(size if used else (16, 128), dtype)

    return pl.pallas_call(
        functools.partial(forward_kernel, last, phase),
        out_shape=outs,
        in_specs=[SMEM] * 4 + [HBM] * (11 + len(attended)),
        out_specs=[HBM] * len(outs),
        scratch_shapes=[
            pltpu.VMEM((length, width), BF16),
            held(attends, (width, 3 * width)),
            held(finishes, (width, width)),
            held(True, (width, units)),
            held(finishes, (units, width)),
            pltpu.VMEM(weights[8].shape, BF16),
            held(attends, (length, 3 * width)),
            pltpu.VMEM((length, width), BF16),
            pltpu.VMEM((length, 128), F32),
            held(finishes, (length, units)),
            held(finishes, (length, units)),
            held(finishes, (length, width)),
            held(finishes, (length, width)),
            held(finishes, (ROWS, width), F32),
            held(finishes, (ROWS, width)),
            pltpu.VMEM((8, units), F32),
            pltpu.VMEM((2, 128, ROWS), F32),
            held(finishes and last, (length, width // 2), F32),
            held(finishes, (length, width // 2 if last else width)),
            pltpu.SemaphoreType.DMA((blocks,)),
            pltpu.SemaphoreType.DMA((5,)),
            pltpu.SemaphoreType.DMA((9, blocks)),
        ],
        compiler_params=pltpu.CompilerParams(vmem_limit_bytes=VMEM_BYTES),
        cost_estimate=pl.CostEstimate(
            flops=60_000_000_000 if phase == "attend" else 10_000_000_000,
            bytes_accessed=0,
            transcendentals=0,
        ),
        name="layer_forward_" + phase,
    )(*scalars, x, *weights, *attended)


def ffn_back_kernel(
    first_pass,
    own_counts, other_counts, assigned, lengths,
    g_hbm,
    wu0, wu1, wd0, wd1, v0, v1,
    stat_hbm, gated_hbm, slope_hbm, x1_hbm, x2_hbm,
    *rest,
):
    if not first_pass:
        rest = rest[4:]
    (
    res_hbm, gd_keep, gd_send, gu_keep, gu_send, vec_hbm,
    g_out, wu, wd, vec, stat, gated, slope, x1, x2, res, down, normed, gd, gu, acc, sums, sums_up,
    in_sem, w_sem, out_sem, gd_sem, gu_sem,
    ) = rest
    layer = 1 if first_pass else 0
    s = facts(layer, own_counts, other_counts, assigned, lengths)
    most = g_out.shape[0] // ROWS
    width = g_out.shape[1]
    units = wu.shape[1]
    chunks = units // UNITS
    blocks = s[BLOCKS]

    def load(what, block):
        target, source = (
            (g_out, g_hbm.at[s[SLOT]] if first_pass else g_hbm),
            (stat, stat_hbm), (gated, gated_hbm), (slope, slope_hbm), (x1, x1_hbm), (x2, x2_hbm),
        )[what]
        return pltpu.make_async_copy(
            source.at[rows_at(block)], target.at[rows_at(block)], in_sem.at[what, block]
        )

    @pl.when(blocks > 0)
    def _():
        fetch_start(s, vec, v0, v1, w_sem.at[0])

    for block in range(most):
        @pl.when(block < blocks)
        def _(block=block):
            for what in (0, 1, 5, 3, 4):
                load(what, block).start()

        if block == 0:
            @pl.when(blocks > 0)
            def _():
                fetch_start(s, wd, wd0, wd1, w_sem.at[2])
                fetch_start(s, wu, wu0, wu1, w_sem.at[1])

    for block in range(most):
        pl.when(block < blocks)(lambda block=block: load(2, block).start())

    sums[...] = jnp.zeros(sums.shape, F32)
    sums_up[...] = jnp.zeros(sums_up.shape, F32)

    @pl.when(blocks > 0)
    def _():
        pltpu.make_async_copy(v0, vec, w_sem.at[0]).wait()

        def step(block, carry):
            rows = rows_at(block)
            for what in (0, 1, 5):
                load(what, block).wait()
            inverse_one = stat[rows, HEADS : HEADS + 1]
            inverse_two = stat[rows, HEADS + 1 : HEADS + 2]
            gn = jnp.where(live_column(s, block), g_out[rows, :].astype(F32), 0.0)
            hat = x2[rows, :].astype(F32)
            sums[2:3, :] += jnp.sum(gn * hat, axis=0, keepdims=True)
            sums[3:4, :] += jnp.sum(gn, axis=0, keepdims=True)
            gh = gn * vec_row(vec, V_G2)
            mean_one = jnp.mean(gh, axis=-1, keepdims=True)
            mean_two = jnp.mean(gh * hat, axis=-1, keepdims=True)
            g_res = (gh - mean_one - hat * mean_two) * inverse_two
            down_b = g_res.astype(BF16)
            sums[4:5, :] += jnp.sum(down_b.astype(F32), axis=0, keepdims=True)
            down[rows, :] = down_b
            acc[...] = g_res

            @pl.when(block == 0)
            def _():
                pltpu.make_async_copy(wd0, wd, w_sem.at[2]).wait()
                pltpu.make_async_copy(wu0, wu, w_sem.at[1]).wait()

            load(3, block).wait()
            load(4, block).wait()

            def units(start, stop):
                def gate(c):
                    return dot_nt(down[rows, :], wd[c * UNITS : (c + 1) * UNITS, :])

                more = None
                later = gate(start)
                for c in range(start, stop):
                    cols = slice(c * UNITS, (c + 1) * UNITS)
                    g_gated = later
                    if c + 1 < stop:
                        later = gate(c + 1)
                    lift = (g_gated * slope[rows, cols].astype(F32)).astype(BF16)
                    slope[rows, cols] = lift
                    sums_up[0:1, cols] += jnp.sum(lift.astype(F32), axis=0, keepdims=True)
                    part = dot_nt(lift, wu[:, cols])
                    more = part if more is None else more + part
                acc[...] += more

            by_chunks(s[CHUNKS], chunks, units)
            g_normed = acc[...]
            hat = x1[rows, :].astype(F32)
            normed[rows, :] = (hat * vec_row(vec, V_G1) + vec_row(vec, V_B1)).astype(BF16)
            sums[0:1, :] += jnp.sum(g_normed * hat, axis=0, keepdims=True)
            sums[1:2, :] += jnp.sum(g_normed, axis=0, keepdims=True)
            gh = g_normed * vec_row(vec, V_G1)
            mean_one = jnp.mean(gh, axis=-1, keepdims=True)
            mean_two = jnp.mean(gh * hat, axis=-1, keepdims=True)
            res[rows, :] = (gh - mean_one - hat * mean_two) * inverse_one
            pltpu.make_async_copy(res.at[rows], res_hbm.at[rows], out_sem.at[block]).start()
            return carry

        lax.fori_loop(0, blocks, step, 0)
        for block in range(most):
            pl.when(block < blocks)(lambda block=block: load(2, block).wait())


    half_rows = units // 2
    half_cols = units // 2
    per_half = chunks // 2

    def chunk_copies(c):
        half, inside = c // per_half, c % per_half
        down_part = gd.at[cols_at(c * UNITS, UNITS), :]
        up_part = gu.at[:, cols_at(c * UNITS, UNITS)]
        place = cols_at(inside * UNITS, UNITS)
        return half, down_part, up_part, place

    def send_chunk(c):
        half, down_part, up_part, place = chunk_copies(c)

        @pl.when(half == s[SECTION])
        def _():
            pltpu.make_async_copy(down_part, gd_keep.at[layer, place, :], gd_sem.at[c]).start()
            pltpu.make_async_copy(up_part, gu_keep.at[layer, :, place], gu_sem.at[c]).start()

        @pl.when(half != s[SECTION])
        def _():
            pltpu.make_async_copy(down_part, gd_send.at[layer, place, :], gd_sem.at[c]).start()
            pltpu.make_async_copy(up_part, gu_send.at[layer, :, place], gu_sem.at[c]).start()

    def weigh(count):
        span = count * ROWS

        def one(c, carry):
            cols = cols_at(c * UNITS, UNITS)
            gd[cols, :] = dot_tn(gated[0:span, cols], down[0:span, :]).astype(BF16)
            gu[:, cols] = dot_tn(normed[0:span, :], slope[0:span, cols]).astype(BF16)
            send_chunk(c)
            return carry

        lax.fori_loop(0, s[CHUNKS], one, 0)

    clear_odd(blocks, gated, down, normed, slope)
    by_blocks(blocks, most, weigh)

    def nothing(c, carry):
        cols = cols_at(c * UNITS, UNITS)
        gd[cols, :] = jnp.zeros((UNITS, width), BF16)
        gu[:, cols] = jnp.zeros((width, UNITS), BF16)
        send_chunk(c)
        return carry

    lax.fori_loop(s[CHUNKS], chunks, nothing, 0)

    for c in range(chunks):
        _, down_part, up_part, place = chunk_copies(c)
        pltpu.make_async_copy(down_part, gd_keep.at[layer, place, :], gd_sem.at[c]).wait()
        pltpu.make_async_copy(up_part, gu_keep.at[layer, :, place], gu_sem.at[c]).wait()
    for piece in range(units // width):
        sums[8 + piece : 9 + piece, :] = sums_up[0:1, piece * width : (piece + 1) * width]
    pltpu.sync_copy(sums, vec_hbm)
    for block in range(most):
        @pl.when(block < blocks)
        def _(block=block):
            rows = rows_at(block)
            pltpu.make_async_copy(res.at[rows], res_hbm.at[rows], out_sem.at[block]).wait()


def ffn_back(first_pass, scalars, g_out, weights, saved, grads=()):
    length, width = g_out.shape[-2:]
    units = weights[4].shape[1]
    blocks = length // ROWS
    chunks = units // UNITS
    shape = jax.ShapeDtypeStruct
    _, _, stat, gated, slope, x1, x2 = saved
    return pl.pallas_call(
        functools.partial(ffn_back_kernel, first_pass),
        out_shape=[
            shape((length, width), F32),
            shape((2, units // 2, width), BF16),
            shape((2, units // 2, width), BF16),
            shape((2, width, units // 2), BF16),
            shape((2, width, units // 2), BF16),
            shape((16, width), F32),
        ],
        in_specs=[SMEM] * 4 + [HBM] * (12 + len(grads)),
        out_specs=[HBM] * 6,
        input_output_aliases={16 + i: 1 + i for i in range(len(grads))},
        scratch_shapes=[
            pltpu.VMEM((length, width), BF16),
            pltpu.VMEM((width, units), BF16),
            pltpu.VMEM((units, width), BF16),
            pltpu.VMEM(weights[8].shape, BF16),
            pltpu.VMEM((length, 128), F32),
            pltpu.VMEM((length, units), BF16),
            pltpu.VMEM((length, units), BF16),
            pltpu.VMEM((length, width), BF16),
            pltpu.VMEM((length, width), BF16),
            pltpu.VMEM((length, width), F32),
            pltpu.VMEM((length, width), BF16),
            pltpu.VMEM((length, width), BF16),
            pltpu.VMEM((units, width), BF16),
            pltpu.VMEM((width, units), BF16),
            pltpu.VMEM((ROWS, width), F32),
            pltpu.VMEM((16, width), F32),
            pltpu.VMEM((8, units), F32),
            pltpu.SemaphoreType.DMA((6, blocks)),
            pltpu.SemaphoreType.DMA((3,)),
            pltpu.SemaphoreType.DMA((blocks,)),
            pltpu.SemaphoreType.DMA((chunks,)),
            pltpu.SemaphoreType.DMA((chunks,)),
        ],
        compiler_params=pltpu.CompilerParams(vmem_limit_bytes=VMEM_BYTES),
        name="ffn_back",
    )(*scalars, g_out, *weights[4:8], *weights[8:10], stat, gated, slope, x1, x2, *grads)


def attention_back_kernel(
    first_layer,
    own_counts, other_counts, assigned, lengths,
    res_hbm, g_hbm, x_hbm,
    wq0, wq1, wo0, wo1,
    proj_hbm, ctx_hbm, stat_hbm, ffn_sums_hbm,
    *rest,
):
    layer = 0 if first_layer else 1
    s = facts(layer, own_counts, other_counts, assigned, lengths)
    rest = rest[3 if first_layer else 0 :]
    if first_layer:
        in_keep, in_send = rest[:2]
        rest = rest[2:]
    else:
        in_hbm = rest[0]
        rest = rest[1:]
    (
        ga_keep, ga_send,
        res, g_in, h, wq, wo, proj, ctx, stat, attn, g_ctx, g_proj, rows_log, rows_delta,
        go, gq, out_a, out_b, sums, ffn_sums, extra,
        in_sem, w_sem, out_sem, go_sem, gq_sem, extra_sem,
    ) = rest
    most = res.shape[0] // ROWS
    width = res.shape[1]
    half = width // 2
    pairs_all = width // 128
    blocks = s[BLOCKS]
    live = s[LIVE]
    lane = lax.broadcasted_iota(jnp.int32, (1, 128), 1)
    low = lane < 64
    zero_pair = jnp.zeros((1, 128), BF16)

    def load(what, block):
        target, source = (
            (res, res_hbm), (ctx, ctx_hbm), (stat, stat_hbm), (proj, proj_hbm),
            (h, x_hbm.at[s[SLOT]] if first_layer else x_hbm),
        )[what]
        return pltpu.make_async_copy(
            source.at[rows_at(block)], target.at[rows_at(block)], in_sem.at[what, block]
        )

    def load_g(block):
        source = g_hbm if first_layer else g_hbm.at[s[SLOT]]
        return pltpu.make_async_copy(
            source.at[rows_at(block)], g_in.at[rows_at(block)], in_sem.at[0, block]
        )

    for what in (0, 1):
        for block in range(most):
            pl.when(block < blocks)(lambda what=what, block=block: load(what, block).start())

    @pl.when(blocks > 0)
    def _():
        fetch_start(s, wo, wo0, wo1, w_sem.at[0])

    for what in (2, 3, 4):
        for block in range(most):
            pl.when(block < blocks)(lambda what=what, block=block: load(what, block).start())

    @pl.when(blocks > 0)
    def _():
        fetch_start(s, wq, wq0, wq1, w_sem.at[1])

    sums[...] = jnp.zeros(sums.shape, F32)
    ffn_load = pltpu.make_async_copy(ffn_sums_hbm, ffn_sums, extra_sem.at[2])
    ffn_load.start()

    def out_copies(block, wait):
        rows = rows_at(block)
        if first_layer:
            copies = [
                pltpu.make_async_copy(out_a.at[rows], in_keep.at[rows], out_sem.at[0, block]),
                pltpu.make_async_copy(out_b.at[rows], in_send.at[1, rows], out_sem.at[1, block]),
            ]
        else:
            copies = [pltpu.make_async_copy(out_b.at[rows], in_hbm.at[rows], out_sem.at[0, block])]
        for copy in copies:
            copy.wait() if wait else copy.start()

    def emit(block, value):
        rows = rows_at(block)
        if first_layer:
            front = s[SECTION] == 0
            out_a[rows, :] = jnp.where(front, value[:, :half], value[:, half:])
            out_b[rows, :] = jnp.where(front, value[:, half:], value[:, :half]).astype(BF16)
        else:
            out_b[rows, :] = value.astype(BF16)
        out_copies(block, False)

    def go_copy(part, keep):
        target = (ga_keep if keep else ga_send).at[layer, 0:width, 0:half]
        return pltpu.make_async_copy(go.at[:, part * half : (part + 1) * half], target, go_sem.at[part])

    def gq_copy(part, keep):
        target = (ga_keep if keep else ga_send).at[layer, 0:width, half : 4 * half]
        cols = slice(part * 3 * half, (part + 1) * 3 * half)
        return pltpu.make_async_copy(gq.at[:, cols], target, gq_sem.at[part])

    def start_halves(make):
        for part in range(2):
            pl.when(s[SECTION] == part)(lambda part=part: make(part, True).start())
            pl.when(s[SECTION] != part)(lambda part=part: make(part, False).start())

    @pl.when(blocks > 0)
    def _():
        pltpu.make_async_copy(wo0, wo, w_sem.at[0]).wait()
        spread = spread_heads(width)

        def before(block, carry):
            rows = rows_at(block)
            load(0, block).wait()
            load(1, block).wait()
            attn_b = res[rows, :].astype(BF16)
            attn[rows, :] = attn_b
            sums[2:3, :] += jnp.sum(attn_b.astype(F32), axis=0, keepdims=True)
            g_context = dot_nt(attn_b, wo[...]).astype(BF16)
            g_ctx[rows, :] = g_context
            product = (g_context.astype(F32) * ctx[rows, :].astype(F32)).astype(BF16)
            rows_delta[:, rows] = dot_nt(spread, product)
            load(2, block).wait()
            rows_log[:, rows] = stat[rows, :].T
            load(3, block).wait()
            return carry

        lax.fori_loop(0, blocks, before, 0)
        clear_odd(blocks, proj, g_ctx, ctx, attn, h)

        @pl.when(blocks % 2 == 1)
        def _():
            rows_log[:, rows_at(blocks)] = jnp.zeros((128, ROWS), F32)
            rows_delta[:, rows_at(blocks)] = jnp.zeros((128, ROWS), F32)

        def weigh_out(count):
            span = count * ROWS
            go[...] = dot_tn(ctx[0:span, :], attn[0:span, :]).astype(BF16)

        by_blocks(blocks, most, weigh_out)
        start_halves(go_copy)

        for pair in range(pairs_all):
            @pl.when(pair >= s[PAIRS])
            def _(pair=pair):
                for part in range(3):
                    cols = slice(part * width + pair * 128, part * width + (pair + 1) * 128)
                    g_proj[:, cols] = jnp.zeros((g_proj.shape[0], 128), BF16)

        def attend_back(count):
            span = count * ROWS

            def one_pair(pair, carry):
                cols = cols_at(pair * 128, 128)
                total_q = None
                for block in range(count):
                    rows = rows_at(block)
                    q = proj[0:span, cols]
                    d_ctx = g_ctx[0:span, cols]
                    k = proj[rows, cols_at(width + pair * 128, 128)] * jnp.asarray(0.125, BF16)
                    v = proj[rows, cols_at(2 * width + pair * 128, 128)]
                    fill = jnp.where(live_column(s, block), 0.0, NEG_FILL) if block >= count - 2 else 0.0
                    found_k, found_v, found_q = [], [], []
                    for head, own in ((0, low), (1, ~low)):
                        k_own = jnp.where(own, k, zero_pair)
                        v_own = jnp.where(own, v, zero_pair)
                        log_row = rows_log[pl.ds(2 * pair + head, 1), 0:span]
                        delta_row = rows_delta[pl.ds(2 * pair + head, 1), 0:span]
                        probs = jnp.exp(dot_nt(k_own, q) + fill - log_row)
                        g_probs = dot_nt(v_own, d_ctx)
                        g_scores = (probs * (g_probs - delta_row)).astype(BF16)
                        found_v.append(dot(probs.astype(BF16), d_ctx))
                        found_k.append(dot(g_scores, q))
                        found_q.append(dot_tn(g_scores, k_own))
                    more_q = found_q[0] + found_q[1]
                    total_q = more_q if block == 0 else total_q + more_q
                    g_k = jnp.where(low, found_k[0], found_k[1]) * 0.125
                    g_v = jnp.where(low, found_v[0], found_v[1])
                    g_proj[rows, cols_at(width + pair * 128, 128)] = g_k.astype(BF16)
                    g_proj[rows, cols_at(2 * width + pair * 128, 128)] = g_v.astype(BF16)
                g_proj[0:span, cols] = total_q.astype(BF16)
                return carry

            lax.fori_loop(0, s[PAIRS], one_pair, 0)

        by_blocks(blocks, most, attend_back)

        for block in range(most):
            pl.when(block < blocks)(lambda block=block: load(4, block).wait())
        pltpu.make_async_copy(wq0, wq, w_sem.at[1]).wait()

        def weigh_in(count):
            span = count * ROWS

            def one(part, carry):
                cols = cols_at(part * width, width)
                gq[:, cols] = dot_tn(h[0:span, :], g_proj[0:span, cols]).astype(BF16)
                return carry

            lax.fori_loop(0, 3, one, 0)

        by_blocks(blocks, most, weigh_in)
        start_halves(gq_copy)

        def after(block, carry):
            rows = rows_at(block)
            grad = g_proj[rows, :]
            sums[0:1, :] += jnp.sum(grad[:, :width].astype(F32), axis=0, keepdims=True)
            sums[1:2, :] += jnp.sum(grad[:, 2 * width :].astype(F32), axis=0, keepdims=True)
            emit(block, res[rows, :] + dot_nt(grad, wq[...]))
            return carry

        lax.fori_loop(0, blocks, after, 0)

    @pl.when(s[SKIP] == 1)
    def _():
        go[...] = jnp.zeros(go.shape, BF16)
        gq[...] = jnp.zeros(gq.shape, BF16)
        start_halves(go_copy)
        start_halves(gq_copy)
        for block in range(most):
            pl.when(block < live)(lambda block=block: load_g(block).start())
        for block in range(most):
            pl.when(block < live)(lambda block=block: load_g(block).wait())

        def carry_on(block, carry):
            value = g_in[rows_at(block), :].astype(F32)
            emit(block, jnp.where(live_column(s, block), value, 0.0))
            return carry

        lax.fori_loop(0, live, carry_on, 0)

    if first_layer:
        def clear(block, carry):
            emit(block, jnp.zeros((ROWS, width), F32))
            return carry

        lax.fori_loop(live, most, clear, 0)

    ffn_load.wait()
    own_sums = jnp.concatenate([sums[...], jnp.zeros(sums.shape, F32)], axis=0)
    extra[...] = jnp.concatenate([ffn_sums[...], own_sums], axis=1).astype(BF16)
    extra_copies = [
        pltpu.make_async_copy(extra, target.at[layer, width : width + 16], extra_sem.at[at])
        for at, target in enumerate((ga_keep, ga_send))
    ]
    for copy in extra_copies:
        copy.start()
    for copy in extra_copies:
        copy.wait()
    for part in range(2):
        go_copy(part, True).wait()
        gq_copy(part, True).wait()
    for block in range(most):
        if first_layer:
            out_copies(block, True)
        else:
            pl.when(block < live)(lambda block=block: out_copies(block, True))


def attention_back(first_layer, scalars, res, g_out, x, weights, saved, ffn_sums, grads=()):
    length, width = res.shape
    blocks = length // ROWS
    shape = jax.ShapeDtypeStruct
    proj, ctx, stat = saved[:3]
    outs = (
        [shape((length, width // 2), F32), shape((2, length, width // 2), BF16)]
        if first_layer
        else [shape((length, width), BF16)]
    )
    outs += [
        shape((2, width + 16, 2 * width), BF16),
        shape((2, width + 16, 2 * width), BF16),
    ]
    return pl.pallas_call(
        functools.partial(attention_back_kernel, first_layer),
        out_shape=outs,
        in_specs=[SMEM] * 4 + [HBM] * (11 + len(grads)),
        out_specs=[HBM] * len(outs),
        input_output_aliases={15 + i: len(outs) - len(grads) + i for i in range(len(grads))},
        scratch_shapes=[
            pltpu.VMEM((length, width), F32),
            pltpu.VMEM((length, width), BF16),
            pltpu.VMEM((length, width), BF16),
            pltpu.VMEM((width, 3 * width), BF16),
            pltpu.VMEM((width, width), BF16),
            pltpu.VMEM((length, 3 * width), BF16),
            pltpu.VMEM((length, width), BF16),
            pltpu.VMEM((length, 128), F32),
            pltpu.VMEM((length, width), BF16),
            pltpu.VMEM((length, width), BF16),
            pltpu.VMEM((length, 3 * width), BF16),
            pltpu.VMEM((128, length), F32),
            pltpu.VMEM((128, length), F32),
            pltpu.VMEM((width, width), BF16),
            pltpu.VMEM((width, 3 * width), BF16),
            pltpu.VMEM((length if first_layer else 8, width // 2), F32),
            pltpu.VMEM((length, width // 2 if first_layer else width), BF16),
            pltpu.VMEM((8, width), F32),
            pltpu.VMEM((16, width), F32),
            pltpu.VMEM((16, 2 * width), BF16),
            pltpu.SemaphoreType.DMA((5, blocks)),
            pltpu.SemaphoreType.DMA((2,)),
            pltpu.SemaphoreType.DMA((2, blocks)),
            pltpu.SemaphoreType.DMA((2,)),
            pltpu.SemaphoreType.DMA((2,)),
            pltpu.SemaphoreType.DMA((3,)),
        ],
        compiler_params=pltpu.CompilerParams(vmem_limit_bytes=VMEM_BYTES),
        name="attention_back",
    )(*scalars, res, g_out, x, *weights[0:4], proj, ctx, stat, ffn_sums, *grads)


def swap(part):
    return lax.ppermute(part, "section", [(0, 1), (1, 0)])


def across(part, bit):
    pairs = [(i, i ^ 1 << bit) for i in range(lax.axis_size("dp"))]
    return lax.ppermute(part, "dp", pairs)


FREE = pl.CostEstimate(flops=0, bytes_accessed=0, transcendentals=0)
SHORT = pl.CostEstimate(flops=4_000_000_000, bytes_accessed=0, transcendentals=0)
LONG = pl.CostEstimate(flops=20_000_000_000, bytes_accessed=0, transcendentals=0)


def my_bit(bit):
    return (lax.axis_index("dp") >> bit) & 1


def half_sum_kernel(bit, turn, extra, keep, got, before, out, own, new, in_sem, out_sem):
    layers, rows, _ = keep.shape
    half = (rows - extra) // 2
    at = 1 - my_bit(bit) if turn == 0 else my_bit(bit)
    spans = [(pl.ds(pl.multiple_of(at * half, 16), half), slice(0, half))]
    if extra:
        spans.append((slice(rows - extra, rows), slice(half, half + extra)))

    def loads(layer):
        copies = []
        for i, (source, target) in enumerate(spans):
            for j, (ref, held) in enumerate(((keep, own), (got, new))):
                copies.append(
                    pltpu.make_async_copy(
                        ref.at[layer, source], held.at[layer, target], in_sem.at[layer, i, j]
                    )
                )
        return copies

    def store(layer):
        return pltpu.make_async_copy(own.at[layer], out.at[layer], out_sem.at[layer])

    for layer in range(layers):
        for copy in loads(layer):
            copy.start()
    for layer in range(layers):
        for copy in loads(layer):
            copy.wait()

        def add_rows(i, carry, layer=layer):
            place = pl.ds(pl.multiple_of(i * 16, 16), 16)
            total = own[layer, place, :].astype(F32) + new[layer, place, :].astype(F32)
            own[layer, place, :] = total.astype(BF16)
            return carry

        lax.fori_loop(0, (half + extra) // 16, add_rows, 0, unroll=3)
        store(layer).start()
    for layer in range(layers):
        store(layer).wait()


def half_sum(bit, turn, extra, keep, got, before):
    layers, rows, cols = keep.shape
    half = (rows - extra) // 2
    if half % 48:
        at = 1 - my_bit(bit) if turn == 0 else my_bit(bit)

        def parts(a):
            own = lax.dynamic_slice_in_dim(a, at * half, half, 1)
            return jnp.concatenate([own, a[:, rows - extra :]], axis=1).astype(F32)

        return (parts(keep) + parts(got)).astype(BF16)
    return pl.pallas_call(
        functools.partial(half_sum_kernel, bit, turn, extra),
        out_shape=jax.ShapeDtypeStruct((layers, half + extra, cols), BF16),
        in_specs=[HBM, HBM, HBM],
        out_specs=HBM,
        scratch_shapes=[
            pltpu.VMEM((layers, half + extra, cols), BF16),
            pltpu.VMEM((layers, half + extra, cols), BF16),
            pltpu.SemaphoreType.DMA((layers, 2, 2)),
            pltpu.SemaphoreType.DMA((layers,)),
        ],
        compiler_params=pltpu.CompilerParams(vmem_limit_bytes=VMEM_BYTES),
        cost_estimate=FREE if turn else SHORT,
        name="half_sum",
    )(keep, got, before)


def split_kernel(extra, one, two, before, own, send, *vec):
    layers, rows, _ = one.shape
    rows -= extra
    section = lax.axis_index("section")
    mine, theirs = (section, 1 - section) if layers == 2 else (0, 0)

    def total(at, where):
        return (one[pl.ds(at, 1), where].astype(F32) + two[pl.ds(at, 1), where].astype(F32)).astype(BF16)

    own[...] = total(mine, slice(0, rows))
    send[...] = total(theirs, slice(0, rows))
    if extra:
        vec[0][...] = total(mine, slice(rows, rows + extra))


def split(one, two, before, extra):
    layers, rows, cols = one.shape
    rows -= extra
    if rows % 16:
        total = (one.astype(F32) + two.astype(F32)).astype(BF16)
        own = send = total
        if layers == 2:
            section = lax.axis_index("section")
            own = lax.dynamic_slice_in_dim(total, section, 1)
            send = lax.dynamic_slice_in_dim(total, 1 - section, 1)
        return (own[:, :rows], send[:, :rows]) + ((own[:, rows:],) if extra else ())
    whole = pl.BlockSpec(memory_space=pltpu.VMEM)
    outs = [jax.ShapeDtypeStruct((1, rows, cols), BF16)] * 2
    if extra:
        outs.append(jax.ShapeDtypeStruct((1, extra, cols), BF16))
    return pl.pallas_call(
        functools.partial(split_kernel, extra),
        out_shape=outs,
        in_specs=[whole, whole, HBM],
        out_specs=[whole] * len(outs),
        cost_estimate=SHORT,
        name="split",
    )(one, two, before)


def join_kernel(bit, part, got, before, both, held, in_sem, out_sem):
    layers, rows, _ = part.shape
    mine = my_bit(bit)
    steps = [(at, layer) for at in range(2) for layer in range(layers)]

    def load(at, layer):
        source = (part, got)[at].at[layer]
        return pltpu.make_async_copy(source, held.at[at, layer], in_sem.at[at, layer])

    def store(at, layer):
        place = mine if at == 0 else 1 - mine
        target = both.at[layer, pl.ds(pl.multiple_of(place * rows, 16), rows)]
        return pltpu.make_async_copy(held.at[at, layer], target, out_sem.at[at, layer])

    for step in steps:
        load(*step).start()
    for step in steps:
        load(*step).wait()
        store(*step).start()
    for step in steps:
        store(*step).wait()


def join(bit, part, got, before):
    layers, rows, cols = part.shape
    if rows % 16:
        at = jnp.arange(2)[:, None, None]
        both = jnp.where(at == my_bit(bit), part[:, None], got[:, None])
        return both.reshape(layers, 2 * rows, cols)
    return pl.pallas_call(
        functools.partial(join_kernel, bit),
        out_shape=jax.ShapeDtypeStruct((layers, 2 * rows, cols), BF16),
        in_specs=[HBM, HBM, HBM],
        out_specs=HBM,
        scratch_shapes=[
            pltpu.VMEM((2, layers, rows, cols), BF16),
            pltpu.SemaphoreType.DMA((2, layers)),
            pltpu.SemaphoreType.DMA((2, layers)),
        ],
        compiler_params=pltpu.CompilerParams(vmem_limit_bytes=VMEM_BYTES),
        cost_estimate=SHORT,
        name="join",
    )(part, got, before)


class Stream:
    def __init__(self, layers, keep, send, order, extra):
        self.layers, self.keep, self.send, self.order, self.extra = layers, keep, send, order, extra

    def enter(self):
        self.got = swap(self.send)

    def send_half(self, turn, chain):
        bit = self.order[turn]
        self.old = (self.keep, self.got)
        send = half_sum(bit, 0, self.extra, *self.old, chain[-1])
        chain.append(send)
        self.got = across(send, bit)

    def keep_half(self, turn, chain):
        self.keep = half_sum(self.order[turn], 1, self.extra, *self.old, chain[-1])
        chain.append(self.keep)

    def exchange(self, chain):
        self.own, send, *self.vec = split(self.keep, self.got, chain[-1], self.extra)
        chain.append(send)
        if len(self.layers) == 1:
            live = self.layers[0]
            self.got = lax.ppermute(send, "section", [(1 - live, live)])
        else:
            self.got = swap(send)

    def gather(self, turn, chain):
        bits = len(self.order)
        bit = self.order[bits - 1 - turn]
        if turn == 0:
            place = jnp.arange(2)[:, None, None]
            self.part = jnp.where(place == lax.axis_index("section"), self.own, self.got)
        else:
            self.part = join(self.order[bits - turn], self.part, self.got, chain[-1])
        chain.append(self.part)
        if len(self.layers) == 1:
            devices = lax.axis_size("dp")
            first = self.layers[0] * devices
            pairs = [(first + i, first + (i ^ 1 << bit)) for i in range(devices)]
            self.got = lax.ppermute(self.part, ("section", "dp"), pairs)
        else:
            self.got = across(self.part, bit)


def place_kernel(kind, turn, layers, first_bit, part, *refs):
    outs_count = 2 if kind == "attn" else 1
    refs = refs[outs_count + 1 if turn else 1 :]
    outs = refs[:outs_count]
    held, wide, in_sem, out_sem = refs[outs_count:]
    rows, cols = held.shape[1:]
    side = my_bit(first_bit) if turn == 0 else 1 - my_bit(first_bit)
    live = True if len(layers) == 2 else lax.axis_index("section") == layers[0]

    def target(half, at):
        if kind == "rows":
            return outs[0].at[0, pl.ds(pl.multiple_of((2 * half + side) * rows, 8), rows), :]
        at_rows = pl.ds(pl.multiple_of(side * rows, 8), rows)
        width = cols if kind == "cols" else (cols // 4 if at == 0 else 3 * cols // 4)
        return outs[at].at[0, at_rows, half * width : (half + 1) * width]

    def out_copies(half, wait):
        pieces = [(0, slice(0, cols))]
        if kind == "attn":
            pieces = [(0, slice(0, cols // 4)), (1, slice(cols // 4, cols))]
        for at, where in pieces:
            copy = pltpu.make_async_copy(wide.at[half, :, where], target(half, at), out_sem.at[half, at])
            copy.wait() if wait else copy.start()

    def load(half):
        return pltpu.make_async_copy(part.at[half], held.at[half], in_sem.at[half])

    for half in range(2):
        load(half).start()
    for half in range(2):
        load(half).wait()

        def convert(i, carry, half=half):
            at = pl.ds(pl.multiple_of(i * 16, 16), 16)
            value = held[half, at, :].astype(F32)
            wide[half, at, :] = value if live is True else jnp.where(live, value, 0.0)
            return carry

        lax.fori_loop(0, rows // 16, convert, 0, unroll=2)
        out_copies(half, False)
    for half in range(2):
        out_copies(half, True)


def place(kind, turn, layers, first_bit, part, shapes, extra):
    rows, cols = part.shape[1:]
    return pl.pallas_call(
        functools.partial(place_kernel, kind, turn, layers, first_bit),
        out_shape=[jax.ShapeDtypeStruct(out, F32) for out in shapes],
        in_specs=[HBM] * (1 + len(extra)),
        out_specs=[HBM] * len(shapes),
        input_output_aliases={1 + i: i for i in range(len(shapes))} if turn else {},
        scratch_shapes=[
            pltpu.VMEM((2, rows, cols), BF16),
            pltpu.VMEM((2, rows, cols), F32),
            pltpu.SemaphoreType.DMA((2,)),
            pltpu.SemaphoreType.DMA((2, 2)),
        ],
        compiler_params=pltpu.CompilerParams(vmem_limit_bytes=VMEM_BYTES),
        cost_estimate=LONG,
        name="place_" + kind,
    )(part, *extra)


def slots_kernel(index, keep, got, before, out, own, new, wide, in_sem, out_sem):
    section = lax.axis_index("section")
    mine = pltpu.make_async_copy(keep, own, in_sem.at[0])
    theirs = pltpu.make_async_copy(got.at[index], new, in_sem.at[1])
    mine.start()
    theirs.start()
    mine.wait()
    store_mine = pltpu.make_async_copy(own, out.at[section], out_sem.at[0])
    store_mine.start()
    theirs.wait()

    def convert(i, carry):
        at = pl.ds(pl.multiple_of(i * 32, 32), 32)
        wide[at, :] = new[at, :].astype(F32)
        return carry

    lax.fori_loop(0, new.shape[0] // 32, convert, 0)
    store_theirs = pltpu.make_async_copy(wide, out.at[1 - section], out_sem.at[1])
    store_theirs.start()
    store_mine.wait()
    store_theirs.wait()


def both_slots(index, keep, got, before):
    return pl.pallas_call(
        functools.partial(slots_kernel, index),
        out_shape=jax.ShapeDtypeStruct((2, *keep.shape), F32),
        in_specs=[HBM, HBM, HBM],
        out_specs=HBM,
        scratch_shapes=[
            pltpu.VMEM(keep.shape, F32),
            pltpu.VMEM(keep.shape, BF16),
            pltpu.VMEM(keep.shape, F32),
            pltpu.SemaphoreType.DMA((2,)),
            pltpu.SemaphoreType.DMA((2,)),
        ],
        compiler_params=pltpu.CompilerParams(vmem_limit_bytes=VMEM_BYTES),
        cost_estimate=FREE,
        name="both_slots",
    )(keep, got, before)


def tail(layers, grads, out_keep, in_keep, sends, weight_shapes):
    bits = lax.axis_size("dp").bit_length() - 1
    by_x = list(range(bits))
    orders = (by_x[:1] + by_x[2:] + by_x[1:2], [1, 0] + by_x[2:], by_x[2:-1] + [1, 0] + by_x[-1:])
    streams = []
    for (keep, send), order in zip(grads, orders):
        extra = keep.shape[1] - keep.shape[2] // 2 if keep is grads[2][0] else 0
        if len(layers) == 1:
            keep, send = [a[layers[0] : layers[0] + 1] for a in (keep, send)]
        streams.append(Stream(layers, keep, send, order, extra))
    for stream in streams:
        stream.enter()
    slots_got = swap(sends)
    chain = [sends]
    for turn in range(bits):
        for stream in streams:
            stream.send_half(turn, chain)
        for stream in streams:
            stream.keep_half(turn, chain)
        if turn == 0:
            out_half = both_slots(0, out_keep, slots_got, chain[-1])
            grad_half = both_slots(1, in_keep, slots_got, out_half)
            chain.append(grad_half)
    for stream in streams:
        stream.exchange(chain)
    for turn in range(bits):
        for stream in streams:
            stream.gather(turn, chain)
    kinds = ("rows", "cols", "attn")
    placed, results = [], []
    for kind, stream, shapes in zip(kinds, streams, weight_shapes):
        placed.append(place(kind, 0, layers, stream.order[0], stream.part, shapes, [chain[-1]]))
        chain.append(placed[-1][0])
    for kind, stream, shapes, half in zip(kinds, streams, weight_shapes, placed):
        half = [*half, chain[-1]]
        results += place(kind, 1, layers, stream.order[0], stream.got, shapes, half)
        chain.append(results[-1])
    vec = streams[2].vec[0][0].astype(F32)
    if len(layers) == 1:
        vec = jnp.where(lax.axis_index("section") == layers[0], vec, 0.0)
    return (*results, vec, out_half, grad_half)


def on_device(
    inputs, cotangent, lengths, assignment, skip_flags, head_counts, ffn_counts,
    w_qkv, bias_q, bias_v, w_out, bias_out, norm1_gain, norm1_bias, w_up, bias_up, w_down,
    bias_down, norm2_gain, norm2_bias,
):
    section = lax.axis_index("section")
    first = section == 0
    slots, length, width = inputs.shape
    units = w_up.shape[2]
    zeros = jnp.zeros((1, width), BF16)
    own_counts = jnp.concatenate([skip_flags, head_counts, ffn_counts], axis=0).reshape(3 * MICRO)
    coded = jnp.concatenate([own_counts // 64, own_counts % 64]).astype(BF16).reshape(1, 6 * MICRO)
    own_vec = jnp.concatenate(
        [
            bias_q, zeros, bias_v, bias_out, norm1_gain, norm1_bias,
            bias_up.reshape(units // width, width),
            bias_down, norm2_gain, norm2_bias,
            jnp.pad(coded, ((0, 0), (0, width - 6 * MICRO))), zeros, zeros,
        ],
        axis=0,
    )
    other_vec = swap(own_vec)
    codes = other_vec[13, : 6 * MICRO].astype(jnp.int32)
    other_counts = codes[: 3 * MICRO] * 64 + codes[3 * MICRO :]
    weights = []
    for mine in (w_qkv[0], w_out[0], w_up[0], w_down[0]):
        weights += [mine, swap(mine)]
    weights += [own_vec, other_vec]
    scalars = [own_counts, other_counts, assignment, lengths]

    early = weights[:2] * 4 + weights[8:]
    proj, ctx, stat = layer_forward(False, "attend", scalars, inputs, early)
    passed, *saved_one = layer_forward(
        False, "finish", scalars, inputs, weights[2:4] + weights[2:], [ctx, stat]
    )
    saved_one = [proj, ctx, *saved_one]
    out_keep, sends, *saved_two = layer_forward(True, "all", scalars, passed, weights)
    saved_two = saved_two[:2] + saved_two[3:]

    res, *ffn, sums = ffn_back(True, scalars, cotangent, weights, saved_two)
    g_mid, *attn = attention_back(
        False, scalars, res, cotangent, passed, weights, saved_two, sums
    )
    res, *ffn, sums = ffn_back(False, scalars, g_mid, weights, saved_one, ffn)
    in_keep, sends, *attn = attention_back(
        True, scalars, res, g_mid, inputs, weights, saved_one, sums, [sends, *attn]
    )

    grads = (ffn[:2], ffn[2:], attn)
    weight_shapes = (
        [(1, units, width)], [(1, width, units)], [(1, width, width), (1, width, 3 * width)],
    )
    skips = [jnp.where(section == layer, own_counts, other_counts)[:MICRO] for layer in range(2)]
    used = [jnp.sum(skip) < MICRO for skip in skips]
    which = jnp.where(used[0] & used[1], 0, jnp.where(used[0], 1, 2))
    branches = [
        functools.partial(tail, layers, weight_shapes=weight_shapes) for layers in ((0, 1), (0,), (1,))
    ]
    grad_w_down, grad_w_up, grad_w_out, grad_w_qkv, vec, out_half, grad_half = lax.switch(
        which, branches, grads, out_keep, in_keep, sends
    )
    by_ffn, by_attn = vec[:, :width], vec[:, width:]
    grad_bias_up = by_ffn[8 : 8 + units // width].reshape(1, units)
    return (
        out_half, grad_half, grad_w_qkv, by_attn[0:1], by_attn[1:2], grad_w_out, by_attn[2:3],
        by_ffn[0:1], by_ffn[1:2], grad_w_up, grad_bias_up, grad_w_down, by_ffn[4:5], by_ffn[2:3],
        by_ffn[3:4],
    )


def solution(mesh):
    three, two = P("section", None, None), P("section", None)
    return jax.shard_map(
        on_device,
        mesh=mesh,
        in_specs=(
            P("dp", None, None), P("dp", None, None), P(), P("dp"),
            P(None, "section"), P(None, "section"), P(None, "section"),
            three, two, two, three, two, two, two, three, two, three, two, two, two,
        ),
        out_specs=(
            P("dp", None, "section"), P("dp", None, "section"),
            three, two, two, three, two, two, two, three, two, three, two, two, two,
        ),
        check_vma=False,
    )
```

```python
import functools

import jax
import jax.numpy as jnp
from jax import lax
from jax.experimental import pallas as pl
from jax.experimental.pallas import tpu as pltpu
from jax.sharding import PartitionSpec as P

HEADS = 12
MICRO = 2
NORM_EPS = 1e-05
NEG_FILL = -1e30
F32 = jnp.float32
BF16 = jnp.bfloat16

ROWS = 256
UNITS = 512
LEAST = 1920 // UNITS
SAFE = 40.0
VMEM_BYTES = 64 * 1024 * 1024

OWN, BLOCKS, LIVE, LENGTH, PAIRS, COUNT, CHUNKS, SLOT, SKIP, SECTION = range(10)
V_BQ, V_ZERO, V_BV, V_BO, V_G1, V_B1, V_BU, V_BD, V_G2, V_B2 = 0, 1, 2, 3, 4, 5, 6, 10, 11, 12


def dot(left, right):
    return lax.dot_general(left, right, (((1,), (0,)), ((), ())), preferred_element_type=F32)


def dot_nt(left, right):
    return lax.dot_general(left, right, (((1,), (1,)), ((), ())), preferred_element_type=F32)


def dot_tn(left, right):
    return lax.dot_general(left, right, (((0,), (0,)), ((), ())), preferred_element_type=F32)


def rows_at(block):
    if isinstance(block, int):
        return pl.ds(block * ROWS, ROWS)
    return pl.ds(pl.multiple_of(block * ROWS, ROWS), ROWS)


def cols_at(start, size):
    if isinstance(start, int):
        return pl.ds(start, size)
    return pl.ds(pl.multiple_of(start, 128), size)


def facts(layer, own_counts, other_counts, assigned, lengths):
    section = lax.axis_index("section")
    own = section == layer

    def count(row):
        at = row * MICRO + section
        return jnp.where(own, own_counts[at], other_counts[at])

    skip, heads, units = count(0), count(1), count(2)
    length = lengths[assigned[section]]
    live = (length + ROWS - 1) // ROWS
    blocks = jnp.where(skip == 1, 0, live)
    chunks = jnp.where(skip == 1, 0, (units + UNITS - 1) // UNITS)
    return [own.astype(jnp.int32), blocks, live, length, heads // 2, units, chunks, section, skip, section]


def by_blocks(count, most, body):
    pl.when(count > 0)(functools.partial(body, most))


def clear_dead(count, *refs):
    def clear(block, carry):
        for ref in refs:
            ref[rows_at(block), :] = jnp.zeros((ROWS, ref.shape[1]), ref.dtype)
        return carry

    lax.fori_loop(count, refs[0].shape[0] // ROWS, clear, 0)


def by_chunks(count, most, body):
    body(0, LEAST + 1)
    pl.when(count > LEAST + 1)(functools.partial(body, LEAST + 1, most))


def fetch_start(s, dst, own_ref, other_ref, sem):
    @pl.when(s[OWN] == 1)
    def _():
        pltpu.make_async_copy(own_ref, dst, sem).start()

    @pl.when(s[OWN] == 0)
    def _():
        pltpu.make_async_copy(other_ref, dst, sem).start()


def live_column(s, block):
    frame = lax.broadcasted_iota(jnp.int32, (ROWS, 1), 0) + block * ROWS
    return frame < s[LENGTH]


def gelu_parts(values):
    under = 1.0 + 0.2316419 * jnp.abs(values)
    t = pl.reciprocal(under, approx=True)
    t = t * (2.0 - under * t)
    poly = t * (
        0.319381530 + t * (-0.356563782 + t * (1.781477937 + t * (-1.821255978 + t * 1.330274429)))
    )
    bell = jnp.exp2(values * values * -0.7213475204444817) * 0.3989422804014327
    tail = poly * bell
    below = jnp.where(values >= 0, 1.0 - tail, tail)
    return values * below, below + values * bell


def spread_heads(width):
    head = lax.broadcasted_iota(jnp.int32, (128, width), 1) // 64
    return (head == lax.broadcasted_iota(jnp.int32, (128, width), 0)).astype(BF16)


def norm_parts(values):
    center = jnp.mean(values, axis=-1, keepdims=True)
    shifted = values - center
    spread = jnp.mean(shifted * shifted, axis=-1, keepdims=True)
    inverse = lax.rsqrt(spread + NORM_EPS)
    return shifted * inverse, inverse


def vec_row(vec_ref, row):
    return vec_ref[row : row + 1, :].astype(F32)


def forward_kernel(
    last,
    phase,
    own_counts, other_counts, assigned, lengths,
    x_hbm,
    wq0, wq1, wo0, wo1, wu0, wu1, wd0, wd1, v0, v1,
    *rest,
):
    s = facts(1 if last else 0, own_counts, other_counts, assigned, lengths)
    attends, finishes = phase != "finish", phase != "attend"
    if not attends:
        ctx_in, stat_in = rest[:2]
        rest = rest[2:]
    if finishes and last:
        keep_hbm, send_hbm = rest[:2]
        rest = rest[2:]
    elif finishes:
        pass_hbm = rest[0]
        rest = rest[1:]
    if attends:
        proj_hbm, ctx_hbm, lse_hbm = rest[:3]
        rest = rest[3:]
    if finishes:
        stat_hbm, gated_hbm, slope_hbm, x1_hbm, x2_hbm = rest[:5]
        rest = rest[5:]
    (
        h, wq, wo, wu, wd, vec, proj, ctx, stat, gated, slope, x1, x2, acc, normed_b, bias_up, largest, out_a, out_b,
        in_sem, w_sem, out_sem,
    ) = rest
    most = h.shape[0] // ROWS
    width = h.shape[1]
    pairs_all = width // 128
    blocks = s[BLOCKS]
    live = s[LIVE]
    lane = lax.broadcasted_iota(jnp.int32, (1, 128), 1)
    low = lane < 64

    def source(block):
        if last:
            return x_hbm.at[rows_at(block)]
        return x_hbm.at[s[SLOT], rows_at(block)]

    def h_copy(block):
        return pltpu.make_async_copy(source(block), h.at[rows_at(block)], in_sem.at[block])

    for block in range(most):
        pl.when(block < live)(lambda block=block: h_copy(block).start())

    @pl.when(blocks > 0)
    def _():
        fetch_start(s, vec, v0, v1, w_sem.at[0])
        if attends:
            fetch_start(s, wq, wq0, wq1, w_sem.at[1])
        if finishes:
            fetch_start(s, wo, wo0, wo1, w_sem.at[2])
            fetch_start(s, wu, wu0, wu1, w_sem.at[3])
            fetch_start(s, wd, wd0, wd1, w_sem.at[4])

    def reload(what, block):
        target, source = ((ctx, ctx_in), (stat, stat_in))[what]
        return pltpu.make_async_copy(
            source.at[rows_at(block)], target.at[rows_at(block)], out_sem.at[what, block]
        )

    if not attends:
        for block in range(most):
            @pl.when(block < blocks)
            def _(block=block):
                reload(0, block).start()
                reload(1, block).start()

    for block in range(most):
        pl.when(block < live)(lambda block=block: h_copy(block).wait())

    def save(what, source_ref, target_ref, block):
        return pltpu.make_async_copy(
            source_ref.at[rows_at(block)], target_ref.at[rows_at(block)], out_sem.at[what, block]
        )

    def emit(block, value):
        if last:
            half = width // 2
            first = s[SECTION] == 0
            out_a[rows_at(block), :] = jnp.where(first, value[:, :half], value[:, half:])
            out_b[rows_at(block), :] = jnp.where(first, value[:, half:], value[:, :half]).astype(BF16)
            save(7, out_a, keep_hbm, block).start()
            save(8, out_b, send_hbm.at[0], block).start()
        else:
            out_b[rows_at(block), :] = value.astype(BF16)
            save(7, out_b, pass_hbm, block).start()

    def attention():
        pltpu.make_async_copy(wq0, wq, w_sem.at[1]).wait()

        spread = spread_heads(width)
        largest[...] = jnp.zeros(largest.shape, F32)

        def project(block, carry):
            rows = rows_at(block)
            for part, row in ((0, V_BQ), (1, V_ZERO), (2, V_BV)):
                cols = slice(part * width, (part + 1) * width)
                proj[rows, cols] = (dot(h[rows, :], wq[:, cols]) + vec_row(vec, row)).astype(BF16)
            save(0, proj, proj_hbm, block).start()
            for part in range(2):
                value = proj[rows, part * width : (part + 1) * width].astype(F32)
                squares = dot_nt(spread, (value * value).astype(BF16))
                largest[part] = jnp.maximum(largest[part], squares)
            stat[rows, :] = jnp.zeros((ROWS, 128), F32)
            return carry

        lax.fori_loop(0, blocks, project, 0)

        clear_dead(blocks, proj)
        for pair in range(pairs_all):
            @pl.when(pair >= s[PAIRS])
            def _(pair=pair):
                ctx[:, pair * 128 : (pair + 1) * 128] = jnp.zeros((h.shape[0], 128), BF16)

        bound = jnp.max(largest[0]) * jnp.max(largest[1]) * 1.02
        safe = bound <= (SAFE * 8.0) ** 2

        def attend_safe(count):
            key_at = lax.broadcasted_iota(jnp.int32, (1, ROWS), 1)
            fills = [
                jnp.where(key_at + part * ROWS < s[LENGTH], 0.0, NEG_FILL) for part in range(count)
            ]

            span = count * ROWS

            def one(pair, carry):
                cols = cols_at(pair * 128, 128)
                q = proj[0:span, cols] * jnp.asarray(0.125, BF16)
                zero = jnp.zeros_like(q)
                ones = jnp.ones((ROWS, 128), BF16)
                q_own = [jnp.where(own, q, zero) for own in (low, ~low)]
                found = [None, None]
                for part in range(count):
                    keys = slice(part * ROWS, (part + 1) * ROWS)
                    k = proj[keys, cols_at(width + pair * 128, 128)]
                    v = proj[keys, cols_at(2 * width + pair * 128, 128)]
                    for head, own in enumerate((low, ~low)):
                        scores = dot_nt(q_own[head], k)
                        scores = scores + fills[part]
                        exps = jnp.exp(scores).astype(BF16)
                        more = dot(exps, jnp.where(own, v, ones))
                        found[head] = more if part == 0 else found[head] + more
                above = jnp.where(low, found[0], found[1])
                total = pltpu.roll(jnp.where(low, found[1], found[0]), 64, 1)
                ctx[0:span, cols] = (above / total).astype(BF16)
                logs = jnp.log(total)
                kept = stat[0:span, :]
                kept = jnp.where(lane == 2 * pair, logs[:, 0:1], kept)
                kept = jnp.where(lane == 2 * pair + 1, logs[:, 64:65], kept)
                stat[0:span, :] = kept
                return carry

            lax.fori_loop(0, s[PAIRS], one, 0)

        def attend():
            span = most * ROWS
            key_live = lax.broadcasted_iota(jnp.int32, (1, span), 1) < s[LENGTH]

            def clear_rows(block, carry):
                proj[rows_at(block), width:] = jnp.zeros((ROWS, 2 * width), BF16)
                return carry

            lax.fori_loop(blocks, most, clear_rows, 0)

            def one(step, carry):
                pair, block = step // blocks, step % blocks
                rows = rows_at(block)
                cols = cols_at(pair * 128, 128)
                q = proj[rows, cols] * jnp.asarray(0.125, BF16)
                k = proj[:, cols_at(width + pair * 128, 128)]
                v = proj[:, cols_at(2 * width + pair * 128, 128)]
                zero = jnp.zeros_like(q)
                ones = jnp.ones_like(v)
                found, peaks = [], []
                for own in (low, ~low):
                    scores = jnp.where(key_live, dot_nt(jnp.where(own, q, zero), k), NEG_FILL)
                    peak = jnp.max(scores, axis=-1, keepdims=True)
                    exps = jnp.exp(scores - peak).astype(BF16)
                    found.append(dot(exps, jnp.where(own, v, ones)))
                    peaks.append(peak)
                above = jnp.where(low, found[0], found[1])
                total = pltpu.roll(jnp.where(low, found[1], found[0]), 64, 1)
                ctx[rows, cols] = (above / total).astype(BF16)
                logs = jnp.where(low, peaks[0], peaks[1]) + jnp.log(total)
                kept = stat[rows, :]
                kept = jnp.where(lane == 2 * pair, logs[:, 0:1], kept)
                kept = jnp.where(lane == 2 * pair + 1, logs[:, 64:65], kept)
                stat[rows, :] = kept
                return carry

            lax.fori_loop(0, s[PAIRS] * blocks, one, 0)

        by_blocks(jnp.where(safe, blocks, 0), most, attend_safe)
        pl.when(jnp.logical_not(safe))(attend)

    def feed_forward():
        for piece in range(wu.shape[1] // width):
            bias_up[0:1, piece * width : (piece + 1) * width] = vec_row(vec, V_BU + piece)
        pltpu.make_async_copy(wo0, wo, w_sem.at[2]).wait()
        pltpu.make_async_copy(wu0, wu, w_sem.at[3]).wait()
        pltpu.make_async_copy(wd0, wd, w_sem.at[4]).wait()

        def finish(block, carry):
            rows = rows_at(block)
            if attends:
                save(1, ctx, ctx_hbm, block).start()
            else:
                reload(0, block).wait()
                reload(1, block).wait()
            res = h[rows, :].astype(F32) + dot(ctx[rows, :], wo[...]) + vec_row(vec, V_BO)
            hat, inverse_one = norm_parts(res)
            x1[rows, :] = hat.astype(BF16)
            save(5, x1, x1_hbm, block).start()
            normed = hat * vec_row(vec, V_G1) + vec_row(vec, V_B1)
            normed_b[...] = normed.astype(BF16)
            acc[...] = normed + vec_row(vec, V_BD)

            def units(start, stop):
                def lift(c):
                    cols = slice(c * UNITS, (c + 1) * UNITS)
                    return dot(normed_b[...], wu[:, cols]) + bias_up[0:1, cols]

                more = None
                later = lift(start)
                for c in range(start, stop):
                    cols = slice(c * UNITS, (c + 1) * UNITS)
                    lifted = later
                    if c + 1 < stop:
                        later = lift(c + 1)
                    value, grad = gelu_parts(lifted)
                    if c >= LEAST:
                        unit = lax.broadcasted_iota(jnp.int32, (1, UNITS), 1) + c * UNITS
                        value = jnp.where(unit < s[COUNT], value, 0.0)
                        grad = jnp.where(unit < s[COUNT], grad, 0.0)
                    value_b = value.astype(BF16)
                    gated[rows, cols] = value_b
                    slope[rows, cols] = grad.astype(BF16)
                    part = dot(value_b, wd[cols, :])
                    more = part if more is None else more + part
                acc[...] += more

            units(0, wu.shape[1] // UNITS)
            save(3, gated, gated_hbm, block).start()
            save(4, slope, slope_hbm, block).start()
            hat_two, inverse_two = norm_parts(acc[...])
            x2[rows, :] = hat_two.astype(BF16)
            save(6, x2, x2_hbm, block).start()
            kept = stat[rows, :]
            kept = jnp.where(lane == HEADS, inverse_one, kept)
            stat[rows, :] = jnp.where(lane == HEADS + 1, inverse_two, kept)
            save(2, stat, stat_hbm, block).start()
            result = hat_two * vec_row(vec, V_G2) + vec_row(vec, V_B2)
            emit(block, jnp.where(live_column(s, block), result, 0.0))
            return carry

        lax.fori_loop(0, blocks, finish, 0)

    @pl.when(blocks > 0)
    def _():
        pltpu.make_async_copy(v0, vec, w_sem.at[0]).wait()
        if attends:
            attention()
        if finishes:
            feed_forward()

    if not finishes:
        def keep(block, carry):
            save(1, ctx, ctx_hbm, block).start()
            save(2, stat, lse_hbm, block).start()
            return carry

        lax.fori_loop(0, blocks, keep, 0)
        for block in range(most):
            @pl.when(block < blocks)
            def _(block=block):
                save(0, proj, proj_hbm, block).wait()
                save(1, ctx, ctx_hbm, block).wait()
                save(2, stat, lse_hbm, block).wait()
        return

    @pl.when(s[SKIP] == 1)
    def _():
        def carry_on(block, carry):
            value = h[rows_at(block), :].astype(F32)
            emit(block, jnp.where(live_column(s, block), value, 0.0) if last else value)
            return carry

        lax.fori_loop(0, live, carry_on, 0)

    if last:
        def clear(block, carry):
            emit(block, jnp.zeros((ROWS, width), F32))
            return carry

        lax.fori_loop(live, most, clear, 0)

    for block in range(most):
        @pl.when(block < blocks)
        def _(block=block):
            if attends:
                save(0, proj, proj_hbm, block).wait()
                save(1, ctx, ctx_hbm, block).wait()
            save(2, stat, stat_hbm, block).wait()
            save(3, gated, gated_hbm, block).wait()
            save(4, slope, slope_hbm, block).wait()
            save(5, x1, x1_hbm, block).wait()
            save(6, x2, x2_hbm, block).wait()

        if last:
            save(7, out_a, keep_hbm, block).wait()
            save(8, out_b, send_hbm.at[0], block).wait()
        else:
            pl.when(block < live)(lambda block=block: save(7, out_b, pass_hbm, block).wait())


HBM = pl.BlockSpec(memory_space=pltpu.HBM)
SMEM = pl.BlockSpec(memory_space=pltpu.SMEM)


def layer_forward(last, phase, scalars, x, weights, attended=()):
    length, width = x.shape[-2:]
    units = weights[4].shape[1]
    blocks = length // ROWS
    shape = jax.ShapeDtypeStruct
    attends, finishes = phase != "finish", phase != "attend"
    outs = []
    if finishes and last:
        outs += [shape((length, width // 2), F32), shape((2, length, width // 2), BF16)]
    elif finishes:
        outs += [shape((length, width), BF16)]
    if attends:
        outs += [
            shape((length, 3 * width), BF16),
            shape((length, width), BF16),
            shape((length, 128), F32),
        ]
    if finishes:
        outs += [
            shape((length, 128), F32),
            shape((length, units), BF16),
            shape((length, units), BF16),
            shape((length, width), BF16),
            shape((length, width), BF16),
        ]

    def held(used, size, dtype=BF16):
        return pltpu.VMEM(size if used else (16, 128), dtype)

    return pl.pallas_call(
        functools.partial(forward_kernel, last, phase),
        out_shape=outs,
        in_specs=[SMEM] * 4 + [HBM] * (11 + len(attended)),
        out_specs=[HBM] * len(outs),
        scratch_shapes=[
            pltpu.VMEM((length, width), BF16),
            held(attends, (width, 3 * width)),
            held(finishes, (width, width)),
            held(True, (width, units)),
            held(finishes, (units, width)),
            pltpu.VMEM(weights[8].shape, BF16),
            held(attends, (length, 3 * width)),
            pltpu.VMEM((length, width), BF16),
            pltpu.VMEM((length, 128), F32),
            held(finishes, (length, units)),
            held(finishes, (length, units)),
            held(finishes, (length, width)),
            held(finishes, (length, width)),
            held(finishes, (ROWS, width), F32),
            held(finishes, (ROWS, width)),
            pltpu.VMEM((8, units), F32),
            pltpu.VMEM((2, 128, ROWS), F32),
            held(finishes and last, (length, width // 2), F32),
            held(finishes, (length, width // 2 if last else width)),
            pltpu.SemaphoreType.DMA((blocks,)),
            pltpu.SemaphoreType.DMA((5,)),
            pltpu.SemaphoreType.DMA((9, blocks)),
        ],
        compiler_params=pltpu.CompilerParams(vmem_limit_bytes=VMEM_BYTES),
        cost_estimate=pl.CostEstimate(
            flops=60_000_000_000 if phase == "attend" else 10_000_000_000,
            bytes_accessed=0,
            transcendentals=0,
        ),
        name="layer_forward_" + phase,
    )(*scalars, x, *weights, *attended)


def ffn_back_kernel(
    first_pass,
    own_counts, other_counts, assigned, lengths,
    g_hbm,
    wu0, wu1, wd0, wd1, v0, v1,
    stat_hbm, gated_hbm, slope_hbm, x1_hbm, x2_hbm,
    *rest,
):
    if not first_pass:
        rest = rest[4:]
    (
    res_hbm, gd_keep, gd_send, gu_keep, gu_send, vec_hbm,
    g_out, wu, wd, vec, stat, gated, slope, x1, x2, res, down, normed, gd, gu, acc, sums, sums_up,
    in_sem, w_sem, out_sem, gd_sem, gu_sem,
    ) = rest
    layer = 1 if first_pass else 0
    s = facts(layer, own_counts, other_counts, assigned, lengths)
    most = g_out.shape[0] // ROWS
    width = g_out.shape[1]
    units = wu.shape[1]
    chunks = units // UNITS
    blocks = s[BLOCKS]

    def load(what, block):
        target, source = (
            (g_out, g_hbm.at[s[SLOT]] if first_pass else g_hbm),
            (stat, stat_hbm), (gated, gated_hbm), (slope, slope_hbm), (x1, x1_hbm), (x2, x2_hbm),
        )[what]
        return pltpu.make_async_copy(
            source.at[rows_at(block)], target.at[rows_at(block)], in_sem.at[what, block]
        )

    @pl.when(blocks > 0)
    def _():
        fetch_start(s, vec, v0, v1, w_sem.at[0])

    for block in range(most):
        @pl.when(block < blocks)
        def _(block=block):
            for what in (0, 1, 5, 3, 4):
                load(what, block).start()

        if block == 0:
            @pl.when(blocks > 0)
            def _():
                fetch_start(s, wd, wd0, wd1, w_sem.at[2])
                fetch_start(s, wu, wu0, wu1, w_sem.at[1])

    for block in range(most):
        pl.when(block < blocks)(lambda block=block: load(2, block).start())

    sums[...] = jnp.zeros(sums.shape, F32)
    sums_up[...] = jnp.zeros(sums_up.shape, F32)

    @pl.when(blocks > 0)
    def _():
        pltpu.make_async_copy(v0, vec, w_sem.at[0]).wait()

        def step(block, carry):
            rows = rows_at(block)
            for what in (0, 1, 5):
                load(what, block).wait()
            inverse_one = stat[rows, HEADS : HEADS + 1]
            inverse_two = stat[rows, HEADS + 1 : HEADS + 2]
            gn = jnp.where(live_column(s, block), g_out[rows, :].astype(F32), 0.0)
            hat = x2[rows, :].astype(F32)
            sums[2:3, :] += jnp.sum(gn * hat, axis=0, keepdims=True)
            sums[3:4, :] += jnp.sum(gn, axis=0, keepdims=True)
            gh = gn * vec_row(vec, V_G2)
            mean_one = jnp.mean(gh, axis=-1, keepdims=True)
            mean_two = jnp.mean(gh * hat, axis=-1, keepdims=True)
            g_res = (gh - mean_one - hat * mean_two) * inverse_two
            down_b = g_res.astype(BF16)
            sums[4:5, :] += jnp.sum(down_b.astype(F32), axis=0, keepdims=True)
            down[rows, :] = down_b
            acc[...] = g_res

            @pl.when(block == 0)
            def _():
                pltpu.make_async_copy(wd0, wd, w_sem.at[2]).wait()
                pltpu.make_async_copy(wu0, wu, w_sem.at[1]).wait()

            load(3, block).wait()
            load(4, block).wait()

            def units(start, stop):
                def gate(c):
                    return dot_nt(down[rows, :], wd[c * UNITS : (c + 1) * UNITS, :])

                more = None
                later = gate(start)
                for c in range(start, stop):
                    cols = slice(c * UNITS, (c + 1) * UNITS)
                    g_gated = later
                    if c + 1 < stop:
                        later = gate(c + 1)
                    lift = (g_gated * slope[rows, cols].astype(F32)).astype(BF16)
                    slope[rows, cols] = lift
                    sums_up[0:1, cols] += jnp.sum(lift.astype(F32), axis=0, keepdims=True)
                    part = dot_nt(lift, wu[:, cols])
                    more = part if more is None else more + part
                acc[...] += more

            by_chunks(s[CHUNKS], chunks, units)
            g_normed = acc[...]
            hat = x1[rows, :].astype(F32)
            normed[rows, :] = (hat * vec_row(vec, V_G1) + vec_row(vec, V_B1)).astype(BF16)
            sums[0:1, :] += jnp.sum(g_normed * hat, axis=0, keepdims=True)
            sums[1:2, :] += jnp.sum(g_normed, axis=0, keepdims=True)
            gh = g_normed * vec_row(vec, V_G1)
            mean_one = jnp.mean(gh, axis=-1, keepdims=True)
            mean_two = jnp.mean(gh * hat, axis=-1, keepdims=True)
            res[rows, :] = (gh - mean_one - hat * mean_two) * inverse_one
            pltpu.make_async_copy(res.at[rows], res_hbm.at[rows], out_sem.at[block]).start()
            return carry

        lax.fori_loop(0, blocks, step, 0)
        for block in range(most):
            pl.when(block < blocks)(lambda block=block: load(2, block).wait())


    half_rows = units // 2
    half_cols = units // 2
    per_half = chunks // 2

    def chunk_copies(c):
        half, inside = c // per_half, c % per_half
        down_part = gd.at[cols_at(c * UNITS, UNITS), :]
        up_part = gu.at[:, cols_at(c * UNITS, UNITS)]
        place = cols_at(inside * UNITS, UNITS)
        return half, down_part, up_part, place

    def send_chunk(c):
        half, down_part, up_part, place = chunk_copies(c)

        @pl.when(half == s[SECTION])
        def _():
            pltpu.make_async_copy(down_part, gd_keep.at[layer, place, :], gd_sem.at[c]).start()
            pltpu.make_async_copy(up_part, gu_keep.at[layer, :, place], gu_sem.at[c]).start()

        @pl.when(half != s[SECTION])
        def _():
            pltpu.make_async_copy(down_part, gd_send.at[layer, place, :], gd_sem.at[c]).start()
            pltpu.make_async_copy(up_part, gu_send.at[layer, :, place], gu_sem.at[c]).start()

    def weigh(count):
        span = count * ROWS

        def one(c, carry):
            cols = cols_at(c * UNITS, UNITS)
            gd[cols, :] = dot_tn(gated[0:span, cols], down[0:span, :]).astype(BF16)
            gu[:, cols] = dot_tn(normed[0:span, :], slope[0:span, cols]).astype(BF16)
            send_chunk(c)
            return carry

        lax.fori_loop(0, s[CHUNKS], one, 0)

    pl.when(blocks > 0)(lambda: clear_dead(blocks, gated, down, normed, slope))
    by_blocks(blocks, most, weigh)

    def nothing(c, carry):
        cols = cols_at(c * UNITS, UNITS)
        gd[cols, :] = jnp.zeros((UNITS, width), BF16)
        gu[:, cols] = jnp.zeros((width, UNITS), BF16)
        send_chunk(c)
        return carry

    lax.fori_loop(s[CHUNKS], chunks, nothing, 0)

    for c in range(chunks):
        _, down_part, up_part, place = chunk_copies(c)
        pltpu.make_async_copy(down_part, gd_keep.at[layer, place, :], gd_sem.at[c]).wait()
        pltpu.make_async_copy(up_part, gu_keep.at[layer, :, place], gu_sem.at[c]).wait()
    for piece in range(units // width):
        sums[8 + piece : 9 + piece, :] = sums_up[0:1, piece * width : (piece + 1) * width]
    pltpu.sync_copy(sums, vec_hbm)
    for block in range(most):
        @pl.when(block < blocks)
        def _(block=block):
            rows = rows_at(block)
            pltpu.make_async_copy(res.at[rows], res_hbm.at[rows], out_sem.at[block]).wait()


def ffn_back(first_pass, scalars, g_out, weights, saved, grads=()):
    length, width = g_out.shape[-2:]
    units = weights[4].shape[1]
    blocks = length // ROWS
    chunks = units // UNITS
    shape = jax.ShapeDtypeStruct
    _, _, stat, gated, slope, x1, x2 = saved
    return pl.pallas_call(
        functools.partial(ffn_back_kernel, first_pass),
        out_shape=[
            shape((length, width), F32),
            shape((2, units // 2, width), BF16),
            shape((2, units // 2, width), BF16),
            shape((2, width, units // 2), BF16),
            shape((2, width, units // 2), BF16),
            shape((16, width), F32),
        ],
        in_specs=[SMEM] * 4 + [HBM] * (12 + len(grads)),
        out_specs=[HBM] * 6,
        input_output_aliases={16 + i: 1 + i for i in range(len(grads))},
        scratch_shapes=[
            pltpu.VMEM((length, width), BF16),
            pltpu.VMEM((width, units), BF16),
            pltpu.VMEM((units, width), BF16),
            pltpu.VMEM(weights[8].shape, BF16),
            pltpu.VMEM((length, 128), F32),
            pltpu.VMEM((length, units), BF16),
            pltpu.VMEM((length, units), BF16),
            pltpu.VMEM((length, width), BF16),
            pltpu.VMEM((length, width), BF16),
            pltpu.VMEM((length, width), F32),
            pltpu.VMEM((length, width), BF16),
            pltpu.VMEM((length, width), BF16),
            pltpu.VMEM((units, width), BF16),
            pltpu.VMEM((width, units), BF16),
            pltpu.VMEM((ROWS, width), F32),
            pltpu.VMEM((16, width), F32),
            pltpu.VMEM((8, units), F32),
            pltpu.SemaphoreType.DMA((6, blocks)),
            pltpu.SemaphoreType.DMA((3,)),
            pltpu.SemaphoreType.DMA((blocks,)),
            pltpu.SemaphoreType.DMA((chunks,)),
            pltpu.SemaphoreType.DMA((chunks,)),
        ],
        compiler_params=pltpu.CompilerParams(vmem_limit_bytes=VMEM_BYTES),
        name="ffn_back",
    )(*scalars, g_out, *weights[4:8], *weights[8:10], stat, gated, slope, x1, x2, *grads)


def attention_back_kernel(
    first_layer,
    own_counts, other_counts, assigned, lengths,
    res_hbm, g_hbm, x_hbm,
    wq0, wq1, wo0, wo1,
    proj_hbm, ctx_hbm, stat_hbm, ffn_sums_hbm,
    *rest,
):
    layer = 0 if first_layer else 1
    s = facts(layer, own_counts, other_counts, assigned, lengths)
    rest = rest[3 if first_layer else 0 :]
    if first_layer:
        in_keep, in_send = rest[:2]
        rest = rest[2:]
    else:
        in_hbm = rest[0]
        rest = rest[1:]
    (
        ga_keep, ga_send,
        res, g_in, h, wq, wo, proj, ctx, stat, attn, g_ctx, g_proj, rows_log, rows_delta,
        go, gq, out_a, out_b, sums, ffn_sums, extra,
        in_sem, w_sem, out_sem, go_sem, gq_sem, extra_sem,
    ) = rest
    most = res.shape[0] // ROWS
    width = res.shape[1]
    half = width // 2
    pairs_all = width // 128
    blocks = s[BLOCKS]
    live = s[LIVE]
    lane = lax.broadcasted_iota(jnp.int32, (1, 128), 1)
    low = lane < 64
    zero_pair = jnp.zeros((1, 128), BF16)

    def load(what, block):
        target, source = (
            (res, res_hbm), (ctx, ctx_hbm), (stat, stat_hbm), (proj, proj_hbm),
            (h, x_hbm.at[s[SLOT]] if first_layer else x_hbm),
        )[what]
        return pltpu.make_async_copy(
            source.at[rows_at(block)], target.at[rows_at(block)], in_sem.at[what, block]
        )

    def load_g(block):
        source = g_hbm if first_layer else g_hbm.at[s[SLOT]]
        return pltpu.make_async_copy(
            source.at[rows_at(block)], g_in.at[rows_at(block)], in_sem.at[0, block]
        )

    for what in (0, 1):
        for block in range(most):
            pl.when(block < blocks)(lambda what=what, block=block: load(what, block).start())

    @pl.when(blocks > 0)
    def _():
        fetch_start(s, wo, wo0, wo1, w_sem.at[0])

    for what in (2, 3, 4):
        for block in range(most):
            pl.when(block < blocks)(lambda what=what, block=block: load(what, block).start())

    @pl.when(blocks > 0)
    def _():
        fetch_start(s, wq, wq0, wq1, w_sem.at[1])

    sums[...] = jnp.zeros(sums.shape, F32)
    ffn_load = pltpu.make_async_copy(ffn_sums_hbm, ffn_sums, extra_sem.at[2])
    ffn_load.start()

    def out_copies(block, wait):
        rows = rows_at(block)
        if first_layer:
            copies = [
                pltpu.make_async_copy(out_a.at[rows], in_keep.at[rows], out_sem.at[0, block]),
                pltpu.make_async_copy(out_b.at[rows], in_send.at[1, rows], out_sem.at[1, block]),
            ]
        else:
            copies = [pltpu.make_async_copy(out_b.at[rows], in_hbm.at[rows], out_sem.at[0, block])]
        for copy in copies:
            copy.wait() if wait else copy.start()

    def emit(block, value):
        rows = rows_at(block)
        if first_layer:
            front = s[SECTION] == 0
            out_a[rows, :] = jnp.where(front, value[:, :half], value[:, half:])
            out_b[rows, :] = jnp.where(front, value[:, half:], value[:, :half]).astype(BF16)
        else:
            out_b[rows, :] = value.astype(BF16)
        out_copies(block, False)

    def go_copy(part, keep):
        target = (ga_keep if keep else ga_send).at[layer, 0:width, 0:half]
        return pltpu.make_async_copy(go.at[:, part * half : (part + 1) * half], target, go_sem.at[part])

    def gq_copy(part, keep):
        target = (ga_keep if keep else ga_send).at[layer, 0:width, half : 4 * half]
        cols = slice(part * 3 * half, (part + 1) * 3 * half)
        return pltpu.make_async_copy(gq.at[:, cols], target, gq_sem.at[part])

    def start_halves(make):
        for part in range(2):
            pl.when(s[SECTION] == part)(lambda part=part: make(part, True).start())
            pl.when(s[SECTION] != part)(lambda part=part: make(part, False).start())

    @pl.when(blocks > 0)
    def _():
        pltpu.make_async_copy(wo0, wo, w_sem.at[0]).wait()
        spread = spread_heads(width)

        def before(block, carry):
            rows = rows_at(block)
            load(0, block).wait()
            load(1, block).wait()
            attn_b = res[rows, :].astype(BF16)
            attn[rows, :] = attn_b
            sums[2:3, :] += jnp.sum(attn_b.astype(F32), axis=0, keepdims=True)
            g_context = dot_nt(attn_b, wo[...]).astype(BF16)
            g_ctx[rows, :] = g_context
            product = (g_context.astype(F32) * ctx[rows, :].astype(F32)).astype(BF16)
            rows_delta[:, rows] = dot_nt(spread, product)
            load(2, block).wait()
            rows_log[:, rows] = stat[rows, :].T
            load(3, block).wait()
            return carry

        lax.fori_loop(0, blocks, before, 0)
        clear_dead(blocks, proj, g_ctx, ctx, attn, h)

        def clear_columns(block, carry):
            rows_log[:, rows_at(block)] = jnp.zeros((128, ROWS), F32)
            rows_delta[:, rows_at(block)] = jnp.zeros((128, ROWS), F32)
            return carry

        lax.fori_loop(blocks, most, clear_columns, 0)

        def weigh_out(count):
            span = count * ROWS
            go[...] = dot_tn(ctx[0:span, :], attn[0:span, :]).astype(BF16)

        by_blocks(blocks, most, weigh_out)
        start_halves(go_copy)

        for pair in range(pairs_all):
            @pl.when(pair >= s[PAIRS])
            def _(pair=pair):
                for part in range(3):
                    cols = slice(part * width + pair * 128, part * width + (pair + 1) * 128)
                    g_proj[:, cols] = jnp.zeros((g_proj.shape[0], 128), BF16)

        def attend_back(count):
            span = count * ROWS

            def one_pair(pair, carry):
                cols = cols_at(pair * 128, 128)
                total_q = None
                for block in range(count):
                    rows = rows_at(block)
                    q = proj[0:span, cols]
                    d_ctx = g_ctx[0:span, cols]
                    k = proj[rows, cols_at(width + pair * 128, 128)] * jnp.asarray(0.125, BF16)
                    v = proj[rows, cols_at(2 * width + pair * 128, 128)]
                    fill = jnp.where(live_column(s, block), 0.0, NEG_FILL)
                    found_k, found_v, found_q = [], [], []
                    for head, own in ((0, low), (1, ~low)):
                        k_own = jnp.where(own, k, zero_pair)
                        v_own = jnp.where(own, v, zero_pair)
                        log_row = rows_log[pl.ds(2 * pair + head, 1), 0:span]
                        delta_row = rows_delta[pl.ds(2 * pair + head, 1), 0:span]
                        probs = jnp.exp(dot_nt(k_own, q) + fill - log_row)
                        g_probs = dot_nt(v_own, d_ctx)
                        g_scores = (probs * (g_probs - delta_row)).astype(BF16)
                        found_v.append(dot(probs.astype(BF16), d_ctx))
                        found_k.append(dot(g_scores, q))
                        found_q.append(dot_tn(g_scores, k_own))
                    more_q = found_q[0] + found_q[1]
                    total_q = more_q if block == 0 else total_q + more_q
                    g_k = jnp.where(low, found_k[0], found_k[1]) * 0.125
                    g_v = jnp.where(low, found_v[0], found_v[1])
                    g_proj[rows, cols_at(width + pair * 128, 128)] = g_k.astype(BF16)
                    g_proj[rows, cols_at(2 * width + pair * 128, 128)] = g_v.astype(BF16)
                g_proj[0:span, cols] = total_q.astype(BF16)
                return carry

            lax.fori_loop(0, s[PAIRS], one_pair, 0)

        by_blocks(blocks, most, attend_back)

        for block in range(most):
            pl.when(block < blocks)(lambda block=block: load(4, block).wait())
        pltpu.make_async_copy(wq0, wq, w_sem.at[1]).wait()

        def weigh_in(count):
            span = count * ROWS

            def one(part, carry):
                cols = cols_at(part * width, width)
                gq[:, cols] = dot_tn(h[0:span, :], g_proj[0:span, cols]).astype(BF16)
                return carry

            lax.fori_loop(0, 3, one, 0)

        by_blocks(blocks, most, weigh_in)
        start_halves(gq_copy)

        def after(block, carry):
            rows = rows_at(block)
            grad = g_proj[rows, :]
            sums[0:1, :] += jnp.sum(grad[:, :width].astype(F32), axis=0, keepdims=True)
            sums[1:2, :] += jnp.sum(grad[:, 2 * width :].astype(F32), axis=0, keepdims=True)
            emit(block, res[rows, :] + dot_nt(grad, wq[...]))
            return carry

        lax.fori_loop(0, blocks, after, 0)

    @pl.when(s[SKIP] == 1)
    def _():
        go[...] = jnp.zeros(go.shape, BF16)
        gq[...] = jnp.zeros(gq.shape, BF16)
        start_halves(go_copy)
        start_halves(gq_copy)
        for block in range(most):
            pl.when(block < live)(lambda block=block: load_g(block).start())
        for block in range(most):
            pl.when(block < live)(lambda block=block: load_g(block).wait())

        def carry_on(block, carry):
            value = g_in[rows_at(block), :].astype(F32)
            emit(block, jnp.where(live_column(s, block), value, 0.0))
            return carry

        lax.fori_loop(0, live, carry_on, 0)

    if first_layer:
        def clear(block, carry):
            emit(block, jnp.zeros((ROWS, width), F32))
            return carry

        lax.fori_loop(live, most, clear, 0)

    ffn_load.wait()
    own_sums = jnp.concatenate([sums[...], jnp.zeros(sums.shape, F32)], axis=0)
    extra[...] = jnp.concatenate([ffn_sums[...], own_sums], axis=1).astype(BF16)
    extra_copies = [
        pltpu.make_async_copy(extra, target.at[layer, width : width + 16], extra_sem.at[at])
        for at, target in enumerate((ga_keep, ga_send))
    ]
    for copy in extra_copies:
        copy.start()
    for copy in extra_copies:
        copy.wait()
    for part in range(2):
        go_copy(part, True).wait()
        gq_copy(part, True).wait()
    for block in range(most):
        if first_layer:
            out_copies(block, True)
        else:
            pl.when(block < live)(lambda block=block: out_copies(block, True))


def attention_back(first_layer, scalars, res, g_out, x, weights, saved, ffn_sums, grads=()):
    length, width = res.shape
    blocks = length // ROWS
    shape = jax.ShapeDtypeStruct
    proj, ctx, stat = saved[:3]
    outs = (
        [shape((length, width // 2), F32), shape((2, length, width // 2), BF16)]
        if first_layer
        else [shape((length, width), BF16)]
    )
    outs += [
        shape((2, width + 16, 2 * width), BF16),
        shape((2, width + 16, 2 * width), BF16),
    ]
    return pl.pallas_call(
        functools.partial(attention_back_kernel, first_layer),
        out_shape=outs,
        in_specs=[SMEM] * 4 + [HBM] * (11 + len(grads)),
        out_specs=[HBM] * len(outs),
        input_output_aliases={15 + i: len(outs) - len(grads) + i for i in range(len(grads))},
        scratch_shapes=[
            pltpu.VMEM((length, width), F32),
            pltpu.VMEM((length, width), BF16),
            pltpu.VMEM((length, width), BF16),
            pltpu.VMEM((width, 3 * width), BF16),
            pltpu.VMEM((width, width), BF16),
            pltpu.VMEM((length, 3 * width), BF16),
            pltpu.VMEM((length, width), BF16),
            pltpu.VMEM((length, 128), F32),
            pltpu.VMEM((length, width), BF16),
            pltpu.VMEM((length, width), BF16),
            pltpu.VMEM((length, 3 * width), BF16),
            pltpu.VMEM((128, length), F32),
            pltpu.VMEM((128, length), F32),
            pltpu.VMEM((width, width), BF16),
            pltpu.VMEM((width, 3 * width), BF16),
            pltpu.VMEM((length if first_layer else 8, width // 2), F32),
            pltpu.VMEM((length, width // 2 if first_layer else width), BF16),
            pltpu.VMEM((8, width), F32),
            pltpu.VMEM((16, width), F32),
            pltpu.VMEM((16, 2 * width), BF16),
            pltpu.SemaphoreType.DMA((5, blocks)),
            pltpu.SemaphoreType.DMA((2,)),
            pltpu.SemaphoreType.DMA((2, blocks)),
            pltpu.SemaphoreType.DMA((2,)),
            pltpu.SemaphoreType.DMA((2,)),
            pltpu.SemaphoreType.DMA((3,)),
        ],
        compiler_params=pltpu.CompilerParams(vmem_limit_bytes=VMEM_BYTES),
        name="attention_back",
    )(*scalars, res, g_out, x, *weights[0:4], proj, ctx, stat, ffn_sums, *grads)


def swap(part):
    return lax.ppermute(part, "section", [(0, 1), (1, 0)])


def across(part, bit):
    pairs = [(i, i ^ 1 << bit) for i in range(lax.axis_size("dp"))]
    return lax.ppermute(part, "dp", pairs)


FREE = pl.CostEstimate(flops=0, bytes_accessed=0, transcendentals=0)
SHORT = pl.CostEstimate(flops=4_000_000_000, bytes_accessed=0, transcendentals=0)
LONG = pl.CostEstimate(flops=20_000_000_000, bytes_accessed=0, transcendentals=0)


def my_bit(bit):
    return (lax.axis_index("dp") >> bit) & 1


def half_sum_kernel(bit, turn, extra, keep, got, before, out, own, new, in_sem, out_sem):
    layers, rows, _ = keep.shape
    half = (rows - extra) // 2
    at = 1 - my_bit(bit) if turn == 0 else my_bit(bit)
    spans = [(pl.ds(pl.multiple_of(at * half, 16), half), slice(0, half))]
    if extra:
        spans.append((slice(rows - extra, rows), slice(half, half + extra)))

    def loads(layer):
        copies = []
        for i, (source, target) in enumerate(spans):
            for j, (ref, held) in enumerate(((keep, own), (got, new))):
                copies.append(
                    pltpu.make_async_copy(
                        ref.at[layer, source], held.at[layer, target], in_sem.at[layer, i, j]
                    )
                )
        return copies

    def store(layer):
        return pltpu.make_async_copy(own.at[layer], out.at[layer], out_sem.at[layer])

    for layer in range(layers):
        for copy in loads(layer):
            copy.start()
    for layer in range(layers):
        for copy in loads(layer):
            copy.wait()

        def add_rows(i, carry, layer=layer):
            place = pl.ds(pl.multiple_of(i * 16, 16), 16)
            total = own[layer, place, :].astype(F32) + new[layer, place, :].astype(F32)
            own[layer, place, :] = total.astype(BF16)
            return carry

        lax.fori_loop(0, (half + extra) // 16, add_rows, 0, unroll=3)
        store(layer).start()
    for layer in range(layers):
        store(layer).wait()


def half_sum(bit, turn, extra, keep, got, before):
    layers, rows, cols = keep.shape
    half = (rows - extra) // 2
    if half % 48:
        at = 1 - my_bit(bit) if turn == 0 else my_bit(bit)

        def parts(a):
            own = lax.dynamic_slice_in_dim(a, at * half, half, 1)
            return jnp.concatenate([own, a[:, rows - extra :]], axis=1).astype(F32)

        return (parts(keep) + parts(got)).astype(BF16)
    return pl.pallas_call(
        functools.partial(half_sum_kernel, bit, turn, extra),
        out_shape=jax.ShapeDtypeStruct((layers, half + extra, cols), BF16),
        in_specs=[HBM, HBM, HBM],
        out_specs=HBM,
        scratch_shapes=[
            pltpu.VMEM((layers, half + extra, cols), BF16),
            pltpu.VMEM((layers, half + extra, cols), BF16),
            pltpu.SemaphoreType.DMA((layers, 2, 2)),
            pltpu.SemaphoreType.DMA((layers,)),
        ],
        compiler_params=pltpu.CompilerParams(vmem_limit_bytes=VMEM_BYTES),
        cost_estimate=FREE if turn else SHORT,
        name="half_sum",
    )(keep, got, before)


def split_kernel(extra, one, two, before, own, send, *vec):
    layers, rows, _ = one.shape
    rows -= extra
    section = lax.axis_index("section")
    mine, theirs = (section, 1 - section) if layers == 2 else (0, 0)

    def total(at, where):
        return (one[pl.ds(at, 1), where].astype(F32) + two[pl.ds(at, 1), where].astype(F32)).astype(BF16)

    own[...] = total(mine, slice(0, rows))
    send[...] = total(theirs, slice(0, rows))
    if extra:
        vec[0][...] = total(mine, slice(rows, rows + extra))


def split(one, two, before, extra):
    layers, rows, cols = one.shape
    rows -= extra
    if rows % 16:
        total = (one.astype(F32) + two.astype(F32)).astype(BF16)
        own = send = total
        if layers == 2:
            section = lax.axis_index("section")
            own = lax.dynamic_slice_in_dim(total, section, 1)
            send = lax.dynamic_slice_in_dim(total, 1 - section, 1)
        return (own[:, :rows], send[:, :rows]) + ((own[:, rows:],) if extra else ())
    whole = pl.BlockSpec(memory_space=pltpu.VMEM)
    outs = [jax.ShapeDtypeStruct((1, rows, cols), BF16)] * 2
    if extra:
        outs.append(jax.ShapeDtypeStruct((1, extra, cols), BF16))
    return pl.pallas_call(
        functools.partial(split_kernel, extra),
        out_shape=outs,
        in_specs=[whole, whole, HBM],
        out_specs=[whole] * len(outs),
        cost_estimate=SHORT,
        name="split",
    )(one, two, before)


def join_kernel(bit, part, got, before, both, held, in_sem, out_sem):
    layers, rows, _ = part.shape
    mine = my_bit(bit)
    steps = [(at, layer) for at in range(2) for layer in range(layers)]

    def load(at, layer):
        source = (part, got)[at].at[layer]
        return pltpu.make_async_copy(source, held.at[at, layer], in_sem.at[at, layer])

    def store(at, layer):
        place = mine if at == 0 else 1 - mine
        target = both.at[layer, pl.ds(pl.multiple_of(place * rows, 16), rows)]
        return pltpu.make_async_copy(held.at[at, layer], target, out_sem.at[at, layer])

    for step in steps:
        load(*step).start()
    for step in steps:
        load(*step).wait()
        store(*step).start()
    for step in steps:
        store(*step).wait()


def join(bit, part, got, before):
    layers, rows, cols = part.shape
    if rows % 16:
        at = jnp.arange(2)[:, None, None]
        both = jnp.where(at == my_bit(bit), part[:, None], got[:, None])
        return both.reshape(layers, 2 * rows, cols)
    return pl.pallas_call(
        functools.partial(join_kernel, bit),
        out_shape=jax.ShapeDtypeStruct((layers, 2 * rows, cols), BF16),
        in_specs=[HBM, HBM, HBM],
        out_specs=HBM,
        scratch_shapes=[
            pltpu.VMEM((2, layers, rows, cols), BF16),
            pltpu.SemaphoreType.DMA((2, layers)),
            pltpu.SemaphoreType.DMA((2, layers)),
        ],
        compiler_params=pltpu.CompilerParams(vmem_limit_bytes=VMEM_BYTES),
        cost_estimate=SHORT,
        name="join",
    )(part, got, before)


class Stream:
    def __init__(self, layers, keep, send, order, extra):
        self.layers, self.keep, self.send, self.order, self.extra = layers, keep, send, order, extra

    def enter(self):
        self.got = swap(self.send)

    def send_half(self, turn, chain):
        bit = self.order[turn]
        self.old = (self.keep, self.got)
        send = half_sum(bit, 0, self.extra, *self.old, chain[-1])
        chain.append(send)
        self.got = across(send, bit)

    def keep_half(self, turn, chain):
        self.keep = half_sum(self.order[turn], 1, self.extra, *self.old, chain[-1])
        chain.append(self.keep)

    def exchange(self, chain):
        self.own, send, *self.vec = split(self.keep, self.got, chain[-1], self.extra)
        chain.append(send)
        if len(self.layers) == 1:
            live = self.layers[0]
            self.got = lax.ppermute(send, "section", [(1 - live, live)])
        else:
            self.got = swap(send)

    def gather(self, turn, chain):
        bits = len(self.order)
        bit = self.order[bits - 1 - turn]
        if turn == 0:
            place = jnp.arange(2)[:, None, None]
            self.part = jnp.where(place == lax.axis_index("section"), self.own, self.got)
        else:
            self.part = join(self.order[bits - turn], self.part, self.got, chain[-1])
        chain.append(self.part)
        if len(self.layers) == 1:
            devices = lax.axis_size("dp")
            first = self.layers[0] * devices
            pairs = [(first + i, first + (i ^ 1 << bit)) for i in range(devices)]
            self.got = lax.ppermute(self.part, ("section", "dp"), pairs)
        else:
            self.got = across(self.part, bit)


def place_kernel(kind, turn, layers, first_bit, part, *refs):
    outs_count = 2 if kind == "attn" else 1
    refs = refs[outs_count + 1 if turn else 1 :]
    outs = refs[:outs_count]
    held, wide, in_sem, out_sem = refs[outs_count:]
    rows, cols = held.shape[1:]
    side = my_bit(first_bit) if turn == 0 else 1 - my_bit(first_bit)
    live = True if len(layers) == 2 else lax.axis_index("section") == layers[0]

    def target(half, at):
        if kind == "rows":
            return outs[0].at[0, pl.ds(pl.multiple_of((2 * half + side) * rows, 8), rows), :]
        at_rows = pl.ds(pl.multiple_of(side * rows, 8), rows)
        width = cols if kind == "cols" else (cols // 4 if at == 0 else 3 * cols // 4)
        return outs[at].at[0, at_rows, half * width : (half + 1) * width]

    def out_copies(half, wait):
        pieces = [(0, slice(0, cols))]
        if kind == "attn":
            pieces = [(0, slice(0, cols // 4)), (1, slice(cols // 4, cols))]
        for at, where in pieces:
            copy = pltpu.make_async_copy(wide.at[half, :, where], target(half, at), out_sem.at[half, at])
            copy.wait() if wait else copy.start()

    def load(half):
        return pltpu.make_async_copy(part.at[half], held.at[half], in_sem.at[half])

    for half in range(2):
        load(half).start()
    for half in range(2):
        load(half).wait()

        def convert(i, carry, half=half):
            at = pl.ds(pl.multiple_of(i * 16, 16), 16)
            value = held[half, at, :].astype(F32)
            wide[half, at, :] = value if live is True else jnp.where(live, value, 0.0)
            return carry

        lax.fori_loop(0, rows // 16, convert, 0, unroll=2)
        out_copies(half, False)
    for half in range(2):
        out_copies(half, True)


def place(kind, turn, layers, first_bit, part, shapes, extra):
    rows, cols = part.shape[1:]
    return pl.pallas_call(
        functools.partial(place_kernel, kind, turn, layers, first_bit),
        out_shape=[jax.ShapeDtypeStruct(out, F32) for out in shapes],
        in_specs=[HBM] * (1 + len(extra)),
        out_specs=[HBM] * len(shapes),
        input_output_aliases={1 + i: i for i in range(len(shapes))} if turn else {},
        scratch_shapes=[
            pltpu.VMEM((2, rows, cols), BF16),
            pltpu.VMEM((2, rows, cols), F32),
            pltpu.SemaphoreType.DMA((2,)),
            pltpu.SemaphoreType.DMA((2, 2)),
        ],
        compiler_params=pltpu.CompilerParams(vmem_limit_bytes=VMEM_BYTES),
        cost_estimate=LONG,
        name="place_" + kind,
    )(part, *extra)


def slots_kernel(index, keep, got, before, out, own, new, wide, in_sem, out_sem):
    section = lax.axis_index("section")
    mine = pltpu.make_async_copy(keep, own, in_sem.at[0])
    theirs = pltpu.make_async_copy(got.at[index], new, in_sem.at[1])
    mine.start()
    theirs.start()
    mine.wait()
    store_mine = pltpu.make_async_copy(own, out.at[section], out_sem.at[0])
    store_mine.start()
    theirs.wait()

    def convert(i, carry):
        at = pl.ds(pl.multiple_of(i * 32, 32), 32)
        wide[at, :] = new[at, :].astype(F32)
        return carry

    lax.fori_loop(0, new.shape[0] // 32, convert, 0)
    store_theirs = pltpu.make_async_copy(wide, out.at[1 - section], out_sem.at[1])
    store_theirs.start()
    store_mine.wait()
    store_theirs.wait()


def both_slots(index, keep, got, before):
    return pl.pallas_call(
        functools.partial(slots_kernel, index),
        out_shape=jax.ShapeDtypeStruct((2, *keep.shape), F32),
        in_specs=[HBM, HBM, HBM],
        out_specs=HBM,
        scratch_shapes=[
            pltpu.VMEM(keep.shape, F32),
            pltpu.VMEM(keep.shape, BF16),
            pltpu.VMEM(keep.shape, F32),
            pltpu.SemaphoreType.DMA((2,)),
            pltpu.SemaphoreType.DMA((2,)),
        ],
        compiler_params=pltpu.CompilerParams(vmem_limit_bytes=VMEM_BYTES),
        cost_estimate=FREE,
        name="both_slots",
    )(keep, got, before)


def tail(layers, grads, out_keep, in_keep, sends, weight_shapes):
    bits = lax.axis_size("dp").bit_length() - 1
    by_x = list(range(bits))
    orders = (by_x[:1] + by_x[2:] + by_x[1:2], [1, 0] + by_x[2:], by_x[2:-1] + [1, 0] + by_x[-1:])
    streams = []
    for (keep, send), order in zip(grads, orders):
        extra = keep.shape[1] - keep.shape[2] // 2 if keep is grads[2][0] else 0
        if len(layers) == 1:
            keep, send = [a[layers[0] : layers[0] + 1] for a in (keep, send)]
        streams.append(Stream(layers, keep, send, order, extra))
    for stream in streams:
        stream.enter()
    slots_got = swap(sends)
    chain = [sends]
    for turn in range(bits):
        for stream in streams:
            stream.send_half(turn, chain)
        for stream in streams:
            stream.keep_half(turn, chain)
        if turn == 0:
            out_half = both_slots(0, out_keep, slots_got, chain[-1])
            grad_half = both_slots(1, in_keep, slots_got, out_half)
            chain.append(grad_half)
    for stream in streams:
        stream.exchange(chain)
    for turn in range(bits):
        for stream in streams:
            stream.gather(turn, chain)
    kinds = ("rows", "cols", "attn")
    placed, results = [], []
    for kind, stream, shapes in zip(kinds, streams, weight_shapes):
        placed.append(place(kind, 0, layers, stream.order[0], stream.part, shapes, [chain[-1]]))
        chain.append(placed[-1][0])
    for kind, stream, shapes, half in zip(kinds, streams, weight_shapes, placed):
        half = [*half, chain[-1]]
        results += place(kind, 1, layers, stream.order[0], stream.got, shapes, half)
        chain.append(results[-1])
    vec = streams[2].vec[0][0].astype(F32)
    if len(layers) == 1:
        vec = jnp.where(lax.axis_index("section") == layers[0], vec, 0.0)
    return (*results, vec, out_half, grad_half)


def on_device(
    inputs, cotangent, lengths, assignment, skip_flags, head_counts, ffn_counts,
    w_qkv, bias_q, bias_v, w_out, bias_out, norm1_gain, norm1_bias, w_up, bias_up, w_down,
    bias_down, norm2_gain, norm2_bias,
):
    section = lax.axis_index("section")
    first = section == 0
    slots, length, width = inputs.shape
    units = w_up.shape[2]
    zeros = jnp.zeros((1, width), BF16)
    own_counts = jnp.concatenate([skip_flags, head_counts, ffn_counts], axis=0).reshape(3 * MICRO)
    coded = jnp.concatenate([own_counts // 64, own_counts % 64]).astype(BF16).reshape(1, 6 * MICRO)
    own_vec = jnp.concatenate(
        [
            bias_q, zeros, bias_v, bias_out, norm1_gain, norm1_bias,
            bias_up.reshape(units // width, width),
            bias_down, norm2_gain, norm2_bias,
            jnp.pad(coded, ((0, 0), (0, width - 6 * MICRO))), zeros, zeros,
        ],
        axis=0,
    )
    other_vec = swap(own_vec)
    codes = other_vec[13, : 6 * MICRO].astype(jnp.int32)
    other_counts = codes[: 3 * MICRO] * 64 + codes[3 * MICRO :]
    weights = []
    for mine in (w_qkv[0], w_out[0], w_up[0], w_down[0]):
        weights += [mine, swap(mine)]
    weights += [own_vec, other_vec]
    scalars = [own_counts, other_counts, assignment, lengths]

    early = weights[:2] * 4 + weights[8:]
    proj, ctx, stat = layer_forward(False, "attend", scalars, inputs, early)
    passed, *saved_one = layer_forward(
        False, "finish", scalars, inputs, weights[2:4] + weights[2:], [ctx, stat]
    )
    saved_one = [proj, ctx, *saved_one]
    out_keep, sends, *saved_two = layer_forward(True, "all", scalars, passed, weights)
    saved_two = saved_two[:2] + saved_two[3:]

    res, *ffn, sums = ffn_back(True, scalars, cotangent, weights, saved_two)
    g_mid, *attn = attention_back(
        False, scalars, res, cotangent, passed, weights, saved_two, sums
    )
    res, *ffn, sums = ffn_back(False, scalars, g_mid, weights, saved_one, ffn)
    in_keep, sends, *attn = attention_back(
        True, scalars, res, g_mid, inputs, weights, saved_one, sums, [sends, *attn]
    )

    grads = (ffn[:2], ffn[2:], attn)
    weight_shapes = (
        [(1, units, width)], [(1, width, units)], [(1, width, width), (1, width, 3 * width)],
    )
    skips = [jnp.where(section == layer, own_counts, other_counts)[:MICRO] for layer in range(2)]
    used = [jnp.sum(skip) < MICRO for skip in skips]
    which = jnp.where(used[0] & used[1], 0, jnp.where(used[0], 1, 2))
    branches = [
        functools.partial(tail, layers, weight_shapes=weight_shapes) for layers in ((0, 1), (0,), (1,))
    ]
    grad_w_down, grad_w_up, grad_w_out, grad_w_qkv, vec, out_half, grad_half = lax.switch(
        which, branches, grads, out_keep, in_keep, sends
    )
    by_ffn, by_attn = vec[:, :width], vec[:, width:]
    grad_bias_up = by_ffn[8 : 8 + units // width].reshape(1, units)
    return (
        out_half, grad_half, grad_w_qkv, by_attn[0:1], by_attn[1:2], grad_w_out, by_attn[2:3],
        by_ffn[0:1], by_ffn[1:2], grad_w_up, grad_bias_up, grad_w_down, by_ffn[4:5], by_ffn[2:3],
        by_ffn[3:4],
    )


def solution(mesh):
    three, two = P("section", None, None), P("section", None)
    return jax.shard_map(
        on_device,
        mesh=mesh,
        in_specs=(
            P("dp", None, None), P("dp", None, None), P(), P("dp"),
            P(None, "section"), P(None, "section"), P(None, "section"),
            three, two, two, three, two, two, two, three, two, three, two, two, two,
        ),
        out_specs=(
            P("dp", None, "section"), P("dp", None, "section"),
            three, two, two, three, two, two, two, three, two, three, two, two, two,
        ),
        check_vma=False,
    )
```

```python
import functools

import jax
import jax.numpy as jnp
from jax import lax
from jax.experimental import pallas as pl
from jax.experimental.pallas import tpu as pltpu
from jax.sharding import PartitionSpec as P

HEADS = 12
MICRO = 2
NORM_EPS = 1e-05
NEG_FILL = -1e30
F32 = jnp.float32
BF16 = jnp.bfloat16

ROWS = 256
UNITS = 512
LEAST = 1920 // UNITS
SAFE = 40.0
VMEM_BYTES = 64 * 1024 * 1024

OWN, BLOCKS, LIVE, LENGTH, PAIRS, COUNT, CHUNKS, SLOT, SKIP, SECTION = range(10)
V_BQ, V_ZERO, V_BV, V_BO, V_G1, V_B1, V_BU, V_BD, V_G2, V_B2 = 0, 1, 2, 3, 4, 5, 6, 10, 11, 12


def dot(left, right):
    return lax.dot_general(left, right, (((1,), (0,)), ((), ())), preferred_element_type=F32)


def dot_nt(left, right):
    return lax.dot_general(left, right, (((1,), (1,)), ((), ())), preferred_element_type=F32)


def dot_tn(left, right):
    return lax.dot_general(left, right, (((0,), (0,)), ((), ())), preferred_element_type=F32)


def rows_at(block):
    if isinstance(block, int):
        return pl.ds(block * ROWS, ROWS)
    return pl.ds(pl.multiple_of(block * ROWS, ROWS), ROWS)


def cols_at(start, size):
    if isinstance(start, int):
        return pl.ds(start, size)
    return pl.ds(pl.multiple_of(start, 128), size)


def facts(layer, own_counts, other_counts, assigned, lengths):
    section = lax.axis_index("section")
    own = section == layer

    def count(row):
        at = row * MICRO + section
        return jnp.where(own, own_counts[at], other_counts[at])

    skip, heads, units = count(0), count(1), count(2)
    length = lengths[assigned[section]]
    live = (length + ROWS - 1) // ROWS
    blocks = jnp.where(skip == 1, 0, live)
    chunks = jnp.where(skip == 1, 0, (units + UNITS - 1) // UNITS)
    return [own.astype(jnp.int32), blocks, live, length, heads // 2, units, chunks, section, skip, section]


def by_blocks(count, most, body):
    pl.when(count > 0)(functools.partial(body, most))


def clear_dead(count, *refs):
    def clear(block, carry):
        for ref in refs:
            ref[rows_at(block), :] = jnp.zeros((ROWS, ref.shape[1]), ref.dtype)
        return carry

    lax.fori_loop(count, refs[0].shape[0] // ROWS, clear, 0)


def by_chunks(count, most, body):
    body(0, LEAST + 1)
    pl.when(count > LEAST + 1)(functools.partial(body, LEAST + 1, most))


def fetch_start(s, dst, own_ref, other_ref, sem):
    @pl.when(s[OWN] == 1)
    def _():
        pltpu.make_async_copy(own_ref, dst, sem).start()

    @pl.when(s[OWN] == 0)
    def _():
        pltpu.make_async_copy(other_ref, dst, sem).start()


def live_column(s, block):
    frame = lax.broadcasted_iota(jnp.int32, (ROWS, 1), 0) + block * ROWS
    return frame < s[LENGTH]


def gelu_parts(values):
    under = 1.0 + 0.2316419 * jnp.abs(values)
    t = pl.reciprocal(under, approx=True)
    t = t * (2.0 - under * t)
    poly = t * (
        0.319381530 + t * (-0.356563782 + t * (1.781477937 + t * (-1.821255978 + t * 1.330274429)))
    )
    bell = jnp.exp2(values * values * -0.7213475204444817) * 0.3989422804014327
    tail = poly * bell
    below = jnp.where(values >= 0, 1.0 - tail, tail)
    return values * below, below + values * bell


def spread_heads(width):
    head = lax.broadcasted_iota(jnp.int32, (128, width), 1) // 64
    return (head == lax.broadcasted_iota(jnp.int32, (128, width), 0)).astype(BF16)


def norm_parts(values):
    center = jnp.mean(values, axis=-1, keepdims=True)
    shifted = values - center
    spread = jnp.mean(shifted * shifted, axis=-1, keepdims=True)
    inverse = lax.rsqrt(spread + NORM_EPS)
    return shifted * inverse, inverse


def vec_row(vec_ref, row):
    return vec_ref[row : row + 1, :].astype(F32)


def forward_kernel(
    last,
    phase,
    own_counts, other_counts, assigned, lengths,
    x_hbm,
    wq0, wq1, wo0, wo1, wu0, wu1, wd0, wd1, v0, v1,
    *rest,
):
    s = facts(1 if last else 0, own_counts, other_counts, assigned, lengths)
    attends, finishes = phase != "finish", phase != "attend"
    if not attends:
        ctx_in, stat_in = rest[:2]
        rest = rest[2:]
    if finishes and last:
        keep_hbm, send_hbm = rest[:2]
        rest = rest[2:]
    elif finishes:
        pass_hbm = rest[0]
        rest = rest[1:]
    if attends:
        proj_hbm, ctx_hbm, lse_hbm = rest[:3]
        rest = rest[3:]
    if finishes:
        stat_hbm, gated_hbm, slope_hbm, x1_hbm, x2_hbm = rest[:5]
        rest = rest[5:]
    (
        h, wq, wo, wu, wd, vec, proj, ctx, stat, gated, slope, x1, x2, acc, normed_b, bias_up, largest, out_a, out_b,
        in_sem, w_sem, out_sem,
    ) = rest
    most = h.shape[0] // ROWS
    width = h.shape[1]
    pairs_all = width // 128
    blocks = s[BLOCKS]
    live = s[LIVE]
    lane = lax.broadcasted_iota(jnp.int32, (1, 128), 1)
    low = lane < 64

    def source(block):
        if last:
            return x_hbm.at[rows_at(block)]
        return x_hbm.at[s[SLOT], rows_at(block)]

    def h_copy(block):
        return pltpu.make_async_copy(source(block), h.at[rows_at(block)], in_sem.at[block])

    for block in range(most):
        pl.when(block < live)(lambda block=block: h_copy(block).start())

    @pl.when(blocks > 0)
    def _():
        fetch_start(s, vec, v0, v1, w_sem.at[0])
        if attends:
            fetch_start(s, wq, wq0, wq1, w_sem.at[1])
        if finishes:
            fetch_start(s, wo, wo0, wo1, w_sem.at[2])
            fetch_start(s, wu, wu0, wu1, w_sem.at[3])
            fetch_start(s, wd, wd0, wd1, w_sem.at[4])

    def reload(what, block):
        target, source = ((ctx, ctx_in), (stat, stat_in))[what]
        return pltpu.make_async_copy(
            source.at[rows_at(block)], target.at[rows_at(block)], out_sem.at[what, block]
        )

    if not attends:
        for block in range(most):
            @pl.when(block < blocks)
            def _(block=block):
                reload(0, block).start()
                reload(1, block).start()

    for block in range(most):
        pl.when(block < live)(lambda block=block: h_copy(block).wait())

    def save(what, source_ref, target_ref, block):
        return pltpu.make_async_copy(
            source_ref.at[rows_at(block)], target_ref.at[rows_at(block)], out_sem.at[what, block]
        )

    def emit(block, value):
        if last:
            half = width // 2
            first = s[SECTION] == 0
            out_a[rows_at(block), :] = jnp.where(first, value[:, :half], value[:, half:])
            out_b[rows_at(block), :] = jnp.where(first, value[:, half:], value[:, :half]).astype(BF16)
            save(7, out_a, keep_hbm, block).start()
            save(8, out_b, send_hbm.at[0], block).start()
        else:
            out_b[rows_at(block), :] = value.astype(BF16)
            save(7, out_b, pass_hbm, block).start()

    def attention():
        pltpu.make_async_copy(wq0, wq, w_sem.at[1]).wait()

        spread = spread_heads(width)
        largest[...] = jnp.zeros(largest.shape, F32)

        def project(block, carry):
            rows = rows_at(block)
            for part, row in ((0, V_BQ), (1, V_ZERO), (2, V_BV)):
                cols = slice(part * width, (part + 1) * width)
                proj[rows, cols] = (dot(h[rows, :], wq[:, cols]) + vec_row(vec, row)).astype(BF16)
            save(0, proj, proj_hbm, block).start()
            for part in range(2):
                value = proj[rows, part * width : (part + 1) * width].astype(F32)
                squares = dot_nt(spread, (value * value).astype(BF16))
                largest[part] = jnp.maximum(largest[part], squares)
            stat[rows, :] = jnp.zeros((ROWS, 128), F32)
            return carry

        lax.fori_loop(0, blocks, project, 0)

        clear_dead(blocks, proj)
        for pair in range(pairs_all):
            @pl.when(pair >= s[PAIRS])
            def _(pair=pair):
                ctx[:, pair * 128 : (pair + 1) * 128] = jnp.zeros((h.shape[0], 128), BF16)

        bound = jnp.max(largest[0]) * jnp.max(largest[1]) * 1.02
        safe = bound <= (SAFE * 8.0) ** 2

        def attend_safe(count):
            key_at = lax.broadcasted_iota(jnp.int32, (1, ROWS), 1)
            fills = [
                jnp.where(key_at + part * ROWS < s[LENGTH], 0.0, NEG_FILL) for part in range(count)
            ]

            span = count * ROWS

            def one(pair, carry):
                cols = cols_at(pair * 128, 128)
                q = proj[0:span, cols] * jnp.asarray(0.125, BF16)
                zero = jnp.zeros_like(q)
                ones = jnp.ones((ROWS, 128), BF16)
                q_own = [jnp.where(own, q, zero) for own in (low, ~low)]
                found = [None, None]
                for part in range(count):
                    keys = slice(part * ROWS, (part + 1) * ROWS)
                    k = proj[keys, cols_at(width + pair * 128, 128)]
                    v = proj[keys, cols_at(2 * width + pair * 128, 128)]
                    for head, own in enumerate((low, ~low)):
                        scores = dot_nt(q_own[head], k)
                        scores = scores + fills[part]
                        exps = jnp.exp(scores).astype(BF16)
                        more = dot(exps, jnp.where(own, v, ones))
                        found[head] = more if part == 0 else found[head] + more
                above = jnp.where(low, found[0], found[1])
                total = pltpu.roll(jnp.where(low, found[1], found[0]), 64, 1)
                ctx[0:span, cols] = (above / total).astype(BF16)
                logs = jnp.log(total)
                kept = stat[0:span, :]
                kept = jnp.where(lane == 2 * pair, logs[:, 0:1], kept)
                kept = jnp.where(lane == 2 * pair + 1, logs[:, 64:65], kept)
                stat[0:span, :] = kept
                return carry

            lax.fori_loop(0, s[PAIRS], one, 0)

        def attend():
            span = most * ROWS
            key_live = lax.broadcasted_iota(jnp.int32, (1, span), 1) < s[LENGTH]

            def clear_rows(block, carry):
                proj[rows_at(block), width:] = jnp.zeros((ROWS, 2 * width), BF16)
                return carry

            lax.fori_loop(blocks, most, clear_rows, 0)

            def one(step, carry):
                pair, block = step // blocks, step % blocks
                rows = rows_at(block)
                cols = cols_at(pair * 128, 128)
                q = proj[rows, cols] * jnp.asarray(0.125, BF16)
                k = proj[:, cols_at(width + pair * 128, 128)]
                v = proj[:, cols_at(2 * width + pair * 128, 128)]
                zero = jnp.zeros_like(q)
                ones = jnp.ones_like(v)
                found, peaks = [], []
                for own in (low, ~low):
                    scores = jnp.where(key_live, dot_nt(jnp.where(own, q, zero), k), NEG_FILL)
                    peak = jnp.max(scores, axis=-1, keepdims=True)
                    exps = jnp.exp(scores - peak).astype(BF16)
                    found.append(dot(exps, jnp.where(own, v, ones)))
                    peaks.append(peak)
                above = jnp.where(low, found[0], found[1])
                total = pltpu.roll(jnp.where(low, found[1], found[0]), 64, 1)
                ctx[rows, cols] = (above / total).astype(BF16)
                logs = jnp.where(low, peaks[0], peaks[1]) + jnp.log(total)
                kept = stat[rows, :]
                kept = jnp.where(lane == 2 * pair, logs[:, 0:1], kept)
                kept = jnp.where(lane == 2 * pair + 1, logs[:, 64:65], kept)
                stat[rows, :] = kept
                return carry

            lax.fori_loop(0, s[PAIRS] * blocks, one, 0)

        by_blocks(jnp.where(safe, blocks, 0), most, attend_safe)
        pl.when(jnp.logical_not(safe))(attend)

    def feed_forward():
        for piece in range(wu.shape[1] // width):
            bias_up[0:1, piece * width : (piece + 1) * width] = vec_row(vec, V_BU + piece)
        pltpu.make_async_copy(wo0, wo, w_sem.at[2]).wait()
        pltpu.make_async_copy(wu0, wu, w_sem.at[3]).wait()
        pltpu.make_async_copy(wd0, wd, w_sem.at[4]).wait()

        def finish(block, carry):
            rows = rows_at(block)
            if attends:
                save(1, ctx, ctx_hbm, block).start()
            else:
                reload(0, block).wait()
                reload(1, block).wait()
            res = h[rows, :].astype(F32) + dot(ctx[rows, :], wo[...]) + vec_row(vec, V_BO)
            hat, inverse_one = norm_parts(res)
            x1[rows, :] = hat.astype(BF16)
            save(5, x1, x1_hbm, block).start()
            normed = hat * vec_row(vec, V_G1) + vec_row(vec, V_B1)
            normed_b[...] = normed.astype(BF16)
            acc[...] = normed + vec_row(vec, V_BD)

            def units(start, stop):
                def lift(c):
                    cols = slice(c * UNITS, (c + 1) * UNITS)
                    return dot(normed_b[...], wu[:, cols]) + bias_up[0:1, cols]

                more = None
                later = lift(start)
                for c in range(start, stop):
                    cols = slice(c * UNITS, (c + 1) * UNITS)
                    lifted = later
                    if c + 1 < stop:
                        later = lift(c + 1)
                    value, grad = gelu_parts(lifted)
                    if c >= LEAST:
                        unit = lax.broadcasted_iota(jnp.int32, (1, UNITS), 1) + c * UNITS
                        value = jnp.where(unit < s[COUNT], value, 0.0)
                        grad = jnp.where(unit < s[COUNT], grad, 0.0)
                    value_b = value.astype(BF16)
                    gated[rows, cols] = value_b
                    slope[rows, cols] = grad.astype(BF16)
                    part = dot(value_b, wd[cols, :])
                    more = part if more is None else more + part
                acc[...] += more

            units(0, wu.shape[1] // UNITS)
            save(3, gated, gated_hbm, block).start()
            save(4, slope, slope_hbm, block).start()
            hat_two, inverse_two = norm_parts(acc[...])
            x2[rows, :] = hat_two.astype(BF16)
            save(6, x2, x2_hbm, block).start()
            kept = stat[rows, :]
            kept = jnp.where(lane == HEADS, inverse_one, kept)
            stat[rows, :] = jnp.where(lane == HEADS + 1, inverse_two, kept)
            save(2, stat, stat_hbm, block).start()
            result = hat_two * vec_row(vec, V_G2) + vec_row(vec, V_B2)
            emit(block, jnp.where(live_column(s, block), result, 0.0))
            return carry

        lax.fori_loop(0, blocks, finish, 0)

    @pl.when(blocks > 0)
    def _():
        pltpu.make_async_copy(v0, vec, w_sem.at[0]).wait()
        if attends:
            attention()
        if finishes:
            feed_forward()

    if not finishes:
        def keep(block, carry):
            save(1, ctx, ctx_hbm, block).start()
            save(2, stat, lse_hbm, block).start()
            return carry

        lax.fori_loop(0, blocks, keep, 0)
        for block in range(most):
            @pl.when(block < blocks)
            def _(block=block):
                save(0, proj, proj_hbm, block).wait()
                save(1, ctx, ctx_hbm, block).wait()
                save(2, stat, lse_hbm, block).wait()
        return

    @pl.when(s[SKIP] == 1)
    def _():
        def carry_on(block, carry):
            value = h[rows_at(block), :].astype(F32)
            emit(block, jnp.where(live_column(s, block), value, 0.0) if last else value)
            return carry

        lax.fori_loop(0, live, carry_on, 0)

    if last:
        def clear(block, carry):
            emit(block, jnp.zeros((ROWS, width), F32))
            return carry

        lax.fori_loop(live, most, clear, 0)

    for block in range(most):
        @pl.when(block < blocks)
        def _(block=block):
            if attends:
                save(0, proj, proj_hbm, block).wait()
                save(1, ctx, ctx_hbm, block).wait()
            save(2, stat, stat_hbm, block).wait()
            save(3, gated, gated_hbm, block).wait()
            save(4, slope, slope_hbm, block).wait()
            save(5, x1, x1_hbm, block).wait()
            save(6, x2, x2_hbm, block).wait()

        if last:
            save(7, out_a, keep_hbm, block).wait()
            save(8, out_b, send_hbm.at[0], block).wait()
        else:
            pl.when(block < live)(lambda block=block: save(7, out_b, pass_hbm, block).wait())


HBM = pl.BlockSpec(memory_space=pltpu.HBM)
SMEM = pl.BlockSpec(memory_space=pltpu.SMEM)


def layer_forward(last, phase, scalars, x, weights, attended=()):
    length, width = x.shape[-2:]
    units = weights[4].shape[1]
    blocks = length // ROWS
    shape = jax.ShapeDtypeStruct
    attends, finishes = phase != "finish", phase != "attend"
    outs = []
    if finishes and last:
        outs += [shape((length, width // 2), F32), shape((2, length, width // 2), BF16)]
    elif finishes:
        outs += [shape((length, width), BF16)]
    if attends:
        outs += [
            shape((length, 3 * width), BF16),
            shape((length, width), BF16),
            shape((length, 128), F32),
        ]
    if finishes:
        outs += [
            shape((length, 128), F32),
            shape((length, units), BF16),
            shape((length, units), BF16),
            shape((length, width), BF16),
            shape((length, width), BF16),
        ]

    def held(used, size, dtype=BF16):
        return pltpu.VMEM(size if used else (16, 128), dtype)

    return pl.pallas_call(
        functools.partial(forward_kernel, last, phase),
        out_shape=outs,
        in_specs=[SMEM] * 4 + [HBM] * (11 + len(attended)),
        out_specs=[HBM] * len(outs),
        scratch_shapes=[
            pltpu.VMEM((length, width), BF16),
            held(attends, (width, 3 * width)),
            held(finishes, (width, width)),
            held(True, (width, units)),
            held(finishes, (units, width)),
            pltpu.VMEM(weights[8].shape, BF16),
            held(attends, (length, 3 * width)),
            pltpu.VMEM((length, width), BF16),
            pltpu.VMEM((length, 128), F32),
            held(finishes, (length, units)),
            held(finishes, (length, units)),
            held(finishes, (length, width)),
            held(finishes, (length, width)),
            held(finishes, (ROWS, width), F32),
            held(finishes, (ROWS, width)),
            pltpu.VMEM((8, units), F32),
            pltpu.VMEM((2, 128, ROWS), F32),
            held(finishes and last, (length, width // 2), F32),
            held(finishes, (length, width // 2 if last else width)),
            pltpu.SemaphoreType.DMA((blocks,)),
            pltpu.SemaphoreType.DMA((5,)),
            pltpu.SemaphoreType.DMA((9, blocks)),
        ],
        compiler_params=pltpu.CompilerParams(vmem_limit_bytes=VMEM_BYTES),
        cost_estimate=pl.CostEstimate(
            flops=60_000_000_000 if phase == "attend" else 10_000_000_000,
            bytes_accessed=0,
            transcendentals=0,
        ),
        name="layer_forward_" + phase,
    )(*scalars, x, *weights, *attended)


def ffn_back_kernel(
    first_pass,
    own_counts, other_counts, assigned, lengths,
    g_hbm,
    wu0, wu1, wd0, wd1, v0, v1,
    stat_hbm, gated_hbm, slope_hbm, x1_hbm, x2_hbm,
    *rest,
):
    if not first_pass:
        rest = rest[4:]
    (
    res_hbm, gd_keep, gd_send, gu_keep, gu_send, vec_hbm,
    g_out, wu, wd, vec, stat, gated, slope, x1, x2, res, down, normed, gd, gu, acc, sums, sums_up,
    in_sem, w_sem, out_sem, gd_sem, gu_sem,
    ) = rest
    layer = 1 if first_pass else 0
    s = facts(layer, own_counts, other_counts, assigned, lengths)
    most = g_out.shape[0] // ROWS
    width = g_out.shape[1]
    units = wu.shape[1]
    chunks = units // UNITS
    blocks = s[BLOCKS]

    def load(what, block):
        target, source = (
            (g_out, g_hbm.at[s[SLOT]] if first_pass else g_hbm),
            (stat, stat_hbm), (gated, gated_hbm), (slope, slope_hbm), (x1, x1_hbm), (x2, x2_hbm),
        )[what]
        return pltpu.make_async_copy(
            source.at[rows_at(block)], target.at[rows_at(block)], in_sem.at[what, block]
        )

    @pl.when(blocks > 0)
    def _():
        fetch_start(s, vec, v0, v1, w_sem.at[0])

    for block in range(most):
        @pl.when(block < blocks)
        def _(block=block):
            for what in (0, 1, 5, 3, 4):
                load(what, block).start()

        if block == 0:
            @pl.when(blocks > 0)
            def _():
                fetch_start(s, wd, wd0, wd1, w_sem.at[2])
                fetch_start(s, wu, wu0, wu1, w_sem.at[1])

    for block in range(most):
        pl.when(block < blocks)(lambda block=block: load(2, block).start())

    sums[...] = jnp.zeros(sums.shape, F32)
    sums_up[...] = jnp.zeros(sums_up.shape, F32)

    @pl.when(blocks > 0)
    def _():
        pltpu.make_async_copy(v0, vec, w_sem.at[0]).wait()

        def step(block, carry):
            rows = rows_at(block)
            for what in (0, 1, 5):
                load(what, block).wait()
            inverse_one = stat[rows, HEADS : HEADS + 1]
            inverse_two = stat[rows, HEADS + 1 : HEADS + 2]
            gn = jnp.where(live_column(s, block), g_out[rows, :].astype(F32), 0.0)
            hat = x2[rows, :].astype(F32)
            sums[2:3, :] += jnp.sum(gn * hat, axis=0, keepdims=True)
            sums[3:4, :] += jnp.sum(gn, axis=0, keepdims=True)
            gh = gn * vec_row(vec, V_G2)
            mean_one = jnp.mean(gh, axis=-1, keepdims=True)
            mean_two = jnp.mean(gh * hat, axis=-1, keepdims=True)
            g_res = (gh - mean_one - hat * mean_two) * inverse_two
            down_b = g_res.astype(BF16)
            sums[4:5, :] += jnp.sum(down_b.astype(F32), axis=0, keepdims=True)
            down[rows, :] = down_b
            acc[...] = g_res

            @pl.when(block == 0)
            def _():
                pltpu.make_async_copy(wd0, wd, w_sem.at[2]).wait()
                pltpu.make_async_copy(wu0, wu, w_sem.at[1]).wait()

            load(3, block).wait()
            load(4, block).wait()

            def units(start, stop):
                def gate(c):
                    return dot_nt(down[rows, :], wd[c * UNITS : (c + 1) * UNITS, :])

                more = None
                later = gate(start)
                for c in range(start, stop):
                    cols = slice(c * UNITS, (c + 1) * UNITS)
                    g_gated = later
                    if c + 1 < stop:
                        later = gate(c + 1)
                    lift = (g_gated * slope[rows, cols].astype(F32)).astype(BF16)
                    slope[rows, cols] = lift
                    sums_up[0:1, cols] += jnp.sum(lift.astype(F32), axis=0, keepdims=True)
                    part = dot_nt(lift, wu[:, cols])
                    more = part if more is None else more + part
                acc[...] += more

            by_chunks(s[CHUNKS], chunks, units)
            g_normed = acc[...]
            hat = x1[rows, :].astype(F32)
            normed[rows, :] = (hat * vec_row(vec, V_G1) + vec_row(vec, V_B1)).astype(BF16)
            sums[0:1, :] += jnp.sum(g_normed * hat, axis=0, keepdims=True)
            sums[1:2, :] += jnp.sum(g_normed, axis=0, keepdims=True)
            gh = g_normed * vec_row(vec, V_G1)
            mean_one = jnp.mean(gh, axis=-1, keepdims=True)
            mean_two = jnp.mean(gh * hat, axis=-1, keepdims=True)
            res[rows, :] = (gh - mean_one - hat * mean_two) * inverse_one
            pltpu.make_async_copy(res.at[rows], res_hbm.at[rows], out_sem.at[block]).start()
            return carry

        lax.fori_loop(0, blocks, step, 0)
        for block in range(most):
            pl.when(block < blocks)(lambda block=block: load(2, block).wait())


    half_rows = units // 2
    half_cols = units // 2
    per_half = chunks // 2

    def chunk_copies(c):
        half, inside = c // per_half, c % per_half
        down_part = gd.at[cols_at(c * UNITS, UNITS), :]
        up_part = gu.at[:, cols_at(c * UNITS, UNITS)]
        place = cols_at(inside * UNITS, UNITS)
        return half, down_part, up_part, place

    def send_chunk(c):
        half, down_part, up_part, place = chunk_copies(c)

        @pl.when(half == s[SECTION])
        def _():
            pltpu.make_async_copy(down_part, gd_keep.at[layer, place, :], gd_sem.at[c]).start()
            pltpu.make_async_copy(up_part, gu_keep.at[layer, :, place], gu_sem.at[c]).start()

        @pl.when(half != s[SECTION])
        def _():
            pltpu.make_async_copy(down_part, gd_send.at[layer, place, :], gd_sem.at[c]).start()
            pltpu.make_async_copy(up_part, gu_send.at[layer, :, place], gu_sem.at[c]).start()

    def weigh(count):
        span = count * ROWS

        def one(c, carry):
            cols = cols_at(c * UNITS, UNITS)
            gd[cols, :] = dot_tn(gated[0:span, cols], down[0:span, :]).astype(BF16)
            gu[:, cols] = dot_tn(normed[0:span, :], slope[0:span, cols]).astype(BF16)
            send_chunk(c)
            return carry

        lax.fori_loop(0, s[CHUNKS], one, 0)

    pl.when(blocks > 0)(lambda: clear_dead(blocks, gated, down, normed, slope))
    by_blocks(blocks, most, weigh)

    def nothing(c, carry):
        cols = cols_at(c * UNITS, UNITS)
        gd[cols, :] = jnp.zeros((UNITS, width), BF16)
        gu[:, cols] = jnp.zeros((width, UNITS), BF16)
        send_chunk(c)
        return carry

    lax.fori_loop(s[CHUNKS], chunks, nothing, 0)

    for c in range(chunks):
        _, down_part, up_part, place = chunk_copies(c)
        pltpu.make_async_copy(down_part, gd_keep.at[layer, place, :], gd_sem.at[c]).wait()
        pltpu.make_async_copy(up_part, gu_keep.at[layer, :, place], gu_sem.at[c]).wait()
    for piece in range(units // width):
        sums[8 + piece : 9 + piece, :] = sums_up[0:1, piece * width : (piece + 1) * width]
    pltpu.sync_copy(sums, vec_hbm)
    for block in range(most):
        @pl.when(block < blocks)
        def _(block=block):
            rows = rows_at(block)
            pltpu.make_async_copy(res.at[rows], res_hbm.at[rows], out_sem.at[block]).wait()


def ffn_back(first_pass, scalars, g_out, weights, saved, grads=()):
    length, width = g_out.shape[-2:]
    units = weights[4].shape[1]
    blocks = length // ROWS
    chunks = units // UNITS
    shape = jax.ShapeDtypeStruct
    _, _, stat, gated, slope, x1, x2 = saved
    return pl.pallas_call(
        functools.partial(ffn_back_kernel, first_pass),
        out_shape=[
            shape((length, width), F32),
            shape((2, units // 2, width), BF16),
            shape((2, units // 2, width), BF16),
            shape((2, width, units // 2), BF16),
            shape((2, width, units // 2), BF16),
            shape((16, width), F32),
        ],
        in_specs=[SMEM] * 4 + [HBM] * (12 + len(grads)),
        out_specs=[HBM] * 6,
        input_output_aliases={16 + i: 1 + i for i in range(len(grads))},
        scratch_shapes=[
            pltpu.VMEM((length, width), BF16),
            pltpu.VMEM((width, units), BF16),
            pltpu.VMEM((units, width), BF16),
            pltpu.VMEM(weights[8].shape, BF16),
            pltpu.VMEM((length, 128), F32),
            pltpu.VMEM((length, units), BF16),
            pltpu.VMEM((length, units), BF16),
            pltpu.VMEM((length, width), BF16),
            pltpu.VMEM((length, width), BF16),
            pltpu.VMEM((length, width), F32),
            pltpu.VMEM((length, width), BF16),
            pltpu.VMEM((length, width), BF16),
            pltpu.VMEM((units, width), BF16),
            pltpu.VMEM((width, units), BF16),
            pltpu.VMEM((ROWS, width), F32),
            pltpu.VMEM((16, width), F32),
            pltpu.VMEM((8, units), F32),
            pltpu.SemaphoreType.DMA((6, blocks)),
            pltpu.SemaphoreType.DMA((3,)),
            pltpu.SemaphoreType.DMA((blocks,)),
            pltpu.SemaphoreType.DMA((chunks,)),
            pltpu.SemaphoreType.DMA((chunks,)),
        ],
        compiler_params=pltpu.CompilerParams(vmem_limit_bytes=VMEM_BYTES),
        name="ffn_back",
    )(*scalars, g_out, *weights[4:8], *weights[8:10], stat, gated, slope, x1, x2, *grads)


def attention_back_kernel(
    first_layer,
    own_counts, other_counts, assigned, lengths,
    res_hbm, g_hbm, x_hbm,
    wq0, wq1, wo0, wo1,
    proj_hbm, ctx_hbm, stat_hbm, ffn_sums_hbm,
    *rest,
):
    layer = 0 if first_layer else 1
    s = facts(layer, own_counts, other_counts, assigned, lengths)
    rest = rest[3 if first_layer else 0 :]
    if first_layer:
        in_keep, in_send = rest[:2]
        rest = rest[2:]
    else:
        in_hbm = rest[0]
        rest = rest[1:]
    (
        ga_keep, ga_send,
        res, g_in, h, wq, wo, proj, ctx, stat, attn, g_ctx, g_proj, rows_log, rows_delta,
        go, gq, out_a, out_b, sums, ffn_sums, extra,
        in_sem, w_sem, out_sem, go_sem, gq_sem, extra_sem,
    ) = rest
    most = res.shape[0] // ROWS
    width = res.shape[1]
    half = width // 2
    pairs_all = width // 128
    blocks = s[BLOCKS]
    live = s[LIVE]
    lane = lax.broadcasted_iota(jnp.int32, (1, 128), 1)
    low = lane < 64
    zero_pair = jnp.zeros((1, 128), BF16)

    def load(what, block):
        target, source = (
            (res, res_hbm), (ctx, ctx_hbm), (stat, stat_hbm), (proj, proj_hbm),
            (h, x_hbm.at[s[SLOT]] if first_layer else x_hbm),
        )[what]
        return pltpu.make_async_copy(
            source.at[rows_at(block)], target.at[rows_at(block)], in_sem.at[what, block]
        )

    def load_g(block):
        source = g_hbm if first_layer else g_hbm.at[s[SLOT]]
        return pltpu.make_async_copy(
            source.at[rows_at(block)], g_in.at[rows_at(block)], in_sem.at[0, block]
        )

    for what in (0, 1):
        for block in range(most):
            pl.when(block < blocks)(lambda what=what, block=block: load(what, block).start())

    @pl.when(blocks > 0)
    def _():
        fetch_start(s, wo, wo0, wo1, w_sem.at[0])

    for what in (2, 3, 4):
        for block in range(most):
            pl.when(block < blocks)(lambda what=what, block=block: load(what, block).start())

    @pl.when(blocks > 0)
    def _():
        fetch_start(s, wq, wq0, wq1, w_sem.at[1])

    sums[...] = jnp.zeros(sums.shape, F32)
    ffn_load = pltpu.make_async_copy(ffn_sums_hbm, ffn_sums, extra_sem.at[2])
    ffn_load.start()

    def out_copies(block, wait):
        rows = rows_at(block)
        if first_layer:
            copies = [
                pltpu.make_async_copy(out_a.at[rows], in_keep.at[rows], out_sem.at[0, block]),
                pltpu.make_async_copy(out_b.at[rows], in_send.at[1, rows], out_sem.at[1, block]),
            ]
        else:
            copies = [pltpu.make_async_copy(out_b.at[rows], in_hbm.at[rows], out_sem.at[0, block])]
        for copy in copies:
            copy.wait() if wait else copy.start()

    def emit(block, value):
        rows = rows_at(block)
        if first_layer:
            front = s[SECTION] == 0
            out_a[rows, :] = jnp.where(front, value[:, :half], value[:, half:])
            out_b[rows, :] = jnp.where(front, value[:, half:], value[:, :half]).astype(BF16)
        else:
            out_b[rows, :] = value.astype(BF16)
        out_copies(block, False)

    def go_copy(part, keep):
        target = (ga_keep if keep else ga_send).at[layer, 0:width, 0:half]
        return pltpu.make_async_copy(go.at[:, part * half : (part + 1) * half], target, go_sem.at[part])

    def gq_copy(part, keep):
        target = (ga_keep if keep else ga_send).at[layer, 0:width, half : 4 * half]
        cols = slice(part * 3 * half, (part + 1) * 3 * half)
        return pltpu.make_async_copy(gq.at[:, cols], target, gq_sem.at[part])

    def start_halves(make):
        for part in range(2):
            pl.when(s[SECTION] == part)(lambda part=part: make(part, True).start())
            pl.when(s[SECTION] != part)(lambda part=part: make(part, False).start())

    @pl.when(blocks > 0)
    def _():
        pltpu.make_async_copy(wo0, wo, w_sem.at[0]).wait()
        spread = spread_heads(width)

        def before(block, carry):
            rows = rows_at(block)
            load(0, block).wait()
            load(1, block).wait()
            attn_b = res[rows, :].astype(BF16)
            attn[rows, :] = attn_b
            sums[2:3, :] += jnp.sum(attn_b.astype(F32), axis=0, keepdims=True)
            g_context = dot_nt(attn_b, wo[...]).astype(BF16)
            g_ctx[rows, :] = g_context
            product = (g_context.astype(F32) * ctx[rows, :].astype(F32)).astype(BF16)
            rows_delta[:, rows] = dot_nt(spread, product)
            load(2, block).wait()
            rows_log[:, rows] = stat[rows, :].T
            load(3, block).wait()
            return carry

        lax.fori_loop(0, blocks, before, 0)
        clear_dead(blocks, proj, g_ctx, ctx, attn, h)

        def clear_columns(block, carry):
            rows_log[:, rows_at(block)] = jnp.zeros((128, ROWS), F32)
            rows_delta[:, rows_at(block)] = jnp.zeros((128, ROWS), F32)
            return carry

        lax.fori_loop(blocks, most, clear_columns, 0)

        def weigh_out(count):
            span = count * ROWS
            go[...] = dot_tn(ctx[0:span, :], attn[0:span, :]).astype(BF16)

        by_blocks(blocks, most, weigh_out)
        start_halves(go_copy)

        for pair in range(pairs_all):
            @pl.when(pair >= s[PAIRS])
            def _(pair=pair):
                for part in range(3):
                    cols = slice(part * width + pair * 128, part * width + (pair + 1) * 128)
                    g_proj[:, cols] = jnp.zeros((g_proj.shape[0], 128), BF16)

        def attend_back(count):
            span = count * ROWS

            def one_pair(pair, carry):
                cols = cols_at(pair * 128, 128)
                total_q = None
                for block in range(count):
                    rows = rows_at(block)
                    q = proj[0:span, cols]
                    d_ctx = g_ctx[0:span, cols]
                    k = proj[rows, cols_at(width + pair * 128, 128)] * jnp.asarray(0.125, BF16)
                    v = proj[rows, cols_at(2 * width + pair * 128, 128)]
                    fill = jnp.where(live_column(s, block), 0.0, NEG_FILL)
                    found_k, found_v, found_q = [], [], []
                    for head, own in ((0, low), (1, ~low)):
                        k_own = jnp.where(own, k, zero_pair)
                        v_own = jnp.where(own, v, zero_pair)
                        log_row = rows_log[pl.ds(2 * pair + head, 1), 0:span]
                        delta_row = rows_delta[pl.ds(2 * pair + head, 1), 0:span]
                        probs = jnp.exp(dot_nt(k_own, q) + fill - log_row)
                        g_probs = dot_nt(v_own, d_ctx)
                        g_scores = (probs * (g_probs - delta_row)).astype(BF16)
                        found_v.append(dot(probs.astype(BF16), d_ctx))
                        found_k.append(dot(g_scores, q))
                        found_q.append(dot_tn(g_scores, k_own))
                    more_q = found_q[0] + found_q[1]
                    total_q = more_q if block == 0 else total_q + more_q
                    g_k = jnp.where(low, found_k[0], found_k[1]) * 0.125
                    g_v = jnp.where(low, found_v[0], found_v[1])
                    g_proj[rows, cols_at(width + pair * 128, 128)] = g_k.astype(BF16)
                    g_proj[rows, cols_at(2 * width + pair * 128, 128)] = g_v.astype(BF16)
                g_proj[0:span, cols] = total_q.astype(BF16)
                return carry

            lax.fori_loop(0, s[PAIRS], one_pair, 0)

        by_blocks(blocks, most, attend_back)

        for block in range(most):
            pl.when(block < blocks)(lambda block=block: load(4, block).wait())
        pltpu.make_async_copy(wq0, wq, w_sem.at[1]).wait()

        def weigh_in(count):
            span = count * ROWS

            def one(part, carry):
                cols = cols_at(part * width, width)
                gq[:, cols] = dot_tn(h[0:span, :], g_proj[0:span, cols]).astype(BF16)
                return carry

            lax.fori_loop(0, 3, one, 0)

        by_blocks(blocks, most, weigh_in)
        start_halves(gq_copy)

        def after(block, carry):
            rows = rows_at(block)
            grad = g_proj[rows, :]
            sums[0:1, :] += jnp.sum(grad[:, :width].astype(F32), axis=0, keepdims=True)
            sums[1:2, :] += jnp.sum(grad[:, 2 * width :].astype(F32), axis=0, keepdims=True)
            emit(block, res[rows, :] + dot_nt(grad, wq[...]))
            return carry

        lax.fori_loop(0, blocks, after, 0)

    @pl.when(s[SKIP] == 1)
    def _():
        go[...] = jnp.zeros(go.shape, BF16)
        gq[...] = jnp.zeros(gq.shape, BF16)
        start_halves(go_copy)
        start_halves(gq_copy)
        for block in range(most):
            pl.when(block < live)(lambda block=block: load_g(block).start())
        for block in range(most):
            pl.when(block < live)(lambda block=block: load_g(block).wait())

        def carry_on(block, carry):
            value = g_in[rows_at(block), :].astype(F32)
            emit(block, jnp.where(live_column(s, block), value, 0.0))
            return carry

        lax.fori_loop(0, live, carry_on, 0)

    if first_layer:
        def clear(block, carry):
            emit(block, jnp.zeros((ROWS, width), F32))
            return carry

        lax.fori_loop(live, most, clear, 0)

    ffn_load.wait()
    own_sums = jnp.concatenate([sums[...], jnp.zeros(sums.shape, F32)], axis=0)
    extra[...] = jnp.concatenate([ffn_sums[...], own_sums], axis=1).astype(BF16)
    extra_copies = [
        pltpu.make_async_copy(extra, target.at[layer, width : width + 16], extra_sem.at[at])
        for at, target in enumerate((ga_keep, ga_send))
    ]
    for copy in extra_copies:
        copy.start()
    for copy in extra_copies:
        copy.wait()
    for part in range(2):
        go_copy(part, True).wait()
        gq_copy(part, True).wait()
    for block in range(most):
        if first_layer:
            out_copies(block, True)
        else:
            pl.when(block < live)(lambda block=block: out_copies(block, True))


def attention_back(first_layer, scalars, res, g_out, x, weights, saved, ffn_sums, grads=()):
    length, width = res.shape
    blocks = length // ROWS
    shape = jax.ShapeDtypeStruct
    proj, ctx, stat = saved[:3]
    outs = (
        [shape((length, width // 2), F32), shape((2, length, width // 2), BF16)]
        if first_layer
        else [shape((length, width), BF16)]
    )
    outs += [
        shape((2, width + 16, 2 * width), BF16),
        shape((2, width + 16, 2 * width), BF16),
    ]
    return pl.pallas_call(
        functools.partial(attention_back_kernel, first_layer),
        out_shape=outs,
        in_specs=[SMEM] * 4 + [HBM] * (11 + len(grads)),
        out_specs=[HBM] * len(outs),
        input_output_aliases={15 + i: len(outs) - len(grads) + i for i in range(len(grads))},
        scratch_shapes=[
            pltpu.VMEM((length, width), F32),
            pltpu.VMEM((length, width), BF16),
            pltpu.VMEM((length, width), BF16),
            pltpu.VMEM((width, 3 * width), BF16),
            pltpu.VMEM((width, width), BF16),
            pltpu.VMEM((length, 3 * width), BF16),
            pltpu.VMEM((length, width), BF16),
            pltpu.VMEM((length, 128), F32),
            pltpu.VMEM((length, width), BF16),
            pltpu.VMEM((length, width), BF16),
            pltpu.VMEM((length, 3 * width), BF16),
            pltpu.VMEM((128, length), F32),
            pltpu.VMEM((128, length), F32),
            pltpu.VMEM((width, width), BF16),
            pltpu.VMEM((width, 3 * width), BF16),
            pltpu.VMEM((length if first_layer else 8, width // 2), F32),
            pltpu.VMEM((length, width // 2 if first_layer else width), BF16),
            pltpu.VMEM((8, width), F32),
            pltpu.VMEM((16, width), F32),
            pltpu.VMEM((16, 2 * width), BF16),
            pltpu.SemaphoreType.DMA((5, blocks)),
            pltpu.SemaphoreType.DMA((2,)),
            pltpu.SemaphoreType.DMA((2, blocks)),
            pltpu.SemaphoreType.DMA((2,)),
            pltpu.SemaphoreType.DMA((2,)),
            pltpu.SemaphoreType.DMA((3,)),
        ],
        compiler_params=pltpu.CompilerParams(vmem_limit_bytes=VMEM_BYTES),
        name="attention_back",
    )(*scalars, res, g_out, x, *weights[0:4], proj, ctx, stat, ffn_sums, *grads)


def swap(part):
    return lax.ppermute(part, "section", [(0, 1), (1, 0)])


def across(part, bit):
    pairs = [(i, i ^ 1 << bit) for i in range(lax.axis_size("dp"))]
    return lax.ppermute(part, "dp", pairs)


FREE = pl.CostEstimate(flops=0, bytes_accessed=0, transcendentals=0)
SHORT = pl.CostEstimate(flops=4_000_000_000, bytes_accessed=0, transcendentals=0)
LONG = pl.CostEstimate(flops=20_000_000_000, bytes_accessed=0, transcendentals=0)


def my_bit(bit):
    return (lax.axis_index("dp") >> bit) & 1


def half_sum_kernel(bit, turn, extra, base, keep, got, before, out, own, new, in_sem, out_sem):
    layers, rows, _ = got.shape
    half = (rows - extra) // 2
    at = 1 - my_bit(bit) if turn == 0 else my_bit(bit)
    spans = [(pl.ds(pl.multiple_of(at * half, 16), half), slice(0, half))]
    if extra:
        spans.append((slice(rows - extra, rows), slice(half, half + extra)))

    def loads(layer):
        copies = []
        for i, (source, target) in enumerate(spans):
            for j, (ref, held) in enumerate(((keep, own), (got, new))):
                start = base if j == 0 else 0
                copies.append(
                    pltpu.make_async_copy(
                        ref.at[start + layer, source], held.at[layer, target], in_sem.at[layer, i, j]
                    )
                )
        return copies

    def store(layer):
        return pltpu.make_async_copy(own.at[layer], out.at[layer], out_sem.at[layer])

    for layer in range(layers):
        for copy in loads(layer):
            copy.start()
    for layer in range(layers):
        for copy in loads(layer):
            copy.wait()

        def add_rows(i, carry, layer=layer):
            place = pl.ds(pl.multiple_of(i * 16, 16), 16)
            total = own[layer, place, :].astype(F32) + new[layer, place, :].astype(F32)
            own[layer, place, :] = total.astype(BF16)
            return carry

        lax.fori_loop(0, (half + extra) // 16, add_rows, 0, unroll=3)
        store(layer).start()
    for layer in range(layers):
        store(layer).wait()


def half_sum(bit, turn, extra, base, keep, got, before):
    layers, rows, cols = got.shape
    half = (rows - extra) // 2
    if half % 48:
        keep = keep[base : base + layers]
        at = 1 - my_bit(bit) if turn == 0 else my_bit(bit)

        def parts(a):
            own = lax.dynamic_slice_in_dim(a, at * half, half, 1)
            return jnp.concatenate([own, a[:, rows - extra :]], axis=1).astype(F32)

        return (parts(keep) + parts(got)).astype(BF16)
    return pl.pallas_call(
        functools.partial(half_sum_kernel, bit, turn, extra, base),
        out_shape=jax.ShapeDtypeStruct((layers, half + extra, cols), BF16),
        in_specs=[HBM, HBM, HBM],
        out_specs=HBM,
        scratch_shapes=[
            pltpu.VMEM((layers, half + extra, cols), BF16),
            pltpu.VMEM((layers, half + extra, cols), BF16),
            pltpu.SemaphoreType.DMA((layers, 2, 2)),
            pltpu.SemaphoreType.DMA((layers,)),
        ],
        compiler_params=pltpu.CompilerParams(vmem_limit_bytes=VMEM_BYTES),
        cost_estimate=FREE if turn else SHORT,
        name="half_sum",
    )(keep, got, before)


def split_kernel(extra, one, two, before, own, send, *vec):
    layers, rows, _ = one.shape
    rows -= extra
    section = lax.axis_index("section")
    mine, theirs = (section, 1 - section) if layers == 2 else (0, 0)

    def total(at, where):
        return (one[pl.ds(at, 1), where].astype(F32) + two[pl.ds(at, 1), where].astype(F32)).astype(BF16)

    own[...] = total(mine, slice(0, rows))
    send[...] = total(theirs, slice(0, rows))
    if extra:
        vec[0][...] = total(mine, slice(rows, rows + extra))


def split(one, two, before, extra):
    layers, rows, cols = one.shape
    rows -= extra
    if rows % 16:
        total = (one.astype(F32) + two.astype(F32)).astype(BF16)
        own = send = total
        if layers == 2:
            section = lax.axis_index("section")
            own = lax.dynamic_slice_in_dim(total, section, 1)
            send = lax.dynamic_slice_in_dim(total, 1 - section, 1)
        return (own[:, :rows], send[:, :rows]) + ((own[:, rows:],) if extra else ())
    whole = pl.BlockSpec(memory_space=pltpu.VMEM)
    outs = [jax.ShapeDtypeStruct((1, rows, cols), BF16)] * 2
    if extra:
        outs.append(jax.ShapeDtypeStruct((1, extra, cols), BF16))
    return pl.pallas_call(
        functools.partial(split_kernel, extra),
        out_shape=outs,
        in_specs=[whole, whole, HBM],
        out_specs=[whole] * len(outs),
        cost_estimate=SHORT,
        name="split",
    )(one, two, before)


def join_kernel(bit, part, got, before, both, held, in_sem, out_sem):
    layers, rows, _ = part.shape
    mine = my_bit(bit)
    steps = [(at, layer) for at in range(2) for layer in range(layers)]

    def load(at, layer):
        source = (part, got)[at].at[layer]
        return pltpu.make_async_copy(source, held.at[at, layer], in_sem.at[at, layer])

    def store(at, layer):
        place = mine if at == 0 else 1 - mine
        target = both.at[layer, pl.ds(pl.multiple_of(place * rows, 16), rows)]
        return pltpu.make_async_copy(held.at[at, layer], target, out_sem.at[at, layer])

    for step in steps:
        load(*step).start()
    for step in steps:
        load(*step).wait()
        store(*step).start()
    for step in steps:
        store(*step).wait()


def join(bit, part, got, before):
    layers, rows, cols = part.shape
    if rows % 16:
        at = jnp.arange(2)[:, None, None]
        both = jnp.where(at == my_bit(bit), part[:, None], got[:, None])
        return both.reshape(layers, 2 * rows, cols)
    return pl.pallas_call(
        functools.partial(join_kernel, bit),
        out_shape=jax.ShapeDtypeStruct((layers, 2 * rows, cols), BF16),
        in_specs=[HBM, HBM, HBM],
        out_specs=HBM,
        scratch_shapes=[
            pltpu.VMEM((2, layers, rows, cols), BF16),
            pltpu.SemaphoreType.DMA((2, layers)),
            pltpu.SemaphoreType.DMA((2, layers)),
        ],
        compiler_params=pltpu.CompilerParams(vmem_limit_bytes=VMEM_BYTES),
        cost_estimate=SHORT,
        name="join",
    )(part, got, before)


class Stream:
    def __init__(self, layers, keep, send, order, extra):
        self.layers, self.keep, self.send, self.order, self.extra = layers, keep, send, order, extra

    def enter(self):
        self.got = swap(self.send)

    def send_half(self, turn, chain):
        bit = self.order[turn]
        self.old = (self.keep, self.got)
        self.base = self.layers[0] if len(self.layers) == 1 and turn == 0 else 0
        send = half_sum(bit, 0, self.extra, self.base, *self.old, chain[-1])
        chain.append(send)
        self.got = across(send, bit)

    def keep_half(self, turn, chain):
        self.keep = half_sum(self.order[turn], 1, self.extra, self.base, *self.old, chain[-1])
        chain.append(self.keep)

    def exchange(self, chain):
        self.own, send, *self.vec = split(self.keep, self.got, chain[-1], self.extra)
        chain.append(send)
        if len(self.layers) == 1:
            live = self.layers[0]
            self.got = lax.ppermute(send, "section", [(1 - live, live)])
        else:
            self.got = swap(send)

    def gather(self, turn, chain):
        bits = len(self.order)
        bit = self.order[bits - 1 - turn]
        if turn == 0:
            place = jnp.arange(2)[:, None, None]
            self.part = jnp.where(place == lax.axis_index("section"), self.own, self.got)
        else:
            self.part = join(self.order[bits - turn], self.part, self.got, chain[-1])
        chain.append(self.part)
        if len(self.layers) == 1:
            devices = lax.axis_size("dp")
            first = self.layers[0] * devices
            pairs = [(first + i, first + (i ^ 1 << bit)) for i in range(devices)]
            self.got = lax.ppermute(self.part, ("section", "dp"), pairs)
        else:
            self.got = across(self.part, bit)


def place_kernel(kind, turn, layers, first_bit, part, *refs):
    outs_count = 2 if kind == "attn" else 1
    refs = refs[outs_count + 1 if turn else 1 :]
    outs = refs[:outs_count]
    held, wide, in_sem, out_sem = refs[outs_count:]
    rows, cols = held.shape[1:]
    side = my_bit(first_bit) if turn == 0 else 1 - my_bit(first_bit)
    live = True if len(layers) == 2 else lax.axis_index("section") == layers[0]

    def target(half, at):
        if kind == "rows":
            return outs[0].at[0, pl.ds(pl.multiple_of((2 * half + side) * rows, 8), rows), :]
        at_rows = pl.ds(pl.multiple_of(side * rows, 8), rows)
        width = cols if kind == "cols" else (cols // 4 if at == 0 else 3 * cols // 4)
        return outs[at].at[0, at_rows, half * width : (half + 1) * width]

    def out_copies(half, wait):
        pieces = [(0, slice(0, cols))]
        if kind == "attn":
            pieces = [(0, slice(0, cols // 4)), (1, slice(cols // 4, cols))]
        for at, where in pieces:
            copy = pltpu.make_async_copy(wide.at[half, :, where], target(half, at), out_sem.at[half, at])
            copy.wait() if wait else copy.start()

    def load(half):
        return pltpu.make_async_copy(part.at[half], held.at[half], in_sem.at[half])

    for half in range(2):
        load(half).start()
    for half in range(2):
        load(half).wait()

        def convert(i, carry, half=half):
            at = pl.ds(pl.multiple_of(i * 16, 16), 16)
            value = held[half, at, :].astype(F32)
            wide[half, at, :] = value if live is True else jnp.where(live, value, 0.0)
            return carry

        lax.fori_loop(0, rows // 16, convert, 0, unroll=2)
        out_copies(half, False)
    for half in range(2):
        out_copies(half, True)


def place(kind, turn, layers, first_bit, part, shapes, extra):
    rows, cols = part.shape[1:]
    return pl.pallas_call(
        functools.partial(place_kernel, kind, turn, layers, first_bit),
        out_shape=[jax.ShapeDtypeStruct(out, F32) for out in shapes],
        in_specs=[HBM] * (1 + len(extra)),
        out_specs=[HBM] * len(shapes),
        input_output_aliases={1 + i: i for i in range(len(shapes))} if turn else {},
        scratch_shapes=[
            pltpu.VMEM((2, rows, cols), BF16),
            pltpu.VMEM((2, rows, cols), F32),
            pltpu.SemaphoreType.DMA((2,)),
            pltpu.SemaphoreType.DMA((2, 2)),
        ],
        compiler_params=pltpu.CompilerParams(vmem_limit_bytes=VMEM_BYTES),
        cost_estimate=LONG,
        name="place_" + kind,
    )(part, *extra)


def slots_kernel(index, keep, got, before, out, own, new, wide, in_sem, out_sem):
    section = lax.axis_index("section")
    mine = pltpu.make_async_copy(keep, own, in_sem.at[0])
    theirs = pltpu.make_async_copy(got.at[index], new, in_sem.at[1])
    mine.start()
    theirs.start()
    mine.wait()
    store_mine = pltpu.make_async_copy(own, out.at[section], out_sem.at[0])
    store_mine.start()
    theirs.wait()

    def convert(i, carry):
        at = pl.ds(pl.multiple_of(i * 32, 32), 32)
        wide[at, :] = new[at, :].astype(F32)
        return carry

    lax.fori_loop(0, new.shape[0] // 32, convert, 0)
    store_theirs = pltpu.make_async_copy(wide, out.at[1 - section], out_sem.at[1])
    store_theirs.start()
    store_mine.wait()
    store_theirs.wait()


def both_slots(index, keep, got, before):
    return pl.pallas_call(
        functools.partial(slots_kernel, index),
        out_shape=jax.ShapeDtypeStruct((2, *keep.shape), F32),
        in_specs=[HBM, HBM, HBM],
        out_specs=HBM,
        scratch_shapes=[
            pltpu.VMEM(keep.shape, F32),
            pltpu.VMEM(keep.shape, BF16),
            pltpu.VMEM(keep.shape, F32),
            pltpu.SemaphoreType.DMA((2,)),
            pltpu.SemaphoreType.DMA((2,)),
        ],
        compiler_params=pltpu.CompilerParams(vmem_limit_bytes=VMEM_BYTES),
        cost_estimate=FREE,
        name="both_slots",
    )(keep, got, before)


def tail(layers, grads, out_keep, in_keep, sends, weight_shapes):
    bits = lax.axis_size("dp").bit_length() - 1
    by_x = list(range(bits))
    orders = (by_x[:1] + by_x[2:] + by_x[1:2], [1, 0] + by_x[2:], by_x[2:-1] + [1, 0] + by_x[-1:])
    streams = []
    for (keep, send), order in zip(grads, orders):
        extra = keep.shape[1] - keep.shape[2] // 2 if keep is grads[2][0] else 0
        if len(layers) == 1:
            send = send[layers[0] : layers[0] + 1]
        streams.append(Stream(layers, keep, send, order, extra))
    for stream in streams:
        stream.enter()
    slots_got = swap(sends)
    chain = [sends]
    for turn in range(bits):
        for stream in streams:
            stream.send_half(turn, chain)
        for stream in streams:
            stream.keep_half(turn, chain)
        if turn == 0:
            out_half = both_slots(0, out_keep, slots_got, chain[-1])
            grad_half = both_slots(1, in_keep, slots_got, out_half)
            chain.append(grad_half)
    for stream in streams:
        stream.exchange(chain)
    for turn in range(bits):
        for stream in streams:
            stream.gather(turn, chain)
    kinds = ("rows", "cols", "attn")
    placed, results = [], []
    for kind, stream, shapes in zip(kinds, streams, weight_shapes):
        placed.append(place(kind, 0, layers, stream.order[0], stream.part, shapes, [chain[-1]]))
        chain.append(placed[-1][0])
    for kind, stream, shapes, half in zip(kinds, streams, weight_shapes, placed):
        half = [*half, chain[-1]]
        results += place(kind, 1, layers, stream.order[0], stream.got, shapes, half)
        chain.append(results[-1])
    vec = streams[2].vec[0][0].astype(F32)
    if len(layers) == 1:
        vec = jnp.where(lax.axis_index("section") == layers[0], vec, 0.0)
    return (*results, vec, out_half, grad_half)


def on_device(
    inputs, cotangent, lengths, assignment, skip_flags, head_counts, ffn_counts,
    w_qkv, bias_q, bias_v, w_out, bias_out, norm1_gain, norm1_bias, w_up, bias_up, w_down,
    bias_down, norm2_gain, norm2_bias,
):
    section = lax.axis_index("section")
    first = section == 0
    slots, length, width = inputs.shape
    units = w_up.shape[2]
    zeros = jnp.zeros((1, width), BF16)
    own_counts = jnp.concatenate([skip_flags, head_counts, ffn_counts], axis=0).reshape(3 * MICRO)
    coded = jnp.concatenate([own_counts // 64, own_counts % 64]).astype(BF16).reshape(1, 6 * MICRO)
    own_vec = jnp.concatenate(
        [
            bias_q, zeros, bias_v, bias_out, norm1_gain, norm1_bias,
            bias_up.reshape(units // width, width),
            bias_down, norm2_gain, norm2_bias,
            jnp.pad(coded, ((0, 0), (0, width - 6 * MICRO))), zeros, zeros,
        ],
        axis=0,
    )
    other_vec = swap(own_vec)
    codes = other_vec[13, : 6 * MICRO].astype(jnp.int32)
    other_counts = codes[: 3 * MICRO] * 64 + codes[3 * MICRO :]
    weights = []
    for mine in (w_qkv[0], w_out[0], w_up[0], w_down[0]):
        weights += [mine, swap(mine)]
    weights += [own_vec, other_vec]
    scalars = [own_counts, other_counts, assignment, lengths]

    early = weights[:2] * 4 + weights[8:]
    proj, ctx, stat = layer_forward(False, "attend", scalars, inputs, early)
    passed, *saved_one = layer_forward(
        False, "finish", scalars, inputs, weights[2:4] + weights[2:], [ctx, stat]
    )
    saved_one = [proj, ctx, *saved_one]
    out_keep, sends, *saved_two = layer_forward(True, "all", scalars, passed, weights)
    saved_two = saved_two[:2] + saved_two[3:]

    res, *ffn, sums = ffn_back(True, scalars, cotangent, weights, saved_two)
    g_mid, *attn = attention_back(
        False, scalars, res, cotangent, passed, weights, saved_two, sums
    )
    res, *ffn, sums = ffn_back(False, scalars, g_mid, weights, saved_one, ffn)
    in_keep, sends, *attn = attention_back(
        True, scalars, res, g_mid, inputs, weights, saved_one, sums, [sends, *attn]
    )

    grads = (ffn[:2], ffn[2:], attn)
    weight_shapes = (
        [(1, units, width)], [(1, width, units)], [(1, width, width), (1, width, 3 * width)],
    )
    skips = [jnp.where(section == layer, own_counts, other_counts)[:MICRO] for layer in range(2)]
    used = [jnp.sum(skip) < MICRO for skip in skips]
    which = jnp.where(used[0] & used[1], 0, jnp.where(used[0], 1, 2))
    branches = [
        functools.partial(tail, layers, weight_shapes=weight_shapes) for layers in ((0, 1), (0,), (1,))
    ]
    grad_w_down, grad_w_up, grad_w_out, grad_w_qkv, vec, out_half, grad_half = lax.switch(
        which, branches, grads, out_keep, in_keep, sends
    )
    by_ffn, by_attn = vec[:, :width], vec[:, width:]
    grad_bias_up = by_ffn[8 : 8 + units // width].reshape(1, units)
    return (
        out_half, grad_half, grad_w_qkv, by_attn[0:1], by_attn[1:2], grad_w_out, by_attn[2:3],
        by_ffn[0:1], by_ffn[1:2], grad_w_up, grad_bias_up, grad_w_down, by_ffn[4:5], by_ffn[2:3],
        by_ffn[3:4],
    )


def solution(mesh):
    three, two = P("section", None, None), P("section", None)
    return jax.shard_map(
        on_device,
        mesh=mesh,
        in_specs=(
            P("dp", None, None), P("dp", None, None), P(), P("dp"),
            P(None, "section"), P(None, "section"), P(None, "section"),
            three, two, two, three, two, two, two, three, two, three, two, two, two,
        ),
        out_specs=(
            P("dp", None, "section"), P("dp", None, "section"),
            three, two, two, three, two, two, two, three, two, three, two, two, two,
        ),
        check_vma=False,
    )
```
